256 devices in a mesh: seq: 32 (over x_lo, z, core), band: 8 (over y, x_hi).
Axes of the slice: x: 4 (x_hi: 2, x_lo: 2; x = x_hi * 2 + x_lo), y: 4, z: 8, core: 2. Of those that a mesh axis runs over, the one named last changes fastest.
Arguments:
- tokens: bfloat16 [4096, 1024], P('seq', 'band'), may hold values from -6 to 6
- mappable: int32 [4096], P('seq'), may hold values 0 or 1
- attn_gain: float32 [1024], replicated, may hold values from 0.1 to 1.9
- w_query: bfloat16 [1024, 1024], P(None, 'band'), may hold values from -1 to 1
- w_key: bfloat16 [1024, 1024], P(None, 'band'), may hold values from -4 to 4
- w_value: bfloat16 [1024, 1024], P(None, 'band'), may hold values from -0.1875 to 0.1875
- w_out: bfloat16 [1024, 1024], P('band'), may hold values from -0.75 to 0.75
- w_left: bfloat16 [1024, 128], replicated, may hold values from -0.1875 to 0.1875
- w_right: bfloat16 [1024, 128], replicated, may hold values from -0.1875 to 0.1875
- conv_gain: float32 [2, 128], replicated, may hold values from 0.1 to 1.9
- conv_kernel: bfloat16 [2, 3, 3, 128, 128], replicated, may hold values from -0.1875 to 0.1875
- conv_bias: float32 [2, 128], replicated, may hold values from -3 to 3
- contact_weight: float32 [128], replicated, may hold values from -0.5 to 0.5
Outputs:
- trunk_out: bfloat16 [4096, 1024], P('seq', 'band')
- contacts: float32 [4096, 256], P('seq', 'band')
The draws below stay inside these ranges and needn't reach their ends.
All inputs are finite; a program needn't handle non-finite values. No bound on the sum of `mappable` on one device may be relied on, other than what follows from the above.
Results may differ from the reference program's by a relative error of at most 0.035.
Values may be sent and summed in bfloat16 or wider, within the bound.
A program may use at most 64 MiB of HBM per device.

```python
import math
import jax
import jax.numpy as jnp
from jax import lax

D = 1024
HEADS = 8
HEAD = 128
C = 128
CONVS = 2
TILE = 128
DIAG = 32
L = 4096
N_SEQ = 32
N_BAND = 8


def paired_weights(key):
    shape = (D, HEADS * HEAD)
    query_part = jnp.clip(jnp.clip(jax.random.normal(jax.random.fold_in(key, 101), shape, jnp.float32), -6.0, 6.0) * (1.4 / math.sqrt(D)), -1.0, 1.0)
    key_part = jnp.clip(jnp.clip(jax.random.normal(jax.random.fold_in(key, 102), shape, jnp.float32), -6.0, 6.0) * (1.4 / math.sqrt(D)), -4.0, 4.0)
    return (query_part, key_part)


def draw_w_query(key, part):
    return paired_weights(key)[0].astype(jnp.bfloat16)


def draw_w_key(key, part):
    return paired_weights(key)[1].astype(jnp.bfloat16)


def place_ends(values, stream_key, least, high):
    longest = values.shape.index(max(values.shape))
    spots = []
    for shift in (0, 1):
        where = [jax.random.randint(jax.random.fold_in(stream_key, axis), (), 0, length) for axis, length in enumerate(values.shape)]
        where[longest] = (where[longest] + shift) % values.shape[longest]
        spots.append(tuple(where))
    return values.at[spots[0]].set(least).at[spots[1]].set(high)


def levels(stream_key, dims, split, least, high):
    def one(position, blocks):
        draws = jax.random.uniform(jax.random.fold_in(jax.random.fold_in(stream_key, 6), position), (blocks,), jnp.float32, least / len(split), high / len(split))
        return jnp.repeat(jnp.exp(draws), dims[position] // blocks).reshape((-1,) + (1,) * (len(dims) - position - 1))

    level = one(*split[0])
    for cut in split[1:]:
        level = level * one(*cut)
    return level


def noise(rng, extent, scale, limit, shards=(), kind=jnp.bfloat16):
    array = scale * jax.random.normal(rng, extent, jnp.float32)
    if shards:
        array = array * levels(rng, extent, shards, -0.22, 0.18)
    return jnp.clip(array, -limit, limit).astype(kind)


def setup_inputs(seed: int = 0) -> dict:
    keys = jax.random.split(jax.random.key(seed), 14)
    tokens = noise(keys[0], (L, D), 1.0, 6.0, ((0, 32), (1, 8)))
    mappable = place_ends((jax.random.randint(keys[1], (L,), 0, 8) < 7).astype(jnp.int32), jax.random.fold_in(keys[1], 1), 0, 1)
    attn_gain = jnp.clip(1.0 + 0.18 * jax.random.normal(keys[2], (D,), jnp.float32), 0.1, 1.9)
    w_query = draw_w_query(jax.random.fold_in(keys[13], 71), 0)
    w_key = draw_w_key(jax.random.fold_in(keys[13], 71), 0)
    w_value = noise(keys[5], (D, HEADS * HEAD), D ** -0.5, 0.1875, ((1, 8),))
    w_out = noise(keys[6], (HEADS * HEAD, D), (4.0 / (HEADS * HEAD) ** 0.5), 0.75, ((0, 8),))
    w_left = noise(keys[7], (D, C), D ** -0.5, 0.1875)
    w_right = noise(keys[8], (D, C), D ** -0.5, 0.1875)
    conv_gain = jnp.clip(1.0 + 0.18 * jax.random.normal(keys[9], (CONVS, C), jnp.float32), 0.1, 1.9)
    conv_kernel = noise(keys[10], (CONVS, 3, 3, C, C), (9 * C) ** -0.5, 0.1875)
    conv_bias = noise(keys[11], (CONVS, C), 0.5, 3.0, (), jnp.float32)
    contact_weight = noise(keys[12], (C,), C ** -0.5, 0.5, (), jnp.float32)
    return dict(tokens=tokens, mappable=mappable, attn_gain=attn_gain, w_query=w_query, w_key=w_key, w_value=w_value, w_out=w_out, w_left=w_left, w_right=w_right, conv_gain=conv_gain, conv_kernel=conv_kernel, conv_bias=conv_bias, contact_weight=contact_weight)


epsilon = 1e-06

def rms_scale(values, gain):
    floats = values.astype(jnp.float32)
    return floats * lax.rsqrt(lax.optimization_barrier(jnp.mean(floats * floats, axis=-1, keepdims=True)) + epsilon) * gain

def shear_conv(padded, kernel, spread):
    out_rows = padded.shape[0] - 2 * spread
    out_diags = padded.shape[1] - 4 * spread
    result = jnp.zeros((out_rows, out_diags, kernel.shape[-1]), jnp.float32)
    for tap_row in range(3):
        for tap_col in range(3):
            row_first = spread * tap_row
            diag_first = 2 * spread + spread * (tap_col - tap_row)
            window = padded[row_first:row_first + out_rows, diag_first:diag_first + out_diags]
            result = result + jnp.einsum('aec,cf->aef', window.astype(jnp.float32), kernel[tap_row, tap_col].astype(jnp.float32))
    return result

def valid_cells(row_first, diag_first, row_count, diag_count, length, band_width):
    rows_glob = row_first + jnp.arange(row_count, dtype=jnp.int32)
    diags_glob = diag_first + jnp.arange(diag_count, dtype=jnp.int32)
    inside = (rows_glob[:, None] >= 0) & (rows_glob[:, None] < length) & (diags_glob[None, :] >= 0) & (diags_glob[None, :] < band_width) & (rows_glob[:, None] + diags_glob[None, :] < length)
    return jnp.where(inside, 1.0, 0.0).astype(jnp.float32)[:, :, None]

def reference(tokens, mappable, attn_gain, w_query, w_key, w_value, w_out, w_left, w_right, conv_gain, conv_kernel, conv_bias, contact_weight):
    length = TILE * N_SEQ
    band_width = DIAG * N_BAND
    normed = rms_scale(tokens, attn_gain).astype(jnp.bfloat16)
    query = jnp.dot(normed, w_query, preferred_element_type=jnp.float32).astype(jnp.bfloat16)
    key_rows = jnp.dot(normed, w_key, preferred_element_type=jnp.float32).astype(jnp.bfloat16)
    value = jnp.dot(normed, w_value, preferred_element_type=jnp.float32).astype(jnp.bfloat16)
    key_offset = ((mappable - 1).astype(jnp.float32) * 1000000000.0).astype(jnp.bfloat16)
    query_heads = query.reshape(length, HEADS, HEAD).transpose(1, 0, 2)
    key_heads = key_rows.reshape(length, HEADS, HEAD).transpose(1, 0, 2)
    value_heads = value.reshape(length, HEADS, HEAD).transpose(1, 0, 2)

    def one_head(parts):
        head_query, head_key, head_value = parts
        scores = jnp.dot(head_query, head_key.T, preferred_element_type=jnp.float32) * HEAD ** (-0.5) + key_offset.astype(jnp.float32)[None, :]
        row_top = lax.optimization_barrier(jnp.max(scores, axis=1, keepdims=True))
        weights = jnp.exp(scores - row_top)
        weight_sum = lax.optimization_barrier(jnp.sum(weights, axis=1, keepdims=True))
        mixed = jnp.dot(weights.astype(jnp.bfloat16), head_value, preferred_element_type=jnp.float32)
        return (mixed / weight_sum).astype(jnp.bfloat16)
    attended_heads = lax.map(one_head, (query_heads, key_heads, value_heads))
    attended = attended_heads.transpose(1, 0, 2).reshape(length, HEADS * HEAD)
    trunk_out = (tokens.astype(jnp.float32) + jnp.dot(attended, w_out, preferred_element_type=jnp.float32)).astype(jnp.bfloat16)
    keep_rows = mappable.astype(jnp.bfloat16)[:, None]
    left_side = jnp.dot(trunk_out, w_left, preferred_element_type=jnp.float32).astype(jnp.bfloat16) * keep_rows
    right_side = jnp.dot(trunk_out, w_right, preferred_element_type=jnp.float32).astype(jnp.bfloat16) * keep_rows
    margin_rows = 2 ** CONVS - 1
    margin_diags = 2 * margin_rows
    left_padded = jnp.pad(left_side, ((margin_rows, margin_rows), (0, 0)))
    right_padded = jnp.pad(right_side, ((margin_rows + margin_diags, margin_rows + margin_diags + band_width), (0, 0)))

    def one_block(block_index):
        row_first = block_index * TILE - margin_rows
        row_count = TILE + 2 * margin_rows
        diag_count = band_width + 2 * margin_diags
        rows_glob = row_first + jnp.arange(row_count, dtype=jnp.int32)
        diags_glob = jnp.arange(diag_count, dtype=jnp.int32) - margin_diags
        left_rows = lax.dynamic_slice_in_dim(left_padded, block_index * TILE, row_count, 0)
        columns = rows_glob[:, None] + diags_glob[None, :] + (margin_rows + margin_diags)
        right_cells = jnp.take(right_padded, columns, axis=0)
        diag_first = -margin_diags
        pair_field = (left_rows[:, None, :].astype(jnp.float32) * right_cells.astype(jnp.float32) * valid_cells(row_first, diag_first, row_count, diag_count, length, band_width)).astype(jnp.bfloat16)
        for layer_index in range(CONVS):
            spread = 2 ** layer_index
            activated = jax.nn.gelu(rms_scale(pair_field, conv_gain[layer_index])).astype(jnp.bfloat16)
            conv_term = shear_conv(activated, conv_kernel[layer_index], spread)
            row_first = row_first + spread
            diag_first = diag_first + 2 * spread
            interior = pair_field[spread:pair_field.shape[0] - spread, 2 * spread:pair_field.shape[1] - 2 * spread]
            pair_field = ((interior.astype(jnp.float32) + conv_term + conv_bias[layer_index]) * valid_cells(row_first, diag_first, interior.shape[0], interior.shape[1], length, band_width)).astype(jnp.bfloat16)
        return lax.optimization_barrier(jnp.sum(pair_field.astype(jnp.float32) * contact_weight, axis=-1))
    contacts = lax.map(one_block, jnp.arange(length // TILE, dtype=jnp.int32)).reshape(length, band_width)
    return (trunk_out, contacts)
```

```python
import jax
import jax.numpy as jnp
from jax import lax
from jax.experimental import pallas as pl
from jax.experimental.pallas import tpu as pltpu
from jax.sharding import PartitionSpec as P

HEAD = 128
DIAG = 32
BINS = 128
EPS = 1e-06
BANDS = 8
RING = 8
SEQ = 32
MESH = pl.DeviceIdType.MESH
F32 = jnp.float32
BF16 = jnp.bfloat16


def remote(src, dst, send_sem, recv_sem, **device):
    return pltpu.make_async_remote_copy(
        src_ref=src,
        dst_ref=dst,
        send_sem=send_sem,
        recv_sem=recv_sem,
        device_id=device,
        device_id_type=MESH,
    )


def trunk_kernel(
    tok_ref,
    map_ref,
    gain_ref,
    wq_ref,
    wk_ref,
    wv_ref,
    wout_ref,
    wl_ref,
    wr_ref,
    trunk_ref,
    left_ref,
    right_ref,
    tok_all,
    wqkv,
    wout,
    wlr,
    m_all,
    wcol_all,
    q_all,
    kv,
    o_send,
    o_recv,
    st_send,
    st_recv,
    att_all,
    leftbuf,
    rightbuf,
    local_sem,
    tok_s,
    tok_r,
    m_s,
    m_r,
    wc_s,
    wc_r,
    q_s,
    q_r,
    kv_s,
    kv_r,
    o_s,
    o_r,
    st_s,
    st_r,
    att_s,
    att_r,
    edge_s,
    edge_r,
):
    seq = lax.axis_index("seq")
    band = lax.axis_index("band")
    core = seq % 2
    ring = (seq // 2) % RING
    half = seq // (2 * RING)

    def seq_of(half_, ring_, core_):
        return half_ * (2 * RING) + ring_ * 2 + core_

    up = seq_of(half, (ring + 1) % RING, core)
    down = seq_of(half, (ring + RING - 1) % RING, core)
    mates = [
        None,
        seq_of(half, ring, 1 - core),
        seq_of(1 - half, ring, core),
        seq_of(1 - half, ring, 1 - core),
    ]
    near = {k: (seq + SEQ + k) % SEQ for k in (-3, -2, -1, 1, 2, 3)}

    def to_band(k):
        return (band + k) % BANDS

    def from_band(k):
        return (band + BANDS - k) % BANDS

    loads = [
        pltpu.make_async_copy(wout_ref, wout, local_sem.at[0]),
        pltpu.make_async_copy(wl_ref, wlr.at[:, pl.ds(0, 128)], local_sem.at[1]),
        pltpu.make_async_copy(wr_ref, wlr.at[:, pl.ds(128, 128)], local_sem.at[2]),
        pltpu.make_async_copy(wq_ref, wqkv.at[:, pl.ds(0, 128)], local_sem.at[3]),
        pltpu.make_async_copy(wk_ref, wqkv.at[:, pl.ds(128, 128)], local_sem.at[4]),
        pltpu.make_async_copy(wv_ref, wqkv.at[:, pl.ds(256, 128)], local_sem.at[5]),
    ]
    for load in loads:
        load.start()

    barrier = pltpu.get_barrier_semaphore()
    greeted = 0
    for k in range(1, BANDS):
        pl.semaphore_signal(barrier, inc=1, device_id={"band": to_band(k)}, device_id_type=MESH)
        greeted += 1
    for other in [up, down] + mates[1:] + list(near.values()):
        pl.semaphore_signal(barrier, inc=1, device_id={"seq": other}, device_id_type=MESH)
        greeted += 1
    pl.semaphore_wait(barrier, greeted)

    def band_send(src, dst_all, s_sem, r_sem, k):
        return remote(src, dst_all.at[band], s_sem.at[k], r_sem.at[k], band=to_band(k))

    def band_recv(dst_all, s_sem, r_sem, k):
        slot = dst_all.at[from_band(k)]
        return remote(slot, slot, s_sem.at[k], r_sem.at[k], band=to_band(k))

    tok_sends = [band_send(tok_ref, tok_all, tok_s, tok_r, k) for k in range(1, BANDS)]
    for send in tok_sends:
        send.start()
    tok_all[band] = tok_ref[...]

    for load in loads:
        load.wait()
    m_all[band] = jnp.dot(wout[...], wlr[...], preferred_element_type=F32).astype(BF16)
    for k in range(1, BANDS):
        band_recv(tok_all, tok_s, tok_r, k).wait_recv()

    floats = jnp.concatenate([tok_all[c] for c in range(BANDS)], axis=1).astype(F32)
    inv = lax.rsqrt(jnp.mean(floats * floats, axis=-1, keepdims=True) + EPS)
    normed = (floats * inv * gain_ref[...]).astype(BF16)
    qkv = jnp.dot(normed, wqkv[...], preferred_element_type=F32)
    offset = ((map_ref[...] - 1).astype(F32) * 1000000000.0).astype(BF16)
    q_all[0] = qkv[:, 0:128].astype(BF16)
    kv[0, 0:128] = qkv[:, 128:256].astype(BF16)
    kv[0, 128:256] = qkv[:, 256:384].T.astype(BF16)
    kv[0, 256:272] = jnp.broadcast_to(offset, (16, 128))

    def kv_copy(src, dst, sem, other):
        return remote(kv.at[src], kv.at[dst], kv_s.at[sem], kv_r.at[dst], seq=other)

    kv_sends = [kv_copy(0, 1, 0, up), kv_copy(0, 7, 4, down)]
    for send in kv_sends:
        send.start()
    q_copies = [
        remote(q_all.at[0], q_all.at[k], q_s.at[k], q_r.at[k], seq=mates[k]) for k in (1, 2, 3)
    ]
    for copy in q_copies:
        copy.start()
    m_sends = [band_send(m_all.at[band], m_all, m_s, m_r, k) for k in range(1, BANDS)]
    wc_sends = [
        band_send(
            wout.at[:, pl.ds(pl.multiple_of(to_band(k) * 128, 128), 128)], wcol_all, wc_s, wc_r, k
        )
        for k in range(1, BANDS)
    ]
    for send in m_sends + wc_sends:
        send.start()
    wcol_all[band] = wout[:, pl.ds(pl.multiple_of(band * 128, 128), 128)]
    lr_tok = jnp.dot(floats.astype(BF16), wlr[...], preferred_element_type=F32)
    for copy in q_copies:
        copy.wait_recv()
    queries = jnp.concatenate([q_all[k] for k in range(4)], axis=0)

    def attend(state, slots):
        keys = jnp.concatenate([kv[j, 0:128] for j in slots], axis=0)
        values_t = jnp.concatenate([kv[j, 128:256] for j in slots], axis=1)
        offs = jnp.concatenate(
            [
                jnp.broadcast_to(kv[j, 256:272][0:1].astype(F32), (128, 128)).T
                for j in slots
            ],
            axis=0,
        )
        offs = jnp.concatenate([offs] * 4, axis=1)
        scores = (
            lax.dot_general(
                keys, queries, (((1,), (1,)), ((), ())), preferred_element_type=F32
            )
            * HEAD ** (-0.5)
            + offs
        )
        block_top = jnp.max(scores, axis=0, keepdims=True)
        if state is None:
            top = block_top
        else:
            top = jnp.maximum(state[0], block_top)
        weights = jnp.exp(scores - top)
        block_sum = jnp.sum(weights, axis=0, keepdims=True)
        mixed = jnp.dot(values_t, weights.astype(BF16), preferred_element_type=F32)
        if state is None:
            return top, block_sum, mixed
        fade = jnp.exp(state[0] - top)
        return top, state[1] * fade + block_sum, state[2] * fade + mixed

    state = attend(None, [0])
    for t in (1, 2, 3, 4):
        kv_copy(t, t, t, up).wait_recv()
        if t < 4:
            send = kv_copy(t, t + 1, t, up)
            send.start()
            kv_sends.append(send)
            low = RING - t
            kv_copy(low, low, t, down).wait_recv()
            if t < 3:
                send = kv_copy(low, low - 1, 4 + t, down)
                send.start()
                kv_sends.append(send)
            state = attend(state, [t, low])
        else:
            state = attend(state, [t])

    top, total, mixed = state
    mixed = mixed / total
    o_copies = []
    for k in (1, 2, 3):
        lanes = slice(k * 128, (k + 1) * 128)
        o_send[k] = mixed[:, lanes].astype(BF16)
        st_send[k, 0:4] = jnp.broadcast_to(top[:, lanes], (4, 128))
        st_send[k, 4:8] = jnp.broadcast_to(total[:, lanes], (4, 128))
        o_copies.append(
            remote(st_send.at[k], st_recv.at[k], st_s.at[k], st_r.at[k], seq=mates[k])
        )
        o_copies.append(remote(o_send.at[k], o_recv.at[k], o_s.at[k], o_r.at[k], seq=mates[k]))
    for copy in o_copies:
        copy.start()
    keep = jnp.broadcast_to(map_ref[...].astype(F32), (128, 128)).T
    keep = jnp.concatenate([keep, keep], axis=1)
    for copy in o_copies:
        copy.wait_recv()
    tops = [top[:, 0:128]] + [st_recv[k, 0:1] for k in (1, 2, 3)]
    sums = [total[:, 0:128]] + [st_recv[k, 4:5] for k in (1, 2, 3)]
    parts = [mixed[:, 0:128]] + [o_recv[k].astype(F32) for k in (1, 2, 3)]
    best = jnp.maximum(jnp.maximum(tops[0], tops[1]), jnp.maximum(tops[2], tops[3]))
    shares = [s * jnp.exp(t - best) for s, t in zip(sums, tops)]
    share_sum = shares[0] + shares[1] + shares[2] + shares[3]
    attended = (
        parts[0] * shares[0] + parts[1] * shares[1] + parts[2] * shares[2] + parts[3] * shares[3]
    ) / share_sum
    att_all[band] = attended.T.astype(BF16)
    att_sends = [band_send(att_all.at[band], att_all, att_s, att_r, k) for k in range(1, BANDS)]
    for send in att_sends:
        send.start()
    for k in range(1, BANDS):
        band_recv(m_all, m_s, m_r, k).wait_recv()
        band_recv(wcol_all, wc_s, wc_r, k).wait_recv()
    for k in range(1, BANDS):
        band_recv(att_all, att_s, att_r, k).wait_recv()

    heads = jnp.concatenate([att_all[c] for c in range(BANDS)], axis=1)
    both = lr_tok + jnp.dot(
        heads, m_all[...].reshape(BANDS * 128, 256), preferred_element_type=F32
    )
    both = (both * keep).astype(BF16)
    leftbuf[16:144] = both[:, 0:128]
    rightbuf[16:144] = both[:, 128:256]

    def edge(src, dst, sem, other):
        return remote(src, dst, edge_s.at[sem], edge_r.at[sem], seq=other)

    own = rightbuf.at[pl.ds(16, 128)]
    edges = [
        edge(own, rightbuf.at[pl.ds(144, 128)], 0, near[-1]),
        edge(own, rightbuf.at[pl.ds(272, 128)], 1, near[-2]),
        edge(rightbuf.at[pl.ds(16, 16)], rightbuf.at[pl.ds(400, 16)], 2, near[-3]),
        edge(rightbuf.at[pl.ds(128, 16)], rightbuf.at[pl.ds(0, 16)], 3, near[1]),
        edge(leftbuf.at[pl.ds(16, 16)], leftbuf.at[pl.ds(144, 16)], 4, near[-1]),
        edge(leftbuf.at[pl.ds(128, 16)], leftbuf.at[pl.ds(0, 16)], 5, near[1]),
    ]
    for copy in edges:
        copy.start()
    summed = jnp.dot(
        heads, wcol_all[...].reshape(BANDS * 128, 128), preferred_element_type=F32
    )
    trunk_ref[...] = (tok_ref[...].astype(F32) + summed).astype(BF16)
    for copy in edges:
        copy.wait_recv()
    left_ref[...] = leftbuf[...]
    right_ref[...] = rightbuf[pl.ds(pl.multiple_of(band * DIAG, DIAG), 192)]
    for send in tok_sends + kv_sends + q_copies + m_sends + wc_sends + o_copies:
        send.wait_send()
    for send in att_sends + edges:
        send.wait_send()


ROWS = 144
LEAD = 8
WIDE0 = 44
WIDE1 = 40
GROUP = 4


def gelu_norm(field, gain):
    inv = lax.rsqrt(jnp.mean(field * field, axis=-1, keepdims=True) + EPS)
    x = field * inv * gain
    inner = x * (0.7978845608028654 + 0.035677408136300125 * (x * x))
    return (0.5 * x) * (1.0 + jnp.tanh(inner))


def map_kernel(
    left_ref,
    right_ref,
    gain_ref,
    kern_ref,
    bias_ref,
    weight_ref,
    out_ref,
    lf,
    rf,
    act0,
    field1,
    act1,
):
    seq = lax.axis_index("seq")
    band = lax.axis_index("band")
    length = SEQ * BINS
    lf[...] = left_ref[...].astype(F32)
    rf[...] = right_ref[...].astype(F32)
    place = lax.broadcasted_iota(jnp.int32, (ROWS, 128), 0)
    first = seq * BINS - LEAD

    def bounds(diag):
        known = (diag >= 0) & (diag < BANDS * DIAG)
        low = -first
        high = jnp.minimum(length, length - diag) - first
        return low, jnp.where(known, high, low)

    def masked(value, diag):
        low, high = bounds(diag)
        return jnp.where((place >= low) & (place < high), value, 0.0)

    def start_field(delta):
        value = lf[LEAD : LEAD + ROWS] * rf[pl.ds(delta + 2, ROWS)]
        return masked(value, band * DIAG + delta - 6).astype(BF16).astype(F32)

    gain0 = gain_ref[0:1]
    gain1 = gain_ref[1:2]

    @pl.loop(0, WIDE0)
    def _(delta):
        act = gelu_norm(start_field(delta), gain0)
        act0[0, delta] = pltpu.roll(act, 1, 0).astype(BF16)
        act0[1, delta] = act.astype(BF16)
        act0[2, delta] = pltpu.roll(act, ROWS - 1, 0).astype(BF16)

    @pl.loop(0, WIDE1 // GROUP)
    def _(step):
        diag = step * GROUP
        taps = jnp.concatenate(
            [
                act0[p, pl.ds(diag + 2 + q - p, GROUP)].reshape(GROUP * ROWS, 128)
                for p in range(3)
                for q in range(3)
            ],
            axis=1,
        )
        term = jnp.dot(taps, kern_ref[0], preferred_element_type=F32)
        for g in range(GROUP):
            value = term[g * ROWS : (g + 1) * ROWS] + start_field(diag + g + 2) + bias_ref[0:1]
            value = masked(value, band * DIAG + diag + g - 4).astype(BF16)
            field1[diag + g] = value
            act = gelu_norm(value.astype(F32), gain1)
            act1[0, diag + g] = pltpu.roll(act, 2, 0)[LEAD : LEAD + BINS].astype(BF16)
            act1[1, diag + g] = act[LEAD : LEAD + BINS].astype(BF16)
            act1[2, diag + g] = pltpu.roll(act, ROWS - 2, 0)[LEAD : LEAD + BINS].astype(BF16)

    lane = lax.broadcasted_iota(jnp.int32, (BINS, 128), 1)
    spot = lax.broadcasted_iota(jnp.int32, (BINS, 128), 0) + seq * BINS

    def last(step, found):
        diag = step * GROUP
        taps = jnp.concatenate(
            [
                act1[p, pl.ds(diag + 4 + 2 * (q - p), GROUP)].reshape(GROUP * BINS, 128)
                for p in range(3)
                for q in range(3)
            ],
            axis=1,
        )
        term = jnp.dot(taps, kern_ref[1], preferred_element_type=F32)
        for g in range(GROUP):
            value = (
                term[g * BINS : (g + 1) * BINS]
                + field1[diag + g + 4].astype(F32)[LEAD : LEAD + BINS]
                + bias_ref[1:2]
            )
            value = jnp.where(spot + (band * DIAG + diag + g) < length, value, 0.0)
            value = value.astype(BF16).astype(F32)
            contact = jnp.sum(value * weight_ref[...], axis=-1, keepdims=True)
            found = jnp.where(lane == diag + g, contact, found)
        return found

    found = lax.fori_loop(0, DIAG // GROUP, last, jnp.zeros((BINS, 128), F32))
    out_ref[...] = found[:, 0:DIAG]


def local(
    tokens,
    mappable,
    attn_gain,
    w_query,
    w_key,
    w_value,
    w_out,
    w_left,
    w_right,
    conv_gain,
    conv_kernel,
    conv_bias,
    contact_weight,
):
    vmem = pl.BlockSpec(memory_space=pltpu.VMEM)
    anywhere = pl.BlockSpec(memory_space=pl.ANY)
    dma = pltpu.SemaphoreType.DMA
    trunk_out, left, right = pl.pallas_call(
        trunk_kernel,
        out_shape=(
            jax.ShapeDtypeStruct((BINS, 128), BF16),
            jax.ShapeDtypeStruct((160, 128), BF16),
            jax.ShapeDtypeStruct((192, 128), BF16),
        ),
        in_specs=[vmem] * 3 + [anywhere] * 6,
        out_specs=(vmem, vmem, vmem),
        scratch_shapes=[
            pltpu.VMEM((BANDS, 128, 128), BF16),
            pltpu.VMEM((1024, 384), BF16),
            pltpu.VMEM((128, 1024), BF16),
            pltpu.VMEM((1024, 256), BF16),
            pltpu.VMEM((BANDS, 128, 256), BF16),
            pltpu.VMEM((BANDS, 128, 128), BF16),
            pltpu.VMEM((4, 128, 128), BF16),
            pltpu.VMEM((RING, 272, 128), BF16),
            pltpu.VMEM((4, 128, 128), BF16),
            pltpu.VMEM((4, 128, 128), BF16),
            pltpu.VMEM((4, 8, 128), F32),
            pltpu.VMEM((4, 8, 128), F32),
            pltpu.VMEM((BANDS, 128, 128), BF16),
            pltpu.VMEM((160, 128), BF16),
            pltpu.VMEM((416, 128), BF16),
            dma((6,)),
        ]
        + [dma((8,)) for _ in range(18)],
        compiler_params=pltpu.CompilerParams(
            collective_id=0, has_side_effects=True, vmem_limit_bytes=32 * 1024 * 1024
        ),
    )(
        tokens,
        mappable.reshape(1, BINS),
        attn_gain.reshape(1, -1),
        w_query,
        w_key,
        w_value,
        w_out,
        w_left,
        w_right,
    )
    contacts = pl.pallas_call(
        map_kernel,
        out_shape=jax.ShapeDtypeStruct((BINS, DIAG), F32),
        in_specs=[vmem] * 6,
        out_specs=vmem,
        scratch_shapes=[
            pltpu.VMEM((160, 128), F32),
            pltpu.VMEM((192, 128), F32),
            pltpu.VMEM((3, WIDE0, ROWS, 128), BF16),
            pltpu.VMEM((WIDE1, ROWS, 128), BF16),
            pltpu.VMEM((3, WIDE1, BINS, 128), BF16),
        ],
        compiler_params=pltpu.CompilerParams(vmem_limit_bytes=40 * 1024 * 1024),
    )(
        left,
        right,
        conv_gain,
        conv_kernel.reshape(2, 9 * 128, 128),
        conv_bias,
        contact_weight.reshape(1, 128),
    )
    return (trunk_out, contacts)


def solution(mesh):
    return jax.shard_map(
        local,
        mesh=mesh,
        in_specs=(
            P("seq", "band"),
            P("seq"),
            P(),
            P(None, "band"),
            P(None, "band"),
            P(None, "band"),
            P("band", None),
            P(),
            P(),
            P(),
            P(),
            P(),
            P(),
        ),
        out_specs=(P("seq", "band"), P("seq", "band")),
        check_vma=False,
    )
```

```python
import jax
import jax.numpy as jnp
from jax import lax
from jax.experimental import pallas as pl
from jax.experimental.pallas import tpu as pltpu
from jax.sharding import PartitionSpec as P

HEAD = 128
DIAG = 32
BINS = 128
EPS = 1e-06
BANDS = 8
RING = 8
SEQ = 32
MESH = pl.DeviceIdType.MESH
F32 = jnp.float32
BF16 = jnp.bfloat16


def remote(src, dst, send_sem, recv_sem, **device):
    return pltpu.make_async_remote_copy(
        src_ref=src,
        dst_ref=dst,
        send_sem=send_sem,
        recv_sem=recv_sem,
        device_id=device,
        device_id_type=MESH,
    )


def trunk_kernel(
    tok_ref,
    map_ref,
    gain_ref,
    wq_ref,
    wk_ref,
    wv_ref,
    wout_ref,
    wl_ref,
    wr_ref,
    trunk_ref,
    left_ref,
    right_ref,
    tok_all,
    gain_v,
    map_v,
    wqkv,
    wout,
    wlr,
    m_all,
    wcol_all,
    q_all,
    kv,
    o_send,
    o_recv,
    st_send,
    st_recv,
    att_all,
    leftbuf,
    rightbuf,
    local_sem,
    tok_s,
    tok_r,
    m_s,
    m_r,
    wc_s,
    wc_r,
    q_s,
    q_r,
    kv_s,
    kv_r,
    o_s,
    o_r,
    st_s,
    st_r,
    att_s,
    att_r,
    edge_s,
    edge_r,
):
    seq = lax.axis_index("seq")
    band = lax.axis_index("band")
    core = seq % 2
    ring = (seq // 2) % RING
    half = seq // (2 * RING)

    def seq_of(half_, ring_, core_):
        return half_ * (2 * RING) + ring_ * 2 + core_

    up = seq_of(half, (ring + 1) % RING, core)
    down = seq_of(half, (ring + RING - 1) % RING, core)
    mates = [
        None,
        seq_of(half, ring, 1 - core),
        seq_of(1 - half, ring, core),
        seq_of(1 - half, ring, 1 - core),
    ]
    near = {k: (seq + SEQ + k) % SEQ for k in (-3, -2, -1, 1, 2, 3)}

    def to_band(k):
        return (band + k) % BANDS

    def from_band(k):
        return (band + BANDS - k) % BANDS

    loads = [
        pltpu.make_async_copy(wout_ref, wout, local_sem.at[0]),
        pltpu.make_async_copy(wl_ref, wlr.at[:, pl.ds(0, 128)], local_sem.at[1]),
        pltpu.make_async_copy(wr_ref, wlr.at[:, pl.ds(128, 128)], local_sem.at[2]),
        pltpu.make_async_copy(wq_ref, wqkv.at[:, pl.ds(0, 128)], local_sem.at[3]),
        pltpu.make_async_copy(wk_ref, wqkv.at[:, pl.ds(128, 128)], local_sem.at[4]),
        pltpu.make_async_copy(wv_ref, wqkv.at[:, pl.ds(256, 128)], local_sem.at[5]),
        pltpu.make_async_copy(gain_ref, gain_v, local_sem.at[6]),
        pltpu.make_async_copy(map_ref, map_v, local_sem.at[7]),
        pltpu.make_async_copy(tok_ref, tok_all.at[band], local_sem.at[8]),
    ]
    for load in loads:
        load.start()

    barrier = pltpu.get_barrier_semaphore()
    greeted = 0
    for k in range(1, BANDS):
        pl.semaphore_signal(barrier, inc=1, device_id={"band": to_band(k)}, device_id_type=MESH)
        greeted += 1
    for other in [up, down] + mates[1:] + list(near.values()):
        pl.semaphore_signal(barrier, inc=1, device_id={"seq": other}, device_id_type=MESH)
        greeted += 1
    pl.semaphore_wait(barrier, greeted)

    def band_send(src, dst_all, s_sem, r_sem, k):
        return remote(src, dst_all.at[band], s_sem.at[k], r_sem.at[k], band=to_band(k))

    def band_recv(dst_all, s_sem, r_sem, k):
        slot = dst_all.at[from_band(k)]
        return remote(slot, slot, s_sem.at[k], r_sem.at[k], band=to_band(k))

    tok_sends = [band_send(tok_ref, tok_all, tok_s, tok_r, k) for k in range(1, BANDS)]
    for send in tok_sends:
        send.start()

    for load in loads:
        load.wait()
    m_all[band] = jnp.dot(wout[...], wlr[...], preferred_element_type=F32).astype(BF16)
    for k in range(1, BANDS):
        band_recv(tok_all, tok_s, tok_r, k).wait_recv()

    floats = jnp.concatenate([tok_all[c] for c in range(BANDS)], axis=1).astype(F32)
    inv = lax.rsqrt(jnp.mean(floats * floats, axis=-1, keepdims=True) + EPS)
    normed = (floats * inv * gain_v[...]).astype(BF16)
    qkv = jnp.dot(normed, wqkv[...], preferred_element_type=F32)
    offset = ((map_v[...] - 1).astype(F32) * 1000000000.0).astype(BF16)
    q_all[0] = qkv[:, 0:128].astype(BF16)
    kv[0, 0:128] = qkv[:, 128:256].astype(BF16)
    kv[0, 128:256] = qkv[:, 256:384].T.astype(BF16)
    kv[0, 256:272] = jnp.broadcast_to(offset, (16, 128))

    def kv_copy(src, dst, sem, other):
        return remote(kv.at[src], kv.at[dst], kv_s.at[sem], kv_r.at[dst], seq=other)

    kv_sends = [kv_copy(0, 1, 0, up), kv_copy(0, 7, 4, down)]
    for send in kv_sends:
        send.start()
    q_copies = [
        remote(q_all.at[0], q_all.at[k], q_s.at[k], q_r.at[k], seq=mates[k]) for k in (1, 2, 3)
    ]
    for copy in q_copies:
        copy.start()
    m_sends = [band_send(m_all.at[band], m_all, m_s, m_r, k) for k in range(1, BANDS)]
    wc_sends = [
        band_send(
            wout.at[:, pl.ds(pl.multiple_of(to_band(k) * 128, 128), 128)], wcol_all, wc_s, wc_r, k
        )
        for k in range(1, BANDS)
    ]
    for send in m_sends + wc_sends:
        send.start()
    wcol_all[band] = wout[:, pl.ds(pl.multiple_of(band * 128, 128), 128)]
    lr_tok = jnp.dot(floats.astype(BF16), wlr[...], preferred_element_type=F32)
    for copy in q_copies:
        copy.wait_recv()
    queries = jnp.concatenate([q_all[k] for k in range(4)], axis=0)

    def attend(state, slots):
        keys = jnp.concatenate([kv[j, 0:128] for j in slots], axis=0)
        values_t = jnp.concatenate([kv[j, 128:256] for j in slots], axis=1)
        offs = jnp.concatenate(
            [
                jnp.broadcast_to(kv[j, 256:272][0:1].astype(F32), (128, 128)).T
                for j in slots
            ],
            axis=0,
        )
        offs = jnp.concatenate([offs] * 4, axis=1)
        scores = (
            lax.dot_general(
                keys, queries, (((1,), (1,)), ((), ())), preferred_element_type=F32
            )
            * HEAD ** (-0.5)
            + offs
        )
        block_top = jnp.max(scores, axis=0, keepdims=True)
        if state is None:
            top = block_top
        else:
            top = jnp.maximum(state[0], block_top)
        weights = jnp.exp(scores - top)
        block_sum = jnp.sum(weights, axis=0, keepdims=True)
        mixed = jnp.dot(values_t, weights.astype(BF16), preferred_element_type=F32)
        if state is None:
            return top, block_sum, mixed
        fade = jnp.exp(state[0] - top)
        return top, state[1] * fade + block_sum, state[2] * fade + mixed

    state = attend(None, [0])
    for t in (1, 2, 3, 4):
        kv_copy(t, t, t, up).wait_recv()
        if t < 4:
            send = kv_copy(t, t + 1, t, up)
            send.start()
            kv_sends.append(send)
            low = RING - t
            kv_copy(low, low, t, down).wait_recv()
            if t < 3:
                send = kv_copy(low, low - 1, 4 + t, down)
                send.start()
                kv_sends.append(send)
            state = attend(state, [t, low])
        else:
            state = attend(state, [t])

    top, total, mixed = state
    mixed = mixed / total
    o_copies = []
    for k in (1, 2, 3):
        lanes = slice(k * 128, (k + 1) * 128)
        o_send[k] = mixed[:, lanes].astype(BF16)
        st_send[k, 0:4] = jnp.broadcast_to(top[:, lanes], (4, 128))
        st_send[k, 4:8] = jnp.broadcast_to(total[:, lanes], (4, 128))
        o_copies.append(
            remote(st_send.at[k], st_recv.at[k], st_s.at[k], st_r.at[k], seq=mates[k])
        )
        o_copies.append(remote(o_send.at[k], o_recv.at[k], o_s.at[k], o_r.at[k], seq=mates[k]))
    for copy in o_copies:
        copy.start()
    keep = jnp.broadcast_to(map_v[...].astype(F32), (128, 128)).T
    keep = jnp.concatenate([keep, keep], axis=1)
    for copy in o_copies:
        copy.wait_recv()
    tops = [top[:, 0:128]] + [st_recv[k, 0:1] for k in (1, 2, 3)]
    sums = [total[:, 0:128]] + [st_recv[k, 4:5] for k in (1, 2, 3)]
    parts = [mixed[:, 0:128]] + [o_recv[k].astype(F32) for k in (1, 2, 3)]
    best = jnp.maximum(jnp.maximum(tops[0], tops[1]), jnp.maximum(tops[2], tops[3]))
    shares = [s * jnp.exp(t - best) for s, t in zip(sums, tops)]
    share_sum = shares[0] + shares[1] + shares[2] + shares[3]
    attended = (
        parts[0] * shares[0] + parts[1] * shares[1] + parts[2] * shares[2] + parts[3] * shares[3]
    ) / share_sum
    att_all[band] = attended.T.astype(BF16)
    att_sends = [band_send(att_all.at[band], att_all, att_s, att_r, k) for k in range(1, BANDS)]
    for send in att_sends:
        send.start()
    for k in range(1, BANDS):
        band_recv(m_all, m_s, m_r, k).wait_recv()
        band_recv(wcol_all, wc_s, wc_r, k).wait_recv()
    for k in range(1, BANDS):
        band_recv(att_all, att_s, att_r, k).wait_recv()

    heads = jnp.concatenate([att_all[c] for c in range(BANDS)], axis=1)
    both = lr_tok + jnp.dot(
        heads, m_all[...].reshape(BANDS * 128, 256), preferred_element_type=F32
    )
    both = (both * keep).astype(BF16)
    leftbuf[16:144] = both[:, 0:128]
    rightbuf[16:144] = both[:, 128:256]

    def edge(src, dst, sem, other):
        return remote(src, dst, edge_s.at[sem], edge_r.at[sem], seq=other)

    own = rightbuf.at[pl.ds(16, 128)]
    edges = [
        edge(own, rightbuf.at[pl.ds(144, 128)], 0, near[-1]),
        edge(own, rightbuf.at[pl.ds(272, 128)], 1, near[-2]),
        edge(rightbuf.at[pl.ds(16, 16)], rightbuf.at[pl.ds(400, 16)], 2, near[-3]),
        edge(rightbuf.at[pl.ds(128, 16)], rightbuf.at[pl.ds(0, 16)], 3, near[1]),
        edge(leftbuf.at[pl.ds(16, 16)], leftbuf.at[pl.ds(144, 16)], 4, near[-1]),
        edge(leftbuf.at[pl.ds(128, 16)], leftbuf.at[pl.ds(0, 16)], 5, near[1]),
    ]
    for copy in edges:
        copy.start()
    summed = jnp.dot(
        heads, wcol_all[...].reshape(BANDS * 128, 128), preferred_element_type=F32
    )
    trunk_ref[...] = (tok_all[band].astype(F32) + summed).astype(BF16)
    for copy in edges:
        copy.wait_recv()
    left_ref[...] = leftbuf[...]
    right_ref[...] = rightbuf[pl.ds(pl.multiple_of(band * DIAG, DIAG), 192)]
    for send in tok_sends + kv_sends + q_copies + m_sends + wc_sends + o_copies:
        send.wait_send()
    for send in att_sends + edges:
        send.wait_send()


CHUNK = 9
LANES = 16
ROWS = CHUNK * LANES
LEAD = 8
WIDE0 = 44
WIDE1 = 40
GROUP = 4


def norm_gelu(field, half_gain, keep):
    squares = jnp.sum(field * field, axis=-1, keepdims=True)
    inv = lax.rsqrt(squares + HEAD * EPS)
    if keep is not None:
        inv = jnp.where(keep, inv, 0.0)
    half = field * inv * half_gain
    inner = half * (1.5957691216057308 + 0.285419265090401 * (half * half))
    return half + half * jnp.tanh(inner)


def map_kernel(
    left_ref,
    right_ref,
    trunk_ref,
    gain_ref,
    kern_ref,
    bias_ref,
    weight_ref,
    out_ref,
    trunk_out_ref,
    lf,
    rf,
    lp,
    rp,
    act0,
    field1,
    act1,
    taps_w,
    plain,
    sems,
):
    seq = lax.axis_index("seq")
    band = lax.axis_index("band")
    length = SEQ * BINS
    copies = [pltpu.make_async_copy(trunk_ref, trunk_out_ref, sems.at[12])]
    for layer in range(2):
        for p in range(3):
            for second in range(2):
                copies.append(
                    pltpu.make_async_copy(
                        kern_ref.at[layer, p],
                        taps_w.at[layer, pl.ds(4 * p + second, 3), :, pl.ds(128 * second, 128)],
                        sems.at[layer * 6 + p * 2 + second],
                    )
                )
    for copy in copies:
        copy.start()
    for layer in range(2):
        for p in range(3):
            taps_w[layer, 4 * p + 3, :, 0:128] = jnp.zeros((128, 128), BF16)
            taps_w[layer, 4 * p, :, 128:256] = jnp.zeros((128, 128), BF16)
    lf[...] = left_ref[...].astype(F32)
    rf[0:192] = right_ref[...].astype(F32)
    for a in range(CHUNK):
        lp[a] = lf[pl.ds(LEAD + a, LANES, stride=CHUNK)]
    for t in range(WIDE0 + CHUNK - 1):
        rp[t] = rf[pl.ds(t + 2, LANES, stride=CHUNK)]

    shape = (CHUNK, LANES, 128)
    first = seq * BINS - LEAD
    spot = (
        lax.broadcasted_iota(jnp.int32, shape, 0)
        + lax.broadcasted_iota(jnp.int32, shape, 1) * CHUNK
        + first
    )

    def inside(diag):
        known = (diag >= 0) & (diag < BANDS * DIAG)
        high = jnp.where(known, jnp.minimum(length, length - diag), 0)
        return (spot >= 0) & (spot < high)

    def start_field(delta):
        return lp[...] * rp[pl.ds(delta, CHUNK)]

    root = float(HEAD) ** 0.5 * 0.5
    gain0 = gain_ref[0:1].reshape(1, 1, 128) * root
    gain1 = gain_ref[1:2].reshape(1, 1, 128) * root
    bias0 = bias_ref[0:1].reshape(1, 1, 128)
    bias1 = bias_ref[1:2].reshape(1, 1, 128)
    weight = weight_ref[...].reshape(1, 1, 128)

    def put(dst, where, act, reach):
        dst[where, pl.ds(reach, CHUNK)] = act.astype(BF16)
        before = pltpu.roll(act[CHUNK - reach :], 1, 1)
        after = pltpu.roll(act[:reach], LANES - 1, 1)
        dst[where, pl.ds(0, reach)] = before.astype(BF16)
        dst[where, pl.ds(reach + CHUNK, reach)] = after.astype(BF16)

    def first_act(delta):
        keep = inside(band * DIAG + delta - 6)
        put(act0, delta, norm_gelu(start_field(delta), gain0, keep), 1)

    def conv(src, layer, slabs, reach):
        taps = jnp.concatenate(
            [
                jnp.concatenate(
                    [
                        src[slab + reach * (j - p), pl.ds(reach * p, CHUNK)].reshape(ROWS, 128)
                        for slab in slabs
                    ],
                    axis=0,
                )
                for p in range(3)
                for j in range(4)
            ],
            axis=1,
        )
        return jnp.dot(
            taps, taps_w[layer].reshape(12 * 128, 256), preferred_element_type=F32
        )

    def second_act(step, term):
        diag = step * GROUP
        for g in range(GROUP):
            pair, half = g // 2, g % 2
            block = term[pair * ROWS : (pair + 1) * ROWS, half * 128 : (half + 1) * 128]
            value = block.reshape(shape) + start_field(diag + g + 2) + bias0
            field1[diag + g] = value.astype(BF16)
            keep = inside(band * DIAG + diag + g - 4)
            put(act1, diag + g, norm_gelu(value, gain1, keep), 2)

    @pl.loop(0, 2)
    def _(step):
        for g in range(GROUP):
            first_act(step * GROUP + g)

    for copy in copies:
        copy.wait()

    def conv0(step):
        slab = step * GROUP + 2
        return conv(act0, 0, [slab, slab + 2], 1)

    def grow(step, term):
        fresh = conv0(step)
        second_act(step - 1, term)
        for g in range(GROUP):
            first_act(step * GROUP + 8 + g)
        return fresh

    steps = WIDE1 // GROUP
    term = conv0(0)
    for g in range(GROUP):
        first_act(8 + g)
    term = lax.fori_loop(1, steps - 1, grow, term)
    fresh = conv0(steps - 1)
    second_act(steps - 2, term)
    second_act(steps - 1, fresh)

    lane = lax.broadcasted_iota(jnp.int32, shape, 2)

    def conv1(step):
        slab = step * GROUP + 4
        return conv(act1, 1, [slab, slab + 1], 2)

    def finish(step, term, found):
        diag = step * GROUP
        for g in range(GROUP):
            pair, half = g % 2, g // 2
            block = term[pair * ROWS : (pair + 1) * ROWS, half * 128 : (half + 1) * 128]
            value = block.reshape(shape) + field1[diag + g + 4].astype(F32) + bias1
            contact = jnp.sum(value * weight, axis=-1, keepdims=True)
            found = jnp.where(lane == diag + g, contact, found)
        return found

    def last(step, carry):
        term, found = carry
        fresh = conv1(step)
        return fresh, finish(step - 1, term, found)

    steps = DIAG // GROUP
    term, found = lax.fori_loop(1, steps, last, (conv1(0), jnp.zeros(shape, F32)))
    found = finish(steps - 1, term, found)
    found = jnp.where(spot + band * DIAG + lane < length, found, 0.0)
    for a in range(CHUNK):
        plain[pl.ds(a, LANES, stride=CHUNK)] = found[a]
    out_ref[...] = plain[LEAD : LEAD + BINS].T[0:DIAG]


def local(
    tokens,
    mappable,
    attn_gain,
    w_query,
    w_key,
    w_value,
    w_out,
    w_left,
    w_right,
    conv_gain,
    conv_kernel,
    conv_bias,
    contact_weight,
):
    vmem = pl.BlockSpec(memory_space=pltpu.VMEM)
    hbm = pl.BlockSpec(memory_space=pltpu.HBM)
    dma = pltpu.SemaphoreType.DMA
    trunk, left, right = pl.pallas_call(
        trunk_kernel,
        out_shape=(
            jax.ShapeDtypeStruct((BINS, 128), BF16),
            jax.ShapeDtypeStruct((160, 128), BF16),
            jax.ShapeDtypeStruct((192, 128), BF16),
        ),
        in_specs=[hbm] * 9,
        out_specs=(vmem, vmem, vmem),
        scratch_shapes=[
            pltpu.VMEM((BANDS, 128, 128), BF16),
            pltpu.VMEM((1, 1024), F32),
            pltpu.VMEM((1, BINS), jnp.int32),
            pltpu.VMEM((1024, 384), BF16),
            pltpu.VMEM((128, 1024), BF16),
            pltpu.VMEM((1024, 256), BF16),
            pltpu.VMEM((BANDS, 128, 256), BF16),
            pltpu.VMEM((BANDS, 128, 128), BF16),
            pltpu.VMEM((4, 128, 128), BF16),
            pltpu.VMEM((RING, 272, 128), BF16),
            pltpu.VMEM((4, 128, 128), BF16),
            pltpu.VMEM((4, 128, 128), BF16),
            pltpu.VMEM((4, 8, 128), F32),
            pltpu.VMEM((4, 8, 128), F32),
            pltpu.VMEM((BANDS, 128, 128), BF16),
            pltpu.VMEM((160, 128), BF16),
            pltpu.VMEM((416, 128), BF16),
            dma((9,)),
        ]
        + [dma((8,)) for _ in range(18)],
        compiler_params=pltpu.CompilerParams(
            collective_id=0, has_side_effects=True, vmem_limit_bytes=32 * 1024 * 1024
        ),
    )(
        tokens,
        mappable.reshape(1, BINS),
        attn_gain.reshape(1, -1),
        w_query,
        w_key,
        w_value,
        w_out,
        w_left,
        w_right,
    )
    contacts, trunk_out = pl.pallas_call(
        map_kernel,
        out_shape=(
            jax.ShapeDtypeStruct((DIAG, BINS), F32),
            jax.ShapeDtypeStruct((BINS, 128), BF16),
        ),
        in_specs=[vmem, vmem, vmem, vmem, hbm, vmem, vmem],
        out_specs=(vmem, hbm),
        scratch_shapes=[
            pltpu.VMEM((160, 128), F32),
            pltpu.VMEM((200, 128), F32),
            pltpu.VMEM((CHUNK, LANES, 128), F32),
            pltpu.VMEM((WIDE0 + CHUNK - 1, LANES, 128), F32),
            pltpu.VMEM((WIDE0, CHUNK + 2, LANES, 128), BF16),
            pltpu.VMEM((WIDE1, CHUNK, LANES, 128), BF16),
            pltpu.VMEM((WIDE1, CHUNK + 4, LANES, 128), BF16),
            pltpu.VMEM((2, 12, 128, 256), BF16),
            pltpu.VMEM((ROWS, 128), F32),
            dma((13,)),
        ],
        compiler_params=pltpu.CompilerParams(vmem_limit_bytes=32 * 1024 * 1024),
    )(
        left,
        right,
        trunk,
        conv_gain,
        conv_kernel,
        conv_bias,
        contact_weight.reshape(1, 128),
    )
    return (trunk_out, contacts.T)


def solution(mesh):
    return jax.shard_map(
        local,
        mesh=mesh,
        in_specs=(
            P("seq", "band"),
            P("seq"),
            P(),
            P(None, "band"),
            P(None, "band"),
            P(None, "band"),
            P("band", None),
            P(),
            P(),
            P(),
            P(),
            P(),
            P(),
        ),
        out_specs=(P("seq", "band"), P("seq", "band")),
        check_vma=False,
    )
```

```python
import jax
import jax.numpy as jnp
from jax import lax
from jax.experimental import pallas as pl
from jax.experimental.pallas import tpu as pltpu
from jax.sharding import PartitionSpec as P

HEAD = 128
DIAG = 32
BINS = 128
EPS = 1e-06
BANDS = 8
RING = 8
SEQ = 32
MESH = pl.DeviceIdType.MESH
F32 = jnp.float32
BF16 = jnp.bfloat16


def remote(src, dst, send_sem, recv_sem, **device):
    return pltpu.make_async_remote_copy(
        src_ref=src,
        dst_ref=dst,
        send_sem=send_sem,
        recv_sem=recv_sem,
        device_id=device,
        device_id_type=MESH,
    )


CHUNK = 9
LANES = 16
ROWS = CHUNK * LANES
LEAD = 8
WIDE0 = 44
WIDE1 = 40
GROUP = 4


def norm_gelu(field, half_gain, keep):
    squares = jnp.sum(field * field, axis=-1, keepdims=True)
    inv = lax.rsqrt(squares + HEAD * EPS)
    if keep is not None:
        inv = jnp.where(keep, inv, 0.0)
    half = field * inv * half_gain
    inner = half * (1.5957691216057308 + 0.285419265090401 * (half * half))
    return half + half * jnp.tanh(inner)


def pair_map(
    seq,
    band,
    leftbuf,
    rightbuf,
    gain_ref,
    bias_ref,
    weight_ref,
    out_ref,
    lf,
    rf,
    lp,
    rp,
    act0,
    field1,
    act1,
    taps_w,
    plain,
    loads,
):
    length = SEQ * BINS
    lf[...] = leftbuf[...].astype(F32)
    rf[0:192] = rightbuf[pl.ds(pl.multiple_of(band * DIAG, DIAG), 192)].astype(F32)
    for a in range(CHUNK):
        lp[a] = lf[pl.ds(LEAD + a, LANES, stride=CHUNK)]
    for t in range(WIDE0 + CHUNK - 1):
        rp[t] = rf[pl.ds(t + 2, LANES, stride=CHUNK)]

    shape = (CHUNK, LANES, 128)
    first = seq * BINS - LEAD
    spot = (
        lax.broadcasted_iota(jnp.int32, shape, 0)
        + lax.broadcasted_iota(jnp.int32, shape, 1) * CHUNK
        + first
    )

    def inside(diag):
        known = (diag >= 0) & (diag < BANDS * DIAG)
        high = jnp.where(known, jnp.minimum(length, length - diag), 0)
        return (spot >= 0) & (spot < high)

    def start_field(delta):
        return lp[...] * rp[pl.ds(delta, CHUNK)]

    root = float(HEAD) ** 0.5 * 0.5
    gain0 = gain_ref[0:1].reshape(1, 1, 128) * root
    gain1 = gain_ref[1:2].reshape(1, 1, 128) * root
    bias0 = bias_ref[0:1].reshape(1, 1, 128)
    bias1 = bias_ref[1:2].reshape(1, 1, 128)
    weight = weight_ref[...].reshape(1, 1, 128)

    def put(dst, where, act, reach):
        dst[where, pl.ds(reach, CHUNK)] = act.astype(BF16)
        before = pltpu.roll(act[CHUNK - reach :], 1, 1)
        after = pltpu.roll(act[:reach], LANES - 1, 1)
        dst[where, pl.ds(0, reach)] = before.astype(BF16)
        dst[where, pl.ds(reach + CHUNK, reach)] = after.astype(BF16)

    def first_act(delta):
        keep = inside(band * DIAG + delta - 6)
        put(act0, delta, norm_gelu(start_field(delta), gain0, keep), 1)

    def conv(src, layer, slabs, reach):
        taps = jnp.concatenate(
            [
                jnp.concatenate(
                    [
                        src[slab + reach * (j - p), pl.ds(reach * p, CHUNK)].reshape(ROWS, 128)
                        for slab in slabs
                    ],
                    axis=0,
                )
                for p in range(3)
                for j in range(4)
            ],
            axis=1,
        )
        return jnp.dot(
            taps, taps_w[layer].reshape(12 * 128, 256), preferred_element_type=F32
        )

    def second_act(step, term):
        diag = step * GROUP
        for g in range(GROUP):
            pair, half = g // 2, g % 2
            block = term[pair * ROWS : (pair + 1) * ROWS, half * 128 : (half + 1) * 128]
            value = block.reshape(shape) + start_field(diag + g + 2) + bias0
            field1[diag + g] = value.astype(BF16)
            keep = inside(band * DIAG + diag + g - 4)
            put(act1, diag + g, norm_gelu(value, gain1, keep), 2)

    @pl.loop(0, 2)
    def _(step):
        for g in range(GROUP):
            first_act(step * GROUP + g)

    for load in loads:
        load.wait()

    def conv0(step):
        slab = step * GROUP + 2
        return conv(act0, 0, [slab, slab + 2], 1)

    def grow(step, term):
        fresh = conv0(step)
        second_act(step - 1, term)
        for g in range(GROUP):
            first_act(step * GROUP + 8 + g)
        return fresh

    steps = WIDE1 // GROUP
    term = conv0(0)
    for g in range(GROUP):
        first_act(8 + g)
    term = lax.fori_loop(1, steps - 1, grow, term)
    fresh = conv0(steps - 1)
    second_act(steps - 2, term)
    second_act(steps - 1, fresh)

    lane = lax.broadcasted_iota(jnp.int32, shape, 2)

    def conv1(step):
        slab = step * GROUP + 4
        return conv(act1, 1, [slab, slab + 1], 2)

    def finish(step, term, found):
        diag = step * GROUP
        for g in range(GROUP):
            pair, half = g % 2, g // 2
            block = term[pair * ROWS : (pair + 1) * ROWS, half * 128 : (half + 1) * 128]
            value = block.reshape(shape) + field1[diag + g + 4].astype(F32) + bias1
            contact = jnp.sum(value * weight, axis=-1, keepdims=True)
            found = jnp.where(lane == diag + g, contact, found)
        return found

    def last(step, carry):
        term, found = carry
        fresh = conv1(step)
        return fresh, finish(step - 1, term, found)

    steps = DIAG // GROUP
    term, found = lax.fori_loop(1, steps, last, (conv1(0), jnp.zeros(shape, F32)))
    found = finish(steps - 1, term, found)
    found = jnp.where(spot + band * DIAG + lane < length, found, 0.0)
    for a in range(CHUNK):
        plain[pl.ds(a, LANES, stride=CHUNK)] = found[a]
    out_ref[...] = plain[LEAD : LEAD + BINS].T[0:DIAG]


def trunk_kernel(
    tok_ref,
    map_ref,
    gain_ref,
    wq_ref,
    wk_ref,
    wv_ref,
    wout_ref,
    wl_ref,
    wr_ref,
    cgain_ref,
    kern_ref,
    bias_ref,
    weight_ref,
    trunk_ref,
    out_ref,
    tok_all,
    gain_v,
    map_v,
    wqkv,
    wout,
    wlr,
    m_all,
    wcol_all,
    q_all,
    kv,
    o_send,
    o_recv,
    st_send,
    st_recv,
    att_all,
    leftbuf,
    rightbuf,
    cgain_v,
    bias_v,
    weight_v,
    lf,
    rf,
    lp,
    rp,
    act0,
    field1,
    act1,
    taps_w,
    plain,
    local_sem,
    tap_sem,
    tok_s,
    tok_r,
    m_s,
    m_r,
    wc_s,
    wc_r,
    q_s,
    q_r,
    kv_s,
    kv_r,
    o_s,
    o_r,
    st_s,
    st_r,
    att_s,
    att_r,
    edge_s,
    edge_r,
):
    seq = lax.axis_index("seq")
    band = lax.axis_index("band")
    core = seq % 2
    ring = (seq // 2) % RING
    half = seq // (2 * RING)
    row = band // 2
    side = band % 2

    def seq_of(half_, ring_, core_):
        return half_ * (2 * RING) + ring_ * 2 + core_

    along = {k: seq_of(half, (ring + RING + k) % RING, core) for k in (-2, -1, 1, 2)}
    mates = [
        None,
        seq_of(half, ring, 1 - core),
        seq_of(1 - half, ring, core),
        seq_of(1 - half, ring, 1 - core),
    ]
    near = {k: (seq + SEQ + k) % SEQ for k in (-3, -2, -1, 1, 2, 3)}

    def to_band(k):
        return (band + k) % BANDS

    def from_band(k):
        return (band + BANDS - k) % BANDS

    loads = [
        pltpu.make_async_copy(tok_ref, tok_all.at[band], local_sem.at[0]),
        pltpu.make_async_copy(gain_ref, gain_v, local_sem.at[1]),
        pltpu.make_async_copy(map_ref, map_v, local_sem.at[2]),
        pltpu.make_async_copy(wout_ref, wout, local_sem.at[3]),
        pltpu.make_async_copy(wl_ref, wlr.at[:, pl.ds(0, 128)], local_sem.at[4]),
        pltpu.make_async_copy(wr_ref, wlr.at[:, pl.ds(128, 128)], local_sem.at[5]),
        pltpu.make_async_copy(wq_ref, wqkv.at[:, pl.ds(0, 128)], local_sem.at[6]),
        pltpu.make_async_copy(wk_ref, wqkv.at[:, pl.ds(128, 128)], local_sem.at[7]),
        pltpu.make_async_copy(wv_ref, wqkv.at[:, pl.ds(256, 128)], local_sem.at[8]),
        pltpu.make_async_copy(cgain_ref, cgain_v, local_sem.at[9]),
        pltpu.make_async_copy(bias_ref, bias_v, local_sem.at[10]),
        pltpu.make_async_copy(weight_ref, weight_v, local_sem.at[11]),
    ]
    tap_loads = [
        pltpu.make_async_copy(
            kern_ref.at[layer, p],
            taps_w.at[layer, pl.ds(4 * p + second, 3), :, pl.ds(128 * second, 128)],
            tap_sem.at[layer * 6 + p * 2 + second],
        )
        for layer in range(2)
        for p in range(3)
        for second in range(2)
    ]
    for load in loads:
        load.start()

    barrier = pltpu.get_barrier_semaphore()
    others = [{"seq": other} for other in list(near.values()) + list(along.values()) + mates[1:]]
    others += [{"band": to_band(k)} for k in range(1, BANDS)]
    for other in others:
        pl.semaphore_signal(barrier, inc=1, device_id=other, device_id_type=MESH)
    for load in tap_loads:
        load.start()
    for layer in range(2):
        for p in range(3):
            taps_w[layer, 4 * p + 3, :, 0:128] = jnp.zeros((128, 128), BF16)
            taps_w[layer, 4 * p, :, 128:256] = jnp.zeros((128, 128), BF16)
    pl.semaphore_wait(barrier, len(others))

    def band_send(src, dst_all, s_sem, r_sem, k):
        return remote(src, dst_all.at[band], s_sem.at[k], r_sem.at[k], band=to_band(k))

    def band_recv(dst_all, s_sem, r_sem, k):
        slot = dst_all.at[from_band(k)]
        return remote(slot, slot, s_sem.at[k], r_sem.at[k], band=to_band(k))

    tok_sends = [band_send(tok_ref, tok_all, tok_s, tok_r, k) for k in range(1, BANDS)]
    for send in tok_sends:
        send.start()

    for load in loads:
        load.wait()
    m_all[band] = jnp.dot(wout[...], wlr[...], preferred_element_type=F32).astype(BF16)
    offset = ((map_v[...] - 1).astype(F32) * 1000000000.0).astype(BF16)
    kv[0, 128:144] = jnp.broadcast_to(offset, (16, 128))
    for k in range(1, BANDS):
        band_recv(tok_all, tok_s, tok_r, k).wait_recv()

    floats = jnp.concatenate([tok_all[c] for c in range(BANDS)], axis=1).astype(F32)
    inv = lax.rsqrt(jnp.mean(floats * floats, axis=-1, keepdims=True) + EPS)
    normed = (floats * inv * gain_v[...]).astype(BF16)
    qkv = jnp.dot(normed, wqkv[...], preferred_element_type=F32)
    kv[0, 0:128] = qkv[:, 128:256].astype(BF16)
    kv[0, 144:272] = qkv[:, 256:384].T.astype(BF16)
    q_all[0] = qkv[:, 0:128].astype(BF16)

    def kv_copy(src, dst, sem, hops, rows=None):
        where, landed = kv.at[src], kv.at[dst]
        arrival = dst
        if rows is not None:
            where, landed = where.at[pl.ds(*rows)], landed.at[pl.ds(*rows)]
            arrival = dst if rows[0] == 0 else 0
        return remote(where, landed, kv_s.at[sem], kv_r.at[arrival], seq=along[hops])

    upper, lower = (0, 144), (144, 128)
    one = kv_copy(0, 1, 0, 1)
    seven = kv_copy(0, 7, 1, -1)
    two = kv_copy(0, 2, 2, 2)
    six = kv_copy(0, 6, 3, -2)
    three = kv_copy(1, 3, 4, 2)
    five = kv_copy(7, 5, 5, -2)
    four_up = kv_copy(2, 4, 6, 2, upper)
    four_low = kv_copy(6, 4, 7, -2, lower)
    q_copies = [
        remote(q_all.at[0], q_all.at[k], q_s.at[k], q_r.at[k], seq=mates[k]) for k in (1, 2, 3)
    ]
    for copy in [one, seven] + q_copies + [two, six]:
        copy.start()

    across = row * 2 + 1 - side

    def row_peer(k, side_):
        return ((row + 4 + k) % 4) * 2 + side_

    m_own = [remote(m_all.at[band], m_all.at[band], m_s.at[0], m_r.at[0], band=across)] + [
        remote(m_all.at[band], m_all.at[band], m_s.at[k], m_r.at[k], band=row_peer(k, side))
        for k in (1, 2, 3)
    ]
    m_relay = [
        remote(
            m_all.at[across], m_all.at[across], m_s.at[3 + k], m_r.at[3 + k], band=row_peer(k, side)
        )
        for k in (1, 2, 3)
    ]
    m_arrivals = [
        remote(m_all.at[slot], m_all.at[slot], m_s.at[sem], m_r.at[sem], band=across)
        for slot, sem in [(across, 0)]
        + [(row_peer(-k, side), k) for k in (1, 2, 3)]
        + [(row_peer(-k, 1 - side), 3 + k) for k in (1, 2, 3)]
    ]
    for send in m_own:
        send.start()
    keep = jnp.broadcast_to(map_v[...].astype(F32), (128, 128)).T
    keep = jnp.concatenate([keep, keep], axis=1)
    lr_tok = jnp.dot(floats.astype(BF16), wlr[...], preferred_element_type=F32)
    for copy in q_copies:
        copy.wait_recv()
    queries = jnp.concatenate([q_all[k] for k in range(4)], axis=0)

    def attend(state, slots):
        keys = jnp.concatenate([kv[j, 0:128] for j in slots], axis=0)
        values_t = jnp.concatenate([kv[j, 144:272] for j in slots], axis=1)
        offs = jnp.concatenate(
            [jnp.broadcast_to(kv[j, 128:144][0:1].astype(F32), (128, 128)).T for j in slots],
            axis=0,
        )
        offs = jnp.concatenate([offs] * 4, axis=1)
        scores = (
            lax.dot_general(
                keys, queries, (((1,), (1,)), ((), ())), preferred_element_type=F32
            )
            * HEAD ** (-0.5)
            + offs
        )
        block_top = jnp.max(scores, axis=0, keepdims=True)
        if state is None:
            top = block_top
        else:
            top = jnp.maximum(state[0], block_top)
        weights = jnp.exp(scores - top)
        block_sum = jnp.sum(weights, axis=0, keepdims=True)
        mixed = jnp.dot(values_t, weights.astype(BF16), preferred_element_type=F32)
        if state is None:
            return top, block_sum, mixed
        fade = jnp.exp(state[0] - top)
        return top, state[1] * fade + block_sum, state[2] * fade + mixed

    state = attend(None, [0])
    one.wait_recv()
    three.start()
    seven.wait_recv()
    five.start()
    state = attend(state, [1, 7])
    m_arrivals[0].wait_recv()
    for send in m_relay:
        send.start()
    two.wait_recv()
    four_up.start()
    six.wait_recv()
    four_low.start()
    state = attend(state, [2, 6])
    three.wait_recv()
    five.wait_recv()
    state = attend(state, [3, 5])
    four_up.wait_recv()
    four_low.wait_recv()
    top, total, mixed = attend(state, [4])

    mixed = mixed / total
    o_copies = []
    for k in (1, 2, 3):
        lanes = slice(k * 128, (k + 1) * 128)
        o_send[k] = mixed[:, lanes].astype(BF16)
        st_send[k, 0:4] = jnp.broadcast_to(top[:, lanes], (4, 128))
        st_send[k, 4:8] = jnp.broadcast_to(total[:, lanes], (4, 128))
        o_copies.append(
            remote(st_send.at[k], st_recv.at[k], st_s.at[k], st_r.at[k], seq=mates[k])
        )
        o_copies.append(remote(o_send.at[k], o_recv.at[k], o_s.at[k], o_r.at[k], seq=mates[k]))
    for copy in o_copies:
        copy.start()
    for copy in o_copies:
        copy.wait_recv()
    tops = [top[:, 0:128]] + [st_recv[k, 0:1] for k in (1, 2, 3)]
    sums = [total[:, 0:128]] + [st_recv[k, 4:5] for k in (1, 2, 3)]
    parts = [mixed[:, 0:128]] + [o_recv[k].astype(F32) for k in (1, 2, 3)]
    best = jnp.maximum(jnp.maximum(tops[0], tops[1]), jnp.maximum(tops[2], tops[3]))
    shares = [s * jnp.exp(t - best) for s, t in zip(sums, tops)]
    share_sum = shares[0] + shares[1] + shares[2] + shares[3]
    attended = (
        parts[0] * shares[0] + parts[1] * shares[1] + parts[2] * shares[2] + parts[3] * shares[3]
    ) / share_sum
    att_all[band] = attended.T.astype(BF16)
    att_sends = [band_send(att_all.at[band], att_all, att_s, att_r, k) for k in range(1, BANDS)]
    for send in att_sends:
        send.start()
    for copy in m_arrivals[1:]:
        copy.wait_recv()
    for k in range(1, BANDS):
        band_recv(att_all, att_s, att_r, k).wait_recv()

    heads = jnp.concatenate([att_all[c] for c in range(BANDS)], axis=1)
    both = lr_tok + jnp.dot(
        heads, m_all[...].reshape(BANDS * 128, 256), preferred_element_type=F32
    )
    both = (both * keep).astype(BF16)
    leftbuf[16:144] = both[:, 0:128]
    rightbuf[16:144] = both[:, 128:256]

    def edge(src, dst, sem, other):
        return remote(src, dst, edge_s.at[sem], edge_r.at[sem], seq=other)

    own = rightbuf.at[pl.ds(16, 128)]
    edges = [
        edge(own, rightbuf.at[pl.ds(272, 128)], 1, near[-2]),
        edge(own, rightbuf.at[pl.ds(144, 128)], 0, near[-1]),
        edge(rightbuf.at[pl.ds(16, 16)], rightbuf.at[pl.ds(400, 16)], 2, near[-3]),
        edge(rightbuf.at[pl.ds(128, 16)], rightbuf.at[pl.ds(0, 16)], 3, near[1]),
        edge(leftbuf.at[pl.ds(16, 16)], leftbuf.at[pl.ds(144, 16)], 4, near[-1]),
        edge(leftbuf.at[pl.ds(128, 16)], leftbuf.at[pl.ds(0, 16)], 5, near[1]),
    ]
    for copy in edges:
        copy.start()
    wc_sends = [
        band_send(
            wout.at[:, pl.ds(pl.multiple_of(to_band(k) * 128, 128), 128)], wcol_all, wc_s, wc_r, k
        )
        for k in range(1, BANDS)
    ]
    for send in wc_sends:
        send.start()
    wcol_all[band] = wout[:, pl.ds(pl.multiple_of(band * 128, 128), 128)]
    for copy in edges:
        copy.wait_recv()
    pair_map(
        seq,
        band,
        leftbuf,
        rightbuf,
        cgain_v,
        bias_v,
        weight_v,
        out_ref,
        lf,
        rf,
        lp,
        rp,
        act0,
        field1,
        act1,
        taps_w,
        plain,
        tap_loads,
    )
    for k in range(1, BANDS):
        band_recv(wcol_all, wc_s, wc_r, k).wait_recv()
    heads = jnp.concatenate([att_all[c] for c in range(BANDS)], axis=1)
    summed = jnp.dot(
        heads, wcol_all[...].reshape(BANDS * 128, 128), preferred_element_type=F32
    )
    trunk_ref[...] = (tok_all[band].astype(F32) + summed).astype(BF16)
    for send in tok_sends + q_copies + m_own + m_relay + o_copies + att_sends + edges + wc_sends:
        send.wait_send()
    for send in [one, two, three, five, six, seven, four_up, four_low]:
        send.wait_send()


def local(
    tokens,
    mappable,
    attn_gain,
    w_query,
    w_key,
    w_value,
    w_out,
    w_left,
    w_right,
    conv_gain,
    conv_kernel,
    conv_bias,
    contact_weight,
):
    vmem = pl.BlockSpec(memory_space=pltpu.VMEM)
    hbm = pl.BlockSpec(memory_space=pltpu.HBM)
    dma = pltpu.SemaphoreType.DMA
    trunk_out, contacts = pl.pallas_call(
        trunk_kernel,
        out_shape=(
            jax.ShapeDtypeStruct((BINS, 128), BF16),
            jax.ShapeDtypeStruct((DIAG, BINS), F32),
        ),
        in_specs=[hbm] * 13,
        out_specs=(vmem, vmem),
        scratch_shapes=[
            pltpu.VMEM((BANDS, 128, 128), BF16),
            pltpu.VMEM((1, 1024), F32),
            pltpu.VMEM((1, BINS), jnp.int32),
            pltpu.VMEM((1024, 384), BF16),
            pltpu.VMEM((128, 1024), BF16),
            pltpu.VMEM((1024, 256), BF16),
            pltpu.VMEM((BANDS, 128, 256), BF16),
            pltpu.VMEM((BANDS, 128, 128), BF16),
            pltpu.VMEM((4, 128, 128), BF16),
            pltpu.VMEM((RING, 272, 128), BF16),
            pltpu.VMEM((4, 128, 128), BF16),
            pltpu.VMEM((4, 128, 128), BF16),
            pltpu.VMEM((4, 8, 128), F32),
            pltpu.VMEM((4, 8, 128), F32),
            pltpu.VMEM((BANDS, 128, 128), BF16),
            pltpu.VMEM((160, 128), BF16),
            pltpu.VMEM((416, 128), BF16),
            pltpu.VMEM((2, 128), F32),
            pltpu.VMEM((2, 128), F32),
            pltpu.VMEM((1, 128), F32),
            pltpu.VMEM((160, 128), F32),
            pltpu.VMEM((200, 128), F32),
            pltpu.VMEM((CHUNK, LANES, 128), F32),
            pltpu.VMEM((WIDE0 + CHUNK - 1, LANES, 128), F32),
            pltpu.VMEM((WIDE0, CHUNK + 2, LANES, 128), BF16),
            pltpu.VMEM((WIDE1, CHUNK, LANES, 128), BF16),
            pltpu.VMEM((WIDE1, CHUNK + 4, LANES, 128), BF16),
            pltpu.VMEM((2, 12, 128, 256), BF16),
            pltpu.VMEM((ROWS, 128), F32),
            dma((12,)),
            dma((12,)),
        ]
        + [dma((8,)) for _ in range(18)],
        compiler_params=pltpu.CompilerParams(
            collective_id=0, has_side_effects=True, vmem_limit_bytes=60 * 1024 * 1024
        ),
    )(
        tokens,
        mappable.reshape(1, BINS),
        attn_gain.reshape(1, -1),
        w_query,
        w_key,
        w_value,
        w_out,
        w_left,
        w_right,
        conv_gain,
        conv_kernel,
        conv_bias,
        contact_weight.reshape(1, 128),
    )
    return (trunk_out, contacts.T)


def solution(mesh):
    return jax.shard_map(
        local,
        mesh=mesh,
        in_specs=(
            P("seq", "band"),
            P("seq"),
            P(),
            P(None, "band"),
            P(None, "band"),
            P(None, "band"),
            P("band", None),
            P(),
            P(),
            P(),
            P(),
            P(),
            P(),
        ),
        out_specs=(P("seq", "band"), P("seq", "band")),
        check_vma=False,
    )
```

```python
import jax
import jax.numpy as jnp
from jax import lax
from jax.experimental import pallas as pl
from jax.experimental.pallas import tpu as pltpu
from jax.sharding import PartitionSpec as P

HEAD = 128
DIAG = 32
BINS = 128
EPS = 1e-06
BANDS = 8
RING = 8
LINE = 4
SEQ = 32
MESH = pl.DeviceIdType.MESH
F32 = jnp.float32
BF16 = jnp.bfloat16


def remote(src, dst, send_sem, recv_sem, **device):
    return pltpu.make_async_remote_copy(
        src_ref=src,
        dst_ref=dst,
        send_sem=send_sem,
        recv_sem=recv_sem,
        device_id=device,
        device_id_type=MESH,
    )


CHUNK = 9
LANES = 16
ROWS = CHUNK * LANES
LEAD = 8
WIDE0 = 44
WIDE1 = 40
GROUP = 4


def norm_gelu(field, half_gain, keep):
    squares = jnp.sum(field * field, axis=-1, keepdims=True)
    inv = lax.rsqrt(squares + HEAD * EPS)
    if keep is not None:
        inv = jnp.where(keep, inv, 0.0)
    half = field * inv * half_gain
    inner = half * (1.5957691216057308 + 0.285419265090401 * (half * half))
    return half + half * jnp.tanh(inner)


def pair_map(
    seq,
    band,
    leftbuf,
    rightbuf,
    gain_ref,
    bias_ref,
    weight_ref,
    out_ref,
    lf,
    rf,
    lp,
    rp,
    act0,
    field1,
    act1,
    taps_w,
    plain,
    loads,
):
    length = SEQ * BINS
    lf[...] = leftbuf[...].astype(F32)
    rf[0:192] = rightbuf[pl.ds(pl.multiple_of(band * DIAG, DIAG), 192)].astype(F32)
    for a in range(CHUNK):
        lp[a] = lf[pl.ds(LEAD + a, LANES, stride=CHUNK)]
    for t in range(WIDE0 + CHUNK - 1):
        rp[t] = rf[pl.ds(t + 2, LANES, stride=CHUNK)]

    shape = (CHUNK, LANES, 128)
    first = seq * BINS - LEAD
    spot = (
        lax.broadcasted_iota(jnp.int32, shape, 0)
        + lax.broadcasted_iota(jnp.int32, shape, 1) * CHUNK
        + first
    )

    def inside(diag):
        known = (diag >= 0) & (diag < BANDS * DIAG)
        high = jnp.where(known, jnp.minimum(length, length - diag), 0)
        return (spot >= 0) & (spot < high)

    def start_field(delta):
        return lp[...] * rp[pl.ds(delta, CHUNK)]

    root = float(HEAD) ** 0.5 * 0.5
    gain0 = gain_ref[0:1].reshape(1, 1, 128) * root
    gain1 = gain_ref[1:2].reshape(1, 1, 128) * root
    bias0 = bias_ref[0:1].reshape(1, 1, 128)
    bias1 = bias_ref[1:2].reshape(1, 1, 128)
    weight = weight_ref[...].reshape(1, 1, 128)

    def put(dst, where, act, reach):
        dst[where, pl.ds(reach, CHUNK)] = act.astype(BF16)
        before = pltpu.roll(act[CHUNK - reach :], 1, 1)
        after = pltpu.roll(act[:reach], LANES - 1, 1)
        dst[where, pl.ds(0, reach)] = before.astype(BF16)
        dst[where, pl.ds(reach + CHUNK, reach)] = after.astype(BF16)

    def first_act(delta):
        keep = inside(band * DIAG + delta - 6)
        put(act0, delta, norm_gelu(start_field(delta), gain0, keep), 1)

    def conv(src, layer, slabs, reach):
        taps = jnp.concatenate(
            [
                jnp.concatenate(
                    [
                        src[slab + reach * (j - p), pl.ds(reach * p, CHUNK)].reshape(ROWS, 128)
                        for slab in slabs
                    ],
                    axis=0,
                )
                for p in range(3)
                for j in range(4)
            ],
            axis=1,
        )
        return jnp.dot(
            taps, taps_w[layer].reshape(12 * 128, 256), preferred_element_type=F32
        )

    def second_act(step, term):
        diag = step * GROUP
        for g in range(GROUP):
            pair, half = g // 2, g % 2
            block = term[pair * ROWS : (pair + 1) * ROWS, half * 128 : (half + 1) * 128]
            value = block.reshape(shape) + start_field(diag + g + 2) + bias0
            field1[diag + g] = value.astype(BF16)
            keep = inside(band * DIAG + diag + g - 4)
            put(act1, diag + g, norm_gelu(value, gain1, keep), 2)

    @pl.loop(0, 2)
    def _(step):
        for g in range(GROUP):
            first_act(step * GROUP + g)

    for load in loads:
        load.wait()

    def conv0(step):
        slab = step * GROUP + 2
        return conv(act0, 0, [slab, slab + 2], 1)

    def grow(step, term):
        fresh = conv0(step)
        second_act(step - 1, term)
        for g in range(GROUP):
            first_act(step * GROUP + 8 + g)
        return fresh

    steps = WIDE1 // GROUP
    term = conv0(0)
    for g in range(GROUP):
        first_act(8 + g)
    term = lax.fori_loop(1, steps - 1, grow, term)
    fresh = conv0(steps - 1)
    second_act(steps - 2, term)
    second_act(steps - 1, fresh)

    lane = lax.broadcasted_iota(jnp.int32, shape, 2)

    def conv1(step):
        slab = step * GROUP + 4
        return conv(act1, 1, [slab, slab + 1], 2)

    def finish(step, term, found):
        diag = step * GROUP
        for g in range(GROUP):
            pair, half = g % 2, g // 2
            block = term[pair * ROWS : (pair + 1) * ROWS, half * 128 : (half + 1) * 128]
            value = block.reshape(shape) + field1[diag + g + 4].astype(F32) + bias1
            contact = jnp.sum(value * weight, axis=-1, keepdims=True)
            found = jnp.where(lane == diag + g, contact, found)
        return found

    def last(step, carry):
        term, found = carry
        fresh = conv1(step)
        return fresh, finish(step - 1, term, found)

    steps = DIAG // GROUP
    term, found = lax.fori_loop(1, steps, last, (conv1(0), jnp.zeros(shape, F32)))
    found = finish(steps - 1, term, found)
    found = jnp.where(spot + band * DIAG + lane < length, found, 0.0)
    for a in range(CHUNK):
        plain[pl.ds(a, LANES, stride=CHUNK)] = found[a]
    out_ref[...] = plain[LEAD : LEAD + BINS].T[0:DIAG]


def trunk_kernel(
    tok_ref,
    map_ref,
    gain_ref,
    wq_ref,
    wk_ref,
    wv_ref,
    wout_ref,
    wl_ref,
    wr_ref,
    cgain_ref,
    kern_ref,
    bias_ref,
    weight_ref,
    trunk_ref,
    out_ref,
    tok_all,
    gain_v,
    map_v,
    wqkv,
    wout,
    wlr,
    m_all,
    wcol_all,
    q_all,
    kv,
    o_send,
    o_recv,
    st_send,
    st_recv,
    att_all,
    leftbuf,
    rightbuf,
    cgain_v,
    bias_v,
    weight_v,
    lf,
    rf,
    lp,
    rp,
    act0,
    field1,
    act1,
    taps_w,
    plain,
    local_sem,
    tap_sem,
    tok_s,
    tok_r,
    m_s,
    m_r,
    wc_s,
    wc_r,
    q_s,
    q_r,
    kv_s,
    kv_r,
    o_s,
    o_r,
    st_s,
    st_r,
    att_s,
    att_r,
    edge_s,
    edge_r,
):
    seq = lax.axis_index("seq")
    band = lax.axis_index("band")
    core = seq % 2
    ring = (seq // 2) % RING
    half = seq // (2 * RING)
    row = band // 2
    side = band % 2

    def seq_of(half_, ring_, core_):
        return half_ * (2 * RING) + ring_ * 2 + core_

    twin = seq_of(half, ring, 1 - core)
    facing = RING - 1 - ring
    sharers = [
        None,
        seq_of(half, facing, core),
        seq_of(1 - half, ring, core),
        seq_of(1 - half, facing, core),
    ]
    line = (ring // LINE) * LINE

    def on_line(k):
        return seq_of(half, line + (ring + LINE + k) % LINE, core)

    near = {k: (seq + SEQ + k) % SEQ for k in (-3, -2, -1, 1, 2, 3)}

    def to_band(k):
        return (band + k) % BANDS

    def from_band(k):
        return (band + BANDS - k) % BANDS

    loads = [
        pltpu.make_async_copy(tok_ref, tok_all.at[band], local_sem.at[0]),
        pltpu.make_async_copy(gain_ref, gain_v, local_sem.at[1]),
        pltpu.make_async_copy(map_ref, map_v, local_sem.at[2]),
        pltpu.make_async_copy(wout_ref, wout, local_sem.at[3]),
        pltpu.make_async_copy(wl_ref, wlr.at[:, pl.ds(0, 128)], local_sem.at[4]),
        pltpu.make_async_copy(wr_ref, wlr.at[:, pl.ds(128, 128)], local_sem.at[5]),
        pltpu.make_async_copy(wq_ref, wqkv.at[:, pl.ds(0, 128)], local_sem.at[6]),
        pltpu.make_async_copy(wk_ref, wqkv.at[:, pl.ds(128, 128)], local_sem.at[7]),
        pltpu.make_async_copy(wv_ref, wqkv.at[:, pl.ds(256, 128)], local_sem.at[8]),
        pltpu.make_async_copy(cgain_ref, cgain_v, local_sem.at[9]),
        pltpu.make_async_copy(bias_ref, bias_v, local_sem.at[10]),
        pltpu.make_async_copy(weight_ref, weight_v, local_sem.at[11]),
    ]
    tap_loads = [
        pltpu.make_async_copy(
            kern_ref.at[layer, p],
            taps_w.at[layer, pl.ds(4 * p + second, 3), :, pl.ds(128 * second, 128)],
            tap_sem.at[layer * 6 + p * 2 + second],
        )
        for layer in range(2)
        for p in range(3)
        for second in range(2)
    ]
    for load in loads:
        load.start()

    barrier = pltpu.get_barrier_semaphore()
    others = [{"seq": other} for other in list(near.values()) + sharers[1:] + [twin]]
    others += [{"seq": on_line(k)} for k in (1, 2, 3)]
    others += [{"band": to_band(k)} for k in range(1, BANDS)]
    for other in others:
        pl.semaphore_signal(barrier, inc=1, device_id=other, device_id_type=MESH)
    for load in tap_loads:
        load.start()
    for layer in range(2):
        for p in range(3):
            taps_w[layer, 4 * p + 3, :, 0:128] = jnp.zeros((128, 128), BF16)
            taps_w[layer, 4 * p, :, 128:256] = jnp.zeros((128, 128), BF16)
    pl.semaphore_wait(barrier, len(others))

    def band_send(src, dst_all, s_sem, r_sem, k):
        return remote(src, dst_all.at[band], s_sem.at[k], r_sem.at[k], band=to_band(k))

    def band_recv(dst_all, s_sem, r_sem, k):
        slot = dst_all.at[from_band(k)]
        return remote(slot, slot, s_sem.at[k], r_sem.at[k], band=to_band(k))

    tok_sends = [band_send(tok_ref, tok_all, tok_s, tok_r, k) for k in range(1, BANDS)]
    for send in tok_sends:
        send.start()

    for load in loads:
        load.wait()
    m_all[band] = jnp.dot(wout[...], wlr[...], preferred_element_type=F32).astype(BF16)
    offset = ((map_v[...] - 1).astype(F32) * 1000000000.0).astype(BF16)
    kv[0, 128:144] = jnp.broadcast_to(offset, (16, 128))
    for k in range(1, BANDS):
        band_recv(tok_all, tok_s, tok_r, k).wait_recv()

    floats = jnp.concatenate([tok_all[c] for c in range(BANDS)], axis=1).astype(F32)
    inv = lax.rsqrt(jnp.mean(floats * floats, axis=-1, keepdims=True) + EPS)
    normed = (floats * inv * gain_v[...]).astype(BF16)
    qkv = jnp.dot(normed, wqkv[...], preferred_element_type=F32)
    kv[0, 0:128] = qkv[:, 128:256].astype(BF16)
    kv[0, 144:272] = qkv[:, 256:384].T.astype(BF16)
    q_all[0] = qkv[:, 0:128].astype(BF16)

    def kv_copy(src, dst, sem, other):
        return remote(kv.at[src], kv.at[dst], kv_s.at[sem], kv_r.at[dst], seq=other)

    kv_direct = [kv_copy(0, j, j, sharers[j]) for j in (1, 2, 3)]
    kv_twin = [kv_copy(j, 4 + j, 4 + j, twin) for j in range(4)]
    q_copies = [
        remote(q_all.at[0], q_all.at[k], q_s.at[k], q_r.at[k], seq=on_line(k)) for k in (1, 2, 3)
    ]
    for copy in kv_direct + q_copies + [kv_twin[0]]:
        copy.start()

    across = row * 2 + 1 - side

    def row_peer(k, side_):
        return ((row + 4 + k) % 4) * 2 + side_

    m_own = [remote(m_all.at[band], m_all.at[band], m_s.at[0], m_r.at[0], band=across)] + [
        remote(m_all.at[band], m_all.at[band], m_s.at[k], m_r.at[k], band=row_peer(k, side))
        for k in (1, 2, 3)
    ]
    m_relay = [
        remote(
            m_all.at[across], m_all.at[across], m_s.at[3 + k], m_r.at[3 + k], band=row_peer(k, side)
        )
        for k in (1, 2, 3)
    ]
    m_arrivals = [
        remote(m_all.at[slot], m_all.at[slot], m_s.at[sem], m_r.at[sem], band=across)
        for slot, sem in [(across, 0)]
        + [(row_peer(-k, side), k) for k in (1, 2, 3)]
        + [(row_peer(-k, 1 - side), 3 + k) for k in (1, 2, 3)]
    ]
    for send in m_own:
        send.start()
    keep = jnp.broadcast_to(map_v[...].astype(F32), (128, 128)).T
    keep = jnp.concatenate([keep, keep], axis=1)
    lr_tok = jnp.dot(floats.astype(BF16), wlr[...], preferred_element_type=F32)
    kv_direct[1].wait_recv()
    kv_twin[2].start()
    for copy in q_copies:
        copy.wait_recv()
    queries = jnp.concatenate([q_all[k] for k in range(4)], axis=0)

    def attend(state, slots):
        keys = jnp.concatenate([kv[j, 0:128] for j in slots], axis=0)
        values_t = jnp.concatenate([kv[j, 144:272] for j in slots], axis=1)
        offs = jnp.concatenate(
            [jnp.broadcast_to(kv[j, 128:144][0:1].astype(F32), (128, 128)).T for j in slots],
            axis=0,
        )
        offs = jnp.concatenate([offs] * 4, axis=1)
        scores = (
            lax.dot_general(
                keys, queries, (((1,), (1,)), ((), ())), preferred_element_type=F32
            )
            * HEAD ** (-0.5)
            + offs
        )
        block_top = jnp.max(scores, axis=0, keepdims=True)
        if state is None:
            top = block_top
        else:
            top = jnp.maximum(state[0], block_top)
        weights = jnp.exp(scores - top)
        block_sum = jnp.sum(weights, axis=0, keepdims=True)
        mixed = jnp.dot(values_t, weights.astype(BF16), preferred_element_type=F32)
        if state is None:
            return top, block_sum, mixed
        fade = jnp.exp(state[0] - top)
        return top, state[1] * fade + block_sum, state[2] * fade + mixed

    kv_direct[0].wait_recv()
    kv_twin[1].start()
    kv_twin[0].wait_recv()
    state = attend(None, [0, 4])
    state = attend(state, [1, 2])
    kv_direct[2].wait_recv()
    kv_twin[3].start()
    m_arrivals[0].wait_recv()
    for send in m_relay:
        send.start()
    kv_twin[1].wait_recv()
    kv_twin[2].wait_recv()
    state = attend(state, [5, 6])
    kv_twin[3].wait_recv()
    top, total, mixed = attend(state, [3, 7])

    mixed = mixed / total
    o_copies = []
    for k in (1, 2, 3):
        lanes = slice(k * 128, (k + 1) * 128)
        o_send[k] = mixed[:, lanes].astype(BF16)
        st_send[k, 0:4] = jnp.broadcast_to(top[:, lanes], (4, 128))
        st_send[k, 4:8] = jnp.broadcast_to(total[:, lanes], (4, 128))
        o_copies.append(
            remote(st_send.at[k], st_recv.at[k], st_s.at[k], st_r.at[k], seq=on_line(-k))
        )
        o_copies.append(
            remote(o_send.at[k], o_recv.at[k], o_s.at[k], o_r.at[k], seq=on_line(-k))
        )
    for copy in o_copies:
        copy.start()
    for copy in o_copies:
        copy.wait_recv()
    tops = [top[:, 0:128]] + [st_recv[k, 0:1] for k in (1, 2, 3)]
    sums = [total[:, 0:128]] + [st_recv[k, 4:5] for k in (1, 2, 3)]
    parts = [mixed[:, 0:128]] + [o_recv[k].astype(F32) for k in (1, 2, 3)]
    best = jnp.maximum(jnp.maximum(tops[0], tops[1]), jnp.maximum(tops[2], tops[3]))
    shares = [s * jnp.exp(t - best) for s, t in zip(sums, tops)]
    share_sum = shares[0] + shares[1] + shares[2] + shares[3]
    attended = (
        parts[0] * shares[0] + parts[1] * shares[1] + parts[2] * shares[2] + parts[3] * shares[3]
    ) / share_sum
    att_all[band] = attended.T.astype(BF16)
    att_sends = [band_send(att_all.at[band], att_all, att_s, att_r, k) for k in range(1, BANDS)]
    for send in att_sends:
        send.start()
    for copy in m_arrivals[1:]:
        copy.wait_recv()
    for k in range(1, BANDS):
        band_recv(att_all, att_s, att_r, k).wait_recv()

    heads = jnp.concatenate([att_all[c] for c in range(BANDS)], axis=1)
    both = lr_tok + jnp.dot(
        heads, m_all[...].reshape(BANDS * 128, 256), preferred_element_type=F32
    )
    both = (both * keep).astype(BF16)
    leftbuf[16:144] = both[:, 0:128]
    rightbuf[16:144] = both[:, 128:256]

    def edge(src, dst, sem, other):
        return remote(src, dst, edge_s.at[sem], edge_r.at[sem], seq=other)

    own = rightbuf.at[pl.ds(16, 128)]
    edges = [
        edge(own, rightbuf.at[pl.ds(272, 128)], 1, near[-2]),
        edge(own, rightbuf.at[pl.ds(144, 128)], 0, near[-1]),
        edge(rightbuf.at[pl.ds(16, 16)], rightbuf.at[pl.ds(400, 16)], 2, near[-3]),
        edge(rightbuf.at[pl.ds(128, 16)], rightbuf.at[pl.ds(0, 16)], 3, near[1]),
        edge(leftbuf.at[pl.ds(16, 16)], leftbuf.at[pl.ds(144, 16)], 4, near[-1]),
        edge(leftbuf.at[pl.ds(128, 16)], leftbuf.at[pl.ds(0, 16)], 5, near[1]),
    ]
    for copy in edges:
        copy.start()
    wc_sends = [
        band_send(
            wout.at[:, pl.ds(pl.multiple_of(to_band(k) * 128, 128), 128)], wcol_all, wc_s, wc_r, k
        )
        for k in range(1, BANDS)
    ]
    for send in wc_sends:
        send.start()
    wcol_all[band] = wout[:, pl.ds(pl.multiple_of(band * 128, 128), 128)]
    for copy in edges:
        copy.wait_recv()
    pair_map(
        seq,
        band,
        leftbuf,
        rightbuf,
        cgain_v,
        bias_v,
        weight_v,
        out_ref,
        lf,
        rf,
        lp,
        rp,
        act0,
        field1,
        act1,
        taps_w,
        plain,
        tap_loads,
    )
    for k in range(1, BANDS):
        band_recv(wcol_all, wc_s, wc_r, k).wait_recv()
    heads = jnp.concatenate([att_all[c] for c in range(BANDS)], axis=1)
    summed = jnp.dot(
        heads, wcol_all[...].reshape(BANDS * 128, 128), preferred_element_type=F32
    )
    trunk_ref[...] = (tok_all[band].astype(F32) + summed).astype(BF16)
    for send in tok_sends + q_copies + m_own + m_relay + o_copies + att_sends + edges + wc_sends:
        send.wait_send()
    for send in kv_direct + kv_twin:
        send.wait_send()


def local(
    tokens,
    mappable,
    attn_gain,
    w_query,
    w_key,
    w_value,
    w_out,
    w_left,
    w_right,
    conv_gain,
    conv_kernel,
    conv_bias,
    contact_weight,
):
    vmem = pl.BlockSpec(memory_space=pltpu.VMEM)
    hbm = pl.BlockSpec(memory_space=pltpu.HBM)
    dma = pltpu.SemaphoreType.DMA
    trunk_out, contacts = pl.pallas_call(
        trunk_kernel,
        out_shape=(
            jax.ShapeDtypeStruct((BINS, 128), BF16),
            jax.ShapeDtypeStruct((DIAG, BINS), F32),
        ),
        in_specs=[hbm] * 13,
        out_specs=(vmem, vmem),
        scratch_shapes=[
            pltpu.VMEM((BANDS, 128, 128), BF16),
            pltpu.VMEM((1, 1024), F32),
            pltpu.VMEM((1, BINS), jnp.int32),
            pltpu.VMEM((1024, 384), BF16),
            pltpu.VMEM((128, 1024), BF16),
            pltpu.VMEM((1024, 256), BF16),
            pltpu.VMEM((BANDS, 128, 256), BF16),
            pltpu.VMEM((BANDS, 128, 128), BF16),
            pltpu.VMEM((4, 128, 128), BF16),
            pltpu.VMEM((RING, 272, 128), BF16),
            pltpu.VMEM((4, 128, 128), BF16),
            pltpu.VMEM((4, 128, 128), BF16),
            pltpu.VMEM((4, 8, 128), F32),
            pltpu.VMEM((4, 8, 128), F32),
            pltpu.VMEM((BANDS, 128, 128), BF16),
            pltpu.VMEM((160, 128), BF16),
            pltpu.VMEM((416, 128), BF16),
            pltpu.VMEM((2, 128), F32),
            pltpu.VMEM((2, 128), F32),
            pltpu.VMEM((1, 128), F32),
            pltpu.VMEM((160, 128), F32),
            pltpu.VMEM((200, 128), F32),
            pltpu.VMEM((CHUNK, LANES, 128), F32),
            pltpu.VMEM((WIDE0 + CHUNK - 1, LANES, 128), F32),
            pltpu.VMEM((WIDE0, CHUNK + 2, LANES, 128), BF16),
            pltpu.VMEM((WIDE1, CHUNK, LANES, 128), BF16),
            pltpu.VMEM((WIDE1, CHUNK + 4, LANES, 128), BF16),
            pltpu.VMEM((2, 12, 128, 256), BF16),
            pltpu.VMEM((ROWS, 128), F32),
            dma((12,)),
            dma((12,)),
        ]
        + [dma((8,)) for _ in range(18)],
        compiler_params=pltpu.CompilerParams(
            collective_id=0, has_side_effects=True, vmem_limit_bytes=60 * 1024 * 1024
        ),
    )(
        tokens,
        mappable.reshape(1, BINS),
        attn_gain.reshape(1, -1),
        w_query,
        w_key,
        w_value,
        w_out,
        w_left,
        w_right,
        conv_gain,
        conv_kernel,
        conv_bias,
        contact_weight.reshape(1, 128),
    )
    return (trunk_out, contacts.T)


def solution(mesh):
    return jax.shard_map(
        local,
        mesh=mesh,
        in_specs=(
            P("seq", "band"),
            P("seq"),
            P(),
            P(None, "band"),
            P(None, "band"),
            P(None, "band"),
            P("band", None),
            P(),
            P(),
            P(),
            P(),
            P(),
            P(),
        ),
        out_specs=(P("seq", "band"), P("seq", "band")),
        check_vma=False,
    )
```

```python
import jax
import jax.numpy as jnp
from jax import lax
from jax.experimental import pallas as pl
from jax.experimental.pallas import tpu as pltpu
from jax.sharding import PartitionSpec as P

HEAD = 128
DIAG = 32
BINS = 128
EPS = 1e-06
BANDS = 8
RING = 8
LINE = 4
SEQ = 32
MESH = pl.DeviceIdType.MESH
F32 = jnp.float32
BF16 = jnp.bfloat16


def remote(src, dst, send_sem, recv_sem, **device):
    return pltpu.make_async_remote_copy(
        src_ref=src,
        dst_ref=dst,
        send_sem=send_sem,
        recv_sem=recv_sem,
        device_id=device,
        device_id_type=MESH,
    )


CHUNK = 9
LANES = 16
ROWS = CHUNK * LANES
LEAD = 8
WIDE0 = 44
WIDE1 = 40
GROUP = 8
LATE = 16


def norm_gelu(field, half_gain, keep):
    squares = jnp.sum(field * field, axis=-1, keepdims=True)
    inv = lax.rsqrt(squares + HEAD * EPS)
    if keep is not None:
        inv = jnp.where(keep, inv, 0.0)
    half = (field * inv * half_gain).astype(BF16)
    inner = half * (1.5957691216057308 + 0.285419265090401 * (half * half))
    return half + half * jnp.tanh(inner)


def pair_map(
    seq,
    band,
    leftbuf,
    rightbuf,
    gain_ref,
    bias_ref,
    weight_ref,
    out_ref,
    lf,
    rf,
    lp,
    rp,
    act0,
    field1,
    act1,
    taps_w,
    plain,
    loads,
):
    length = SEQ * BINS
    bins = lax.broadcasted_iota(jnp.int32, (160, 128), 0) + (seq * BINS - 16)
    lf[...] = jnp.where((bins >= 0) & (bins < length), leftbuf[...].astype(F32), 0.0)
    bins = lax.broadcasted_iota(jnp.int32, (192, 128), 0) + (seq * BINS + band * DIAG - 16)
    window = rightbuf[pl.ds(pl.multiple_of(band * DIAG, DIAG), 192)].astype(F32)
    rf[0:192] = jnp.where((bins >= 0) & (bins < length), window, 0.0)
    for a in range(CHUNK):
        lp[a] = lf[pl.ds(LEAD + a, LANES, stride=CHUNK)]
    for t in range(WIDE0 + CHUNK - 1):
        rp[t] = rf[pl.ds(t + 2, LANES, stride=CHUNK)]

    shape = (CHUNK, LANES, 128)
    first = seq * BINS - LEAD
    spot = (
        lax.broadcasted_iota(jnp.int32, shape, 0)
        + lax.broadcasted_iota(jnp.int32, shape, 1) * CHUNK
        + first
    )

    def inside(diag):
        known = (diag >= 0) & (diag < BANDS * DIAG)
        high = jnp.where(known, jnp.minimum(length, length - diag), 0)
        return (spot >= 0) & (spot < high)

    def start_field(delta):
        return lp[...] * rp[pl.ds(delta, CHUNK)]

    root = float(HEAD) ** 0.5 * 0.5
    gain0 = gain_ref[0:1].reshape(1, 1, 128) * root
    gain1 = gain_ref[1:2].reshape(1, 1, 128) * root
    bias0 = bias_ref[0:1].reshape(1, 1, 128)
    bias1 = bias_ref[1:2].reshape(1, 1, 128)
    weight = weight_ref[...].reshape(1, 1, 128)

    def put(dst, where, act, reach):
        dst[where, pl.ds(reach, CHUNK)] = act
        before = pltpu.roll(act[CHUNK - reach :].astype(F32), 1, 1)
        after = pltpu.roll(act[:reach].astype(F32), LANES - 1, 1)
        dst[where, pl.ds(0, reach)] = before.astype(BF16)
        dst[where, pl.ds(reach + CHUNK, reach)] = after.astype(BF16)

    def first_act(delta):
        diag = band * DIAG + delta - 6
        known = jnp.where((diag >= 0) & (diag < BANDS * DIAG), 1.0, 0.0)
        put(act0, delta, norm_gelu(start_field(delta), gain0 * known, None), 1)

    def conv(src, layer, slabs, reach):
        taps = jnp.concatenate(
            [
                jnp.concatenate(
                    [
                        src[slab + reach * (j - p), pl.ds(reach * p, CHUNK)].reshape(ROWS, 128)
                        for slab in slabs
                    ],
                    axis=0,
                )
                for p in range(3)
                for j in range(4)
            ],
            axis=1,
        )
        return jnp.dot(
            taps, taps_w[layer].reshape(12 * 128, 256), preferred_element_type=F32
        )

    def second_act(step, term):
        diag = step * GROUP
        for g in range(GROUP):
            pair, half = g // 2, g % 2
            block = term[pair * ROWS : (pair + 1) * ROWS, half * 128 : (half + 1) * 128]
            value = block.reshape(shape) + start_field(diag + g + 2) + bias0
            field1[diag + g] = value.astype(BF16)
            keep = inside(band * DIAG + diag + g - 4)
            put(act1, diag + g, norm_gelu(value, gain1, keep), 2)

    for g in range(GROUP + 4):
        first_act(g)

    for load in loads:
        load.wait()

    def conv0(step):
        slab = step * GROUP + 2
        return conv(act0, 0, [slab + g for g in range(0, GROUP, 2)], 1)

    def grow(step, term):
        fresh = conv0(step)
        second_act(step - 1, term)
        for g in range(GROUP):
            first_act(step * GROUP + GROUP + 4 + g)
        return fresh

    steps = WIDE1 // GROUP
    term = conv0(0)
    for g in range(GROUP):
        first_act(GROUP + 4 + g)
    term = lax.fori_loop(1, steps - 1, grow, term)
    fresh = conv0(steps - 1)
    second_act(steps - 2, term)
    second_act(steps - 1, fresh)

    lane = lax.broadcasted_iota(jnp.int32, shape, 2)

    def conv1(step):
        slab = step * LATE + 4
        return conv(act1, 1, [slab + g for g in range(LATE) if g % 4 < 2], 2)

    def finish(step, term, found):
        diag = step * LATE
        for g in range(LATE):
            pair, half = (g // 4) * 2 + g % 2, g % 4 // 2
            block = term[pair * ROWS : (pair + 1) * ROWS, half * 128 : (half + 1) * 128]
            value = block.reshape(shape) + field1[diag + g + 4].astype(F32) + bias1
            contact = jnp.sum(value * weight, axis=-1, keepdims=True)
            found = jnp.where(lane == diag + g, contact, found)
        return found

    def last(step, carry):
        term, found = carry
        fresh = conv1(step)
        return fresh, finish(step - 1, term, found)

    steps = DIAG // LATE
    term, found = lax.fori_loop(1, steps, last, (conv1(0), jnp.zeros(shape, F32)))
    found = finish(steps - 1, term, found)
    found = jnp.where(spot + band * DIAG + lane < length, found, 0.0)
    for a in range(CHUNK):
        plain[pl.ds(a, LANES, stride=CHUNK)] = found[a]
    out_ref[...] = plain[LEAD : LEAD + BINS].T[0:DIAG]


def trunk_kernel(
    tok_ref,
    map_ref,
    gain_ref,
    wq_ref,
    wk_ref,
    wv_ref,
    wout_ref,
    wl_ref,
    wr_ref,
    cgain_ref,
    kern_ref,
    bias_ref,
    weight_ref,
    trunk_ref,
    out_ref,
    tok_all,
    gain_v,
    map_v,
    wqkv,
    wout,
    wlr,
    m_all,
    wcol_all,
    q_all,
    kv,
    o_send,
    o_recv,
    st_send,
    st_recv,
    att_all,
    leftbuf,
    rightbuf,
    cgain_v,
    bias_v,
    weight_v,
    lf,
    rf,
    lp,
    rp,
    act0,
    field1,
    act1,
    taps_w,
    plain,
    local_sem,
    tap_sem,
    tok_s,
    tok_r,
    m_s,
    m_r,
    wc_s,
    wc_r,
    q_s,
    q_r,
    kv_s,
    kv_r,
    o_s,
    o_r,
    st_s,
    st_r,
    att_s,
    att_r,
    edge_s,
    edge_r,
):
    seq = lax.axis_index("seq")
    band = lax.axis_index("band")
    core = seq % 2
    ring = (seq // 2) % RING
    half = seq // (2 * RING)
    row = band // 2
    side = band % 2

    def seq_of(half_, ring_, core_):
        return half_ * (2 * RING) + ring_ * 2 + core_

    twin = seq_of(half, ring, 1 - core)
    facing = RING - 1 - ring
    sharers = [
        None,
        seq_of(half, facing, core),
        seq_of(1 - half, ring, core),
        seq_of(1 - half, facing, core),
    ]
    line = (ring // LINE) * LINE

    def on_line(k):
        return seq_of(half, line + (ring + LINE + k) % LINE, core)

    near = {k: (seq + SEQ + k) % SEQ for k in (-3, -2, -1, 1, 2, 3)}

    def to_band(k):
        return (band + k) % BANDS

    def from_band(k):
        return (band + BANDS - k) % BANDS

    loads = [
        pltpu.make_async_copy(tok_ref, tok_all.at[band], local_sem.at[0]),
        pltpu.make_async_copy(gain_ref, gain_v, local_sem.at[1]),
        pltpu.make_async_copy(map_ref, map_v, local_sem.at[2]),
        pltpu.make_async_copy(wout_ref, wout, local_sem.at[3]),
        pltpu.make_async_copy(wl_ref, wlr.at[:, pl.ds(0, 128)], local_sem.at[4]),
        pltpu.make_async_copy(wr_ref, wlr.at[:, pl.ds(128, 128)], local_sem.at[5]),
        pltpu.make_async_copy(wq_ref, wqkv.at[:, pl.ds(0, 128)], local_sem.at[6]),
        pltpu.make_async_copy(wk_ref, wqkv.at[:, pl.ds(128, 128)], local_sem.at[7]),
        pltpu.make_async_copy(wv_ref, wqkv.at[:, pl.ds(256, 128)], local_sem.at[8]),
        pltpu.make_async_copy(cgain_ref, cgain_v, local_sem.at[9]),
        pltpu.make_async_copy(bias_ref, bias_v, local_sem.at[10]),
        pltpu.make_async_copy(weight_ref, weight_v, local_sem.at[11]),
    ]
    tap_loads = [
        pltpu.make_async_copy(
            kern_ref.at[layer, p],
            taps_w.at[layer, pl.ds(4 * p + second, 3), :, pl.ds(128 * second, 128)],
            tap_sem.at[layer * 6 + p * 2 + second],
        )
        for layer in range(2)
        for p in range(3)
        for second in range(2)
    ]
    for load in loads:
        load.start()

    barrier = pltpu.get_barrier_semaphore()
    others = [{"seq": other} for other in list(near.values()) + sharers[1:] + [twin]]
    others += [{"seq": on_line(k)} for k in (1, 2, 3)]
    others += [{"band": to_band(k)} for k in range(1, BANDS)]
    for other in others:
        pl.semaphore_signal(barrier, inc=1, device_id=other, device_id_type=MESH)
    for load in tap_loads:
        load.start()
    for layer in range(2):
        for p in range(3):
            taps_w[layer, 4 * p + 3, :, 0:128] = jnp.zeros((128, 128), BF16)
            taps_w[layer, 4 * p, :, 128:256] = jnp.zeros((128, 128), BF16)
    pl.semaphore_wait(barrier, len(others))

    def band_send(src, dst_all, s_sem, r_sem, k):
        return remote(src, dst_all.at[band], s_sem.at[k], r_sem.at[k], band=to_band(k))

    def band_recv(dst_all, s_sem, r_sem, k):
        slot = dst_all.at[from_band(k)]
        return remote(slot, slot, s_sem.at[k], r_sem.at[k], band=to_band(k))

    tok_sends = [band_send(tok_ref, tok_all, tok_s, tok_r, k) for k in range(1, BANDS)]
    for send in tok_sends:
        send.start()

    for load in loads:
        load.wait()
    m_all[band] = jnp.dot(wout[...], wlr[...], preferred_element_type=F32).astype(BF16)
    offset = ((map_v[...] - 1).astype(F32) * 1000000000.0).astype(BF16)
    kv[0, 128:144] = jnp.broadcast_to(offset, (16, 128))
    for k in range(1, BANDS):
        band_recv(tok_all, tok_s, tok_r, k).wait_recv()

    floats = jnp.concatenate([tok_all[c] for c in range(BANDS)], axis=1).astype(F32)
    inv = lax.rsqrt(jnp.mean(floats * floats, axis=-1, keepdims=True) + EPS)
    normed = (floats * inv * gain_v[...]).astype(BF16)
    qkv = jnp.dot(normed, wqkv[...], preferred_element_type=F32)
    kv[0, 0:128] = qkv[:, 128:256].astype(BF16)
    kv[0, 144:272] = qkv[:, 256:384].T.astype(BF16)
    q_all[0] = qkv[:, 0:128].astype(BF16)

    def kv_copy(src, dst, sem, other):
        return remote(kv.at[src], kv.at[dst], kv_s.at[sem], kv_r.at[dst], seq=other)

    kv_direct = [kv_copy(0, j, j, sharers[j]) for j in (1, 2, 3)]
    kv_twin = [kv_copy(j, 4 + j, 4 + j, twin) for j in range(4)]
    q_copies = [
        remote(q_all.at[0], q_all.at[k], q_s.at[k], q_r.at[k], seq=on_line(k)) for k in (1, 2, 3)
    ]
    for copy in kv_direct + q_copies + [kv_twin[0]]:
        copy.start()

    across = row * 2 + 1 - side

    def row_peer(k, side_):
        return ((row + 4 + k) % 4) * 2 + side_

    m_own = [remote(m_all.at[band], m_all.at[band], m_s.at[0], m_r.at[0], band=across)] + [
        remote(m_all.at[band], m_all.at[band], m_s.at[k], m_r.at[k], band=row_peer(k, side))
        for k in (1, 2, 3)
    ]
    m_relay = [
        remote(
            m_all.at[across], m_all.at[across], m_s.at[3 + k], m_r.at[3 + k], band=row_peer(k, side)
        )
        for k in (1, 2, 3)
    ]
    m_arrivals = [
        remote(m_all.at[slot], m_all.at[slot], m_s.at[sem], m_r.at[sem], band=across)
        for slot, sem in [(across, 0)]
        + [(row_peer(-k, side), k) for k in (1, 2, 3)]
        + [(row_peer(-k, 1 - side), 3 + k) for k in (1, 2, 3)]
    ]
    keep = jnp.broadcast_to(map_v[...].astype(F32), (128, 128)).T
    keep = jnp.concatenate([keep, keep], axis=1)
    lr_tok = jnp.dot(floats.astype(BF16), wlr[...], preferred_element_type=F32)
    kv_direct[1].wait_recv()
    kv_twin[2].start()
    for copy in q_copies:
        copy.wait_recv()
    queries = jnp.concatenate([q_all[k] for k in range(4)], axis=0)

    def attend(state, slots):
        keys = jnp.concatenate([kv[j, 0:128] for j in slots], axis=0)
        values_t = jnp.concatenate([kv[j, 144:272] for j in slots], axis=1)
        offs = jnp.concatenate(
            [jnp.broadcast_to(kv[j, 128:144][0:1].astype(F32), (128, 128)).T for j in slots],
            axis=0,
        )
        offs = jnp.concatenate([offs] * 4, axis=1)
        scores = (
            lax.dot_general(
                keys, queries, (((1,), (1,)), ((), ())), preferred_element_type=F32
            )
            * HEAD ** (-0.5)
            + offs
        )
        block_top = jnp.max(scores, axis=0, keepdims=True)
        if state is None:
            top = block_top
        else:
            top = jnp.maximum(state[0], block_top)
        weights = jnp.exp(scores - top)
        block_sum = jnp.sum(weights, axis=0, keepdims=True)
        mixed = jnp.dot(values_t, weights.astype(BF16), preferred_element_type=F32)
        if state is None:
            return top, block_sum, mixed
        fade = jnp.exp(state[0] - top)
        return top, state[1] * fade + block_sum, state[2] * fade + mixed

    kv_direct[0].wait_recv()
    kv_twin[1].start()
    kv_twin[0].wait_recv()
    state = attend(None, [0, 4])
    state = attend(state, [1, 2])
    kv_direct[2].wait_recv()
    kv_twin[3].start()
    for send in m_own:
        send.start()
    kv_twin[1].wait_recv()
    kv_twin[2].wait_recv()
    state = attend(state, [5, 6])
    kv_twin[3].wait_recv()
    top, total, mixed = attend(state, [3, 7])

    mixed = mixed / total
    o_copies = []
    for k in (1, 2, 3):
        lanes = slice(k * 128, (k + 1) * 128)
        o_send[k] = mixed[:, lanes].astype(BF16)
        st_send[k, 0:4] = jnp.broadcast_to(top[:, lanes], (4, 128))
        st_send[k, 4:8] = jnp.broadcast_to(total[:, lanes], (4, 128))
        o_copies.append(
            remote(st_send.at[k], st_recv.at[k], st_s.at[k], st_r.at[k], seq=on_line(-k))
        )
        o_copies.append(
            remote(o_send.at[k], o_recv.at[k], o_s.at[k], o_r.at[k], seq=on_line(-k))
        )
    for copy in o_copies:
        copy.start()
    m_arrivals[0].wait_recv()
    for send in m_relay:
        send.start()
    for copy in o_copies:
        copy.wait_recv()
    tops = [top[:, 0:128]] + [st_recv[k, 0:1] for k in (1, 2, 3)]
    sums = [total[:, 0:128]] + [st_recv[k, 4:5] for k in (1, 2, 3)]
    parts = [mixed[:, 0:128]] + [o_recv[k].astype(F32) for k in (1, 2, 3)]
    best = jnp.maximum(jnp.maximum(tops[0], tops[1]), jnp.maximum(tops[2], tops[3]))
    shares = [s * jnp.exp(t - best) for s, t in zip(sums, tops)]
    share_sum = shares[0] + shares[1] + shares[2] + shares[3]
    attended = (
        parts[0] * shares[0] + parts[1] * shares[1] + parts[2] * shares[2] + parts[3] * shares[3]
    ) / share_sum
    att_all[band] = attended.T.astype(BF16)
    att_sends = [band_send(att_all.at[band], att_all, att_s, att_r, k) for k in range(1, BANDS)]
    for send in att_sends:
        send.start()
    for copy in m_arrivals[1:]:
        copy.wait_recv()
    for k in range(1, BANDS):
        band_recv(att_all, att_s, att_r, k).wait_recv()

    heads = jnp.concatenate([att_all[c] for c in range(BANDS)], axis=1)
    both = lr_tok + jnp.dot(
        heads, m_all[...].reshape(BANDS * 128, 256), preferred_element_type=F32
    )
    both = (both * keep).astype(BF16)
    leftbuf[16:144] = both[:, 0:128]
    rightbuf[16:144] = both[:, 128:256]

    def edge(src, dst, sem, other):
        return remote(src, dst, edge_s.at[sem], edge_r.at[sem], seq=other)

    own = rightbuf.at[pl.ds(16, 128)]
    edges = [
        edge(own, rightbuf.at[pl.ds(272, 128)], 1, near[-2]),
        edge(own, rightbuf.at[pl.ds(144, 128)], 0, near[-1]),
        edge(rightbuf.at[pl.ds(16, 16)], rightbuf.at[pl.ds(400, 16)], 2, near[-3]),
        edge(rightbuf.at[pl.ds(128, 16)], rightbuf.at[pl.ds(0, 16)], 3, near[1]),
        edge(leftbuf.at[pl.ds(16, 16)], leftbuf.at[pl.ds(144, 16)], 4, near[-1]),
        edge(leftbuf.at[pl.ds(128, 16)], leftbuf.at[pl.ds(0, 16)], 5, near[1]),
    ]
    for copy in edges:
        copy.start()
    wc_sends = [
        band_send(
            wout.at[:, pl.ds(pl.multiple_of(to_band(k) * 128, 128), 128)], wcol_all, wc_s, wc_r, k
        )
        for k in range(1, BANDS)
    ]
    wcol_all[band] = wout[:, pl.ds(pl.multiple_of(band * 128, 128), 128)]
    for copy in edges:
        copy.wait_recv()
    for send in wc_sends:
        send.start()
    pair_map(
        seq,
        band,
        leftbuf,
        rightbuf,
        cgain_v,
        bias_v,
        weight_v,
        out_ref,
        lf,
        rf,
        lp,
        rp,
        act0,
        field1,
        act1,
        taps_w,
        plain,
        tap_loads,
    )
    for k in range(1, BANDS):
        band_recv(wcol_all, wc_s, wc_r, k).wait_recv()
    heads = jnp.concatenate([att_all[c] for c in range(BANDS)], axis=1)
    summed = jnp.dot(
        heads, wcol_all[...].reshape(BANDS * 128, 128), preferred_element_type=F32
    )
    trunk_ref[...] = (tok_all[band].astype(F32) + summed).astype(BF16)
    for send in tok_sends + q_copies + m_own + m_relay + o_copies + att_sends + edges + wc_sends:
        send.wait_send()
    for send in kv_direct + kv_twin:
        send.wait_send()


def local(
    tokens,
    mappable,
    attn_gain,
    w_query,
    w_key,
    w_value,
    w_out,
    w_left,
    w_right,
    conv_gain,
    conv_kernel,
    conv_bias,
    contact_weight,
):
    vmem = pl.BlockSpec(memory_space=pltpu.VMEM)
    hbm = pl.BlockSpec(memory_space=pltpu.HBM)
    dma = pltpu.SemaphoreType.DMA
    trunk_out, contacts = pl.pallas_call(
        trunk_kernel,
        out_shape=(
            jax.ShapeDtypeStruct((BINS, 128), BF16),
            jax.ShapeDtypeStruct((DIAG, BINS), F32),
        ),
        in_specs=[hbm] * 13,
        out_specs=(vmem, vmem),
        scratch_shapes=[
            pltpu.VMEM((BANDS, 128, 128), BF16),
            pltpu.VMEM((1, 1024), F32),
            pltpu.VMEM((1, BINS), jnp.int32),
            pltpu.VMEM((1024, 384), BF16),
            pltpu.VMEM((128, 1024), BF16),
            pltpu.VMEM((1024, 256), BF16),
            pltpu.VMEM((BANDS, 128, 256), BF16),
            pltpu.VMEM((BANDS, 128, 128), BF16),
            pltpu.VMEM((4, 128, 128), BF16),
            pltpu.VMEM((RING, 272, 128), BF16),
            pltpu.VMEM((4, 128, 128), BF16),
            pltpu.VMEM((4, 128, 128), BF16),
            pltpu.VMEM((4, 8, 128), F32),
            pltpu.VMEM((4, 8, 128), F32),
            pltpu.VMEM((BANDS, 128, 128), BF16),
            pltpu.VMEM((160, 128), BF16),
            pltpu.VMEM((416, 128), BF16),
            pltpu.VMEM((2, 128), F32),
            pltpu.VMEM((2, 128), F32),
            pltpu.VMEM((1, 128), F32),
            pltpu.VMEM((160, 128), F32),
            pltpu.VMEM((200, 128), F32),
            pltpu.VMEM((CHUNK, LANES, 128), F32),
            pltpu.VMEM((WIDE0 + CHUNK - 1, LANES, 128), F32),
            pltpu.VMEM((WIDE0, CHUNK + 2, LANES, 128), BF16),
            pltpu.VMEM((WIDE1, CHUNK, LANES, 128), BF16),
            pltpu.VMEM((WIDE1, CHUNK + 4, LANES, 128), BF16),
            pltpu.VMEM((2, 12, 128, 256), BF16),
            pltpu.VMEM((ROWS, 128), F32),
            dma((12,)),
            dma((12,)),
        ]
        + [dma((8,)) for _ in range(18)],
        compiler_params=pltpu.CompilerParams(
            collective_id=0, has_side_effects=True, vmem_limit_bytes=60 * 1024 * 1024
        ),
    )(
        tokens,
        mappable.reshape(1, BINS),
        attn_gain.reshape(1, -1),
        w_query,
        w_key,
        w_value,
        w_out,
        w_left,
        w_right,
        conv_gain,
        conv_kernel,
        conv_bias,
        contact_weight.reshape(1, 128),
    )
    return (trunk_out, contacts.T)


def solution(mesh):
    return jax.shard_map(
        local,
        mesh=mesh,
        in_specs=(
            P("seq", "band"),
            P("seq"),
            P(),
            P(None, "band"),
            P(None, "band"),
            P(None, "band"),
            P("band", None),
            P(),
            P(),
            P(),
            P(),
            P(),
            P(),
        ),
        out_specs=(P("seq", "band"), P("seq", "band")),
        check_vma=False,
    )
```

```python
import jax
import jax.numpy as jnp
from jax import lax
from jax.experimental import pallas as pl
from jax.experimental.pallas import tpu as pltpu
from jax.sharding import PartitionSpec as P

HEAD = 128
DIAG = 32
BINS = 128
EPS = 1e-06
BANDS = 8
RING = 8
LINE = 4
SEQ = 32
MESH = pl.DeviceIdType.MESH
F32 = jnp.float32
BF16 = jnp.bfloat16


def remote(src, dst, send_sem, recv_sem, **device):
    return pltpu.make_async_remote_copy(
        src_ref=src,
        dst_ref=dst,
        send_sem=send_sem,
        recv_sem=recv_sem,
        device_id=device,
        device_id_type=MESH,
    )


CHUNK = 9
LANES = 16
ROWS = CHUNK * LANES
LEAD = 8
WIDE0 = 44
WIDE1 = 40
GROUP = 8
LATE = 16


def norm_gelu(field, half_gain, keep):
    squares = jnp.sum(field * field, axis=-1, keepdims=True)
    inv = lax.rsqrt(squares + HEAD * EPS)
    if keep is not None:
        inv = jnp.where(keep, inv, 0.0)
    half = (field * inv * half_gain).astype(BF16)
    inner = half * (1.5957691216057308 + 0.285419265090401 * (half * half))
    return half + half * jnp.tanh(inner)


def pair_map(
    seq,
    band,
    leftbuf,
    rightbuf,
    gain_ref,
    bias_ref,
    weight_ref,
    out_ref,
    lf,
    rf,
    lp,
    rp,
    act0,
    field1,
    act1,
    taps_w,
    plain,
    loads,
):
    length = SEQ * BINS
    bins = lax.broadcasted_iota(jnp.int32, (160, 128), 0) + (seq * BINS - 16)
    lf[...] = jnp.where((bins >= 0) & (bins < length), leftbuf[...].astype(F32), 0.0)
    bins = lax.broadcasted_iota(jnp.int32, (192, 128), 0) + (seq * BINS + band * DIAG - 16)
    window = rightbuf[pl.ds(pl.multiple_of(band * DIAG, DIAG), 192)].astype(F32)
    rf[0:192] = jnp.where((bins >= 0) & (bins < length), window, 0.0)
    for a in range(CHUNK):
        lp[a] = lf[pl.ds(LEAD + a, LANES, stride=CHUNK)]
    for t in range(WIDE0 + CHUNK - 1):
        rp[t] = rf[pl.ds(t + 2, LANES, stride=CHUNK)]

    shape = (CHUNK, LANES, 128)
    first = seq * BINS - LEAD
    spot = (
        lax.broadcasted_iota(jnp.int32, shape, 0)
        + lax.broadcasted_iota(jnp.int32, shape, 1) * CHUNK
        + first
    )

    def inside(diag):
        known = (diag >= 0) & (diag < BANDS * DIAG)
        high = jnp.where(known, jnp.minimum(length, length - diag), 0)
        return (spot >= 0) & (spot < high)

    def start_field(delta):
        return lp[...] * rp[pl.ds(delta, CHUNK)]

    root = float(HEAD) ** 0.5 * 0.5
    gain0 = gain_ref[0:1].reshape(1, 1, 128) * root
    gain1 = gain_ref[1:2].reshape(1, 1, 128) * root
    bias0 = bias_ref[0:1].reshape(1, 1, 128)
    bias1 = bias_ref[1:2].reshape(1, 1, 128)
    weight = weight_ref[...].reshape(1, 1, 128)

    def put(dst, where, act, reach):
        dst[where, pl.ds(reach, CHUNK)] = act
        before = pltpu.roll(act[CHUNK - reach :].astype(F32), 1, 1)
        after = pltpu.roll(act[:reach].astype(F32), LANES - 1, 1)
        dst[where, pl.ds(0, reach)] = before.astype(BF16)
        dst[where, pl.ds(reach + CHUNK, reach)] = after.astype(BF16)

    def first_act(delta):
        diag = band * DIAG + delta - 6
        known = jnp.where((diag >= 0) & (diag < BANDS * DIAG), 1.0, 0.0)
        put(act0, delta, norm_gelu(start_field(delta), gain0 * known, None), 1)

    def conv(src, layer, slabs, reach):
        taps = jnp.concatenate(
            [
                jnp.concatenate(
                    [
                        src[slab + reach * (j - p), pl.ds(reach * p, CHUNK)].reshape(ROWS, 128)
                        for slab in slabs
                    ],
                    axis=0,
                )
                for p in range(3)
                for j in range(4)
            ],
            axis=1,
        )
        return jnp.dot(
            taps, taps_w[layer].reshape(12 * 128, 256), preferred_element_type=F32
        )

    def second_act(step, term):
        diag = step * GROUP
        for g in range(GROUP):
            pair, half = g // 2, g % 2
            block = term[pair * ROWS : (pair + 1) * ROWS, half * 128 : (half + 1) * 128]
            value = block.reshape(shape) + start_field(diag + g + 2) + bias0
            field1[diag + g] = value.astype(BF16)
            keep = inside(band * DIAG + diag + g - 4)
            put(act1, diag + g, norm_gelu(value, gain1, keep), 2)

    for g in range(GROUP + 4):
        first_act(g)

    for load in loads:
        load.wait()

    def conv0(step):
        slab = step * GROUP + 2
        return conv(act0, 0, [slab + g for g in range(0, GROUP, 2)], 1)

    def grow(step, term):
        fresh = conv0(step)
        second_act(step - 1, term)
        for g in range(GROUP):
            first_act(step * GROUP + GROUP + 4 + g)
        return fresh

    steps = WIDE1 // GROUP
    term = conv0(0)
    for g in range(GROUP):
        first_act(GROUP + 4 + g)
    term = lax.fori_loop(1, steps - 1, grow, term)
    fresh = conv0(steps - 1)
    second_act(steps - 2, term)
    second_act(steps - 1, fresh)

    lane = lax.broadcasted_iota(jnp.int32, shape, 2)

    def conv1(step):
        slab = step * LATE + 4
        return conv(act1, 1, [slab + g for g in range(LATE) if g % 4 < 2], 2)

    def finish(step, term, found):
        diag = step * LATE
        for g in range(LATE):
            pair, half = (g // 4) * 2 + g % 2, g % 4 // 2
            block = term[pair * ROWS : (pair + 1) * ROWS, half * 128 : (half + 1) * 128]
            value = block.reshape(shape) + field1[diag + g + 4].astype(F32) + bias1
            contact = jnp.sum(value * weight, axis=-1, keepdims=True)
            found = jnp.where(lane == diag + g, contact, found)
        return found

    def last(step, carry):
        term, found = carry
        fresh = conv1(step)
        return fresh, finish(step - 1, term, found)

    steps = DIAG // LATE
    term, found = lax.fori_loop(1, steps, last, (conv1(0), jnp.zeros(shape, F32)))
    found = finish(steps - 1, term, found)
    found = jnp.where(spot + band * DIAG + lane < length, found, 0.0)
    for a in range(CHUNK):
        plain[pl.ds(a, LANES, stride=CHUNK)] = found[a]
    out_ref[...] = plain[LEAD : LEAD + BINS].T[0:DIAG]


def trunk_kernel(
    tok_ref,
    map_ref,
    gain_ref,
    wq_ref,
    wk_ref,
    wv_ref,
    wout_ref,
    wl_ref,
    wr_ref,
    cgain_ref,
    kern_ref,
    bias_ref,
    weight_ref,
    trunk_ref,
    out_ref,
    tok_all,
    gain_v,
    map_v,
    wqkv,
    wout,
    wlr,
    m_all,
    wcol_all,
    q_all,
    kv,
    o_send,
    o_recv,
    st_send,
    st_recv,
    att_all,
    leftbuf,
    rightbuf,
    cgain_v,
    bias_v,
    weight_v,
    lf,
    rf,
    lp,
    rp,
    act0,
    field1,
    act1,
    taps_w,
    plain,
    local_sem,
    tap_sem,
    tok_s,
    tok_r,
    m_s,
    m_r,
    wc_s,
    wc_r,
    q_s,
    q_r,
    kv_s,
    kv_r,
    o_s,
    o_r,
    st_s,
    st_r,
    att_s,
    att_r,
    edge_s,
    edge_r,
):
    seq = lax.axis_index("seq")
    band = lax.axis_index("band")
    core = seq % 2
    ring = (seq // 2) % RING
    half = seq // (2 * RING)
    row = band // 2
    side = band % 2

    def seq_of(half_, ring_, core_):
        return half_ * (2 * RING) + ring_ * 2 + core_

    twin = seq_of(half, ring, 1 - core)
    facing = ring + 1 - 2 * (ring % 2)
    sharers = [
        None,
        seq_of(half, facing, core),
        seq_of(1 - half, ring, core),
        seq_of(1 - half, facing, core),
    ]
    pair = ring // 2
    turn = ring + pair // 2

    def on_line(k):
        other = (pair + LINE + k) % LINE
        return seq_of(half, 2 * other + (turn + other // 2) % 2, core)

    near = {k: (seq + SEQ + k) % SEQ for k in (-3, -2, -1, 1, 2, 3)}

    def to_band(k):
        return (band + k) % BANDS

    def from_band(k):
        return (band + BANDS - k) % BANDS

    loads = [
        pltpu.make_async_copy(tok_ref, tok_all.at[band], local_sem.at[0]),
        pltpu.make_async_copy(gain_ref, gain_v, local_sem.at[1]),
        pltpu.make_async_copy(map_ref, map_v, local_sem.at[2]),
        pltpu.make_async_copy(wout_ref, wout, local_sem.at[3]),
        pltpu.make_async_copy(wl_ref, wlr.at[:, pl.ds(0, 128)], local_sem.at[4]),
        pltpu.make_async_copy(wr_ref, wlr.at[:, pl.ds(128, 128)], local_sem.at[5]),
        pltpu.make_async_copy(wq_ref, wqkv.at[:, pl.ds(0, 128)], local_sem.at[6]),
        pltpu.make_async_copy(wk_ref, wqkv.at[:, pl.ds(128, 128)], local_sem.at[7]),
        pltpu.make_async_copy(wv_ref, wqkv.at[:, pl.ds(256, 128)], local_sem.at[8]),
        pltpu.make_async_copy(cgain_ref, cgain_v, local_sem.at[9]),
        pltpu.make_async_copy(bias_ref, bias_v, local_sem.at[10]),
        pltpu.make_async_copy(weight_ref, weight_v, local_sem.at[11]),
    ]
    tap_loads = [
        pltpu.make_async_copy(
            kern_ref.at[layer, p],
            taps_w.at[layer, pl.ds(4 * p + second, 3), :, pl.ds(128 * second, 128)],
            tap_sem.at[layer * 6 + p * 2 + second],
        )
        for layer in range(2)
        for p in range(3)
        for second in range(2)
    ]
    for load in loads:
        load.start()

    barrier = pltpu.get_barrier_semaphore()
    others = [{"seq": other} for other in list(near.values()) + sharers[1:] + [twin]]
    others += [{"seq": on_line(k)} for k in (1, 2, 3)]
    others += [{"band": to_band(k)} for k in range(1, BANDS)]
    for other in others:
        pl.semaphore_signal(barrier, inc=1, device_id=other, device_id_type=MESH)
    for load in tap_loads:
        load.start()
    for layer in range(2):
        for p in range(3):
            taps_w[layer, 4 * p + 3, :, 0:128] = jnp.zeros((128, 128), BF16)
            taps_w[layer, 4 * p, :, 128:256] = jnp.zeros((128, 128), BF16)
    pl.semaphore_wait(barrier, len(others))

    def band_send(src, dst_all, s_sem, r_sem, k):
        return remote(src, dst_all.at[band], s_sem.at[k], r_sem.at[k], band=to_band(k))

    def band_recv(dst_all, s_sem, r_sem, k):
        slot = dst_all.at[from_band(k)]
        return remote(slot, slot, s_sem.at[k], r_sem.at[k], band=to_band(k))

    tok_sends = [band_send(tok_ref, tok_all, tok_s, tok_r, k) for k in range(1, BANDS)]
    for send in tok_sends:
        send.start()

    for load in loads:
        load.wait()
    m_all[band] = jnp.dot(wout[...], wlr[...], preferred_element_type=F32).astype(BF16)
    offset = ((map_v[...] - 1).astype(F32) * 1000000000.0).astype(BF16)
    kv[0, 128:144] = jnp.broadcast_to(offset, (16, 128))
    for k in range(1, BANDS):
        band_recv(tok_all, tok_s, tok_r, k).wait_recv()

    floats = jnp.concatenate([tok_all[c] for c in range(BANDS)], axis=1).astype(F32)
    inv = lax.rsqrt(jnp.mean(floats * floats, axis=-1, keepdims=True) + EPS)
    normed = (floats * inv * gain_v[...]).astype(BF16)
    qkv = jnp.dot(normed, wqkv[...], preferred_element_type=F32)
    kv[0, 0:128] = qkv[:, 128:256].astype(BF16)
    kv[0, 144:272] = qkv[:, 256:384].T.astype(BF16)
    q_all[0] = qkv[:, 0:128].astype(BF16)

    def kv_copy(src, dst, sem, other):
        return remote(kv.at[src], kv.at[dst], kv_s.at[sem], kv_r.at[dst], seq=other)

    kv_direct = [kv_copy(0, j, j, sharers[j]) for j in (1, 2, 3)]
    kv_twin = [kv_copy(j, 4 + j, 4 + j, twin) for j in range(4)]
    q_copies = [
        remote(q_all.at[0], q_all.at[k], q_s.at[k], q_r.at[k], seq=on_line(k)) for k in (1, 2, 3)
    ]
    for copy in [kv_direct[2], kv_direct[0], kv_direct[1]] + q_copies + [kv_twin[0]]:
        copy.start()

    across = row * 2 + 1 - side

    def row_peer(k, side_):
        return ((row + 4 + k) % 4) * 2 + side_

    m_own = [remote(m_all.at[band], m_all.at[band], m_s.at[0], m_r.at[0], band=across)] + [
        remote(m_all.at[band], m_all.at[band], m_s.at[k], m_r.at[k], band=row_peer(k, side))
        for k in (1, 2, 3)
    ]
    m_relay = [
        remote(
            m_all.at[across], m_all.at[across], m_s.at[3 + k], m_r.at[3 + k], band=row_peer(k, side)
        )
        for k in (1, 2, 3)
    ]
    m_arrivals = [
        remote(m_all.at[slot], m_all.at[slot], m_s.at[sem], m_r.at[sem], band=across)
        for slot, sem in [(across, 0)]
        + [(row_peer(-k, side), k) for k in (1, 2, 3)]
        + [(row_peer(-k, 1 - side), 3 + k) for k in (1, 2, 3)]
    ]
    wc_sends = [
        band_send(
            wout.at[:, pl.ds(pl.multiple_of(to_band(k) * 128, 128), 128)], wcol_all, wc_s, wc_r, k
        )
        for k in range(1, BANDS)
    ]
    wcol_all[band] = wout[:, pl.ds(pl.multiple_of(band * 128, 128), 128)]
    keep = jnp.broadcast_to(map_v[...].astype(F32), (128, 128)).T
    keep = jnp.concatenate([keep, keep], axis=1)
    lr_tok = jnp.dot(floats.astype(BF16), wlr[...], preferred_element_type=F32)
    for j in (2, 1, 3):
        kv_direct[j - 1].wait_recv()
        kv_twin[j].start()
    for copy in q_copies:
        copy.wait_recv()
    for send in m_own + wc_sends:
        send.start()
    queries = jnp.concatenate([q_all[k] for k in range(4)], axis=0)

    def attend(state, slots):
        keys = jnp.concatenate([kv[j, 0:128] for j in slots], axis=0)
        values_t = jnp.concatenate([kv[j, 144:272] for j in slots], axis=1)
        offs = jnp.concatenate(
            [jnp.broadcast_to(kv[j, 128:144][0:1].astype(F32), (128, 128)).T for j in slots],
            axis=0,
        )
        offs = jnp.concatenate([offs] * 4, axis=1)
        scores = (
            lax.dot_general(
                keys, queries, (((1,), (1,)), ((), ())), preferred_element_type=F32
            )
            * HEAD ** (-0.5)
            + offs
        )
        block_top = jnp.max(scores, axis=0, keepdims=True)
        if state is None:
            top = block_top
        else:
            top = jnp.maximum(state[0], block_top)
        weights = jnp.exp(scores - top)
        block_sum = jnp.sum(weights, axis=0, keepdims=True)
        mixed = jnp.dot(values_t, weights.astype(BF16), preferred_element_type=F32)
        if state is None:
            return top, block_sum, mixed
        fade = jnp.exp(state[0] - top)
        return top, state[1] * fade + block_sum, state[2] * fade + mixed

    kv_twin[0].wait_recv()
    state = attend(None, [0, 4])
    state = attend(state, [1, 2])
    kv_twin[1].wait_recv()
    kv_twin[2].wait_recv()
    state = attend(state, [5, 6])
    kv_twin[3].wait_recv()
    top, total, mixed = attend(state, [3, 7])

    mixed = mixed / total
    o_copies = []
    for k in (1, 2, 3):
        lanes = slice(k * 128, (k + 1) * 128)
        o_send[k] = mixed[:, lanes].astype(BF16)
        st_send[k, 0:4] = jnp.broadcast_to(top[:, lanes], (4, 128))
        st_send[k, 4:8] = jnp.broadcast_to(total[:, lanes], (4, 128))
        o_copies.append(
            remote(st_send.at[k], st_recv.at[k], st_s.at[k], st_r.at[k], seq=on_line(-k))
        )
        o_copies.append(
            remote(o_send.at[k], o_recv.at[k], o_s.at[k], o_r.at[k], seq=on_line(-k))
        )
    for copy in o_copies:
        copy.start()
    m_arrivals[0].wait_recv()
    for send in m_relay:
        send.start()
    for copy in o_copies:
        copy.wait_recv()
    tops = [top[:, 0:128]] + [st_recv[k, 0:1] for k in (1, 2, 3)]
    sums = [total[:, 0:128]] + [st_recv[k, 4:5] for k in (1, 2, 3)]
    parts = [mixed[:, 0:128]] + [o_recv[k].astype(F32) for k in (1, 2, 3)]
    best = jnp.maximum(jnp.maximum(tops[0], tops[1]), jnp.maximum(tops[2], tops[3]))
    shares = [s * jnp.exp(t - best) for s, t in zip(sums, tops)]
    share_sum = shares[0] + shares[1] + shares[2] + shares[3]
    attended = (
        parts[0] * shares[0] + parts[1] * shares[1] + parts[2] * shares[2] + parts[3] * shares[3]
    ) / share_sum
    att_all[band] = attended.T.astype(BF16)
    att_sends = [band_send(att_all.at[band], att_all, att_s, att_r, k) for k in range(1, BANDS)]
    for send in att_sends:
        send.start()
    for copy in m_arrivals[1:]:
        copy.wait_recv()
    for k in range(1, BANDS):
        band_recv(att_all, att_s, att_r, k).wait_recv()

    heads = jnp.concatenate([att_all[c] for c in range(BANDS)], axis=1)
    both = lr_tok + jnp.dot(
        heads, m_all[...].reshape(BANDS * 128, 256), preferred_element_type=F32
    )
    both = (both * keep).astype(BF16)
    leftbuf[16:144] = both[:, 0:128]
    rightbuf[16:144] = both[:, 128:256]

    def edge(src, dst, sem, other):
        return remote(src, dst, edge_s.at[sem], edge_r.at[sem], seq=other)

    own = rightbuf.at[pl.ds(16, 128)]
    edges = [
        edge(own, rightbuf.at[pl.ds(272, 128)], 1, near[-2]),
        edge(own, rightbuf.at[pl.ds(144, 128)], 0, near[-1]),
        edge(rightbuf.at[pl.ds(16, 16)], rightbuf.at[pl.ds(400, 16)], 2, near[-3]),
        edge(rightbuf.at[pl.ds(128, 16)], rightbuf.at[pl.ds(0, 16)], 3, near[1]),
        edge(leftbuf.at[pl.ds(16, 16)], leftbuf.at[pl.ds(144, 16)], 4, near[-1]),
        edge(leftbuf.at[pl.ds(128, 16)], leftbuf.at[pl.ds(0, 16)], 5, near[1]),
    ]
    for copy in edges:
        copy.start()
    for k in range(1, BANDS):
        band_recv(wcol_all, wc_s, wc_r, k).wait_recv()
    summed = jnp.dot(
        heads, wcol_all[...].reshape(BANDS * 128, 128), preferred_element_type=F32
    )
    trunk_ref[...] = (tok_all[band].astype(F32) + summed).astype(BF16)
    for send in tok_sends + q_copies + kv_direct + kv_twin + m_own + m_relay + wc_sends:
        send.wait_send()
    for send in o_copies + att_sends:
        send.wait_send()
    for copy in edges:
        copy.wait_recv()
    for send in edges:
        send.wait_send()
    pair_map(
        seq,
        band,
        leftbuf,
        rightbuf,
        cgain_v,
        bias_v,
        weight_v,
        out_ref,
        lf,
        rf,
        lp,
        rp,
        act0,
        field1,
        act1,
        taps_w,
        plain,
        tap_loads,
    )


def local(
    tokens,
    mappable,
    attn_gain,
    w_query,
    w_key,
    w_value,
    w_out,
    w_left,
    w_right,
    conv_gain,
    conv_kernel,
    conv_bias,
    contact_weight,
):
    vmem = pl.BlockSpec(memory_space=pltpu.VMEM)
    hbm = pl.BlockSpec(memory_space=pltpu.HBM)
    dma = pltpu.SemaphoreType.DMA
    trunk_out, contacts = pl.pallas_call(
        trunk_kernel,
        out_shape=(
            jax.ShapeDtypeStruct((BINS, 128), BF16),
            jax.ShapeDtypeStruct((DIAG, BINS), F32),
        ),
        in_specs=[hbm] * 13,
        out_specs=(vmem, vmem),
        scratch_shapes=[
            pltpu.VMEM((BANDS, 128, 128), BF16),
            pltpu.VMEM((1, 1024), F32),
            pltpu.VMEM((1, BINS), jnp.int32),
            pltpu.VMEM((1024, 384), BF16),
            pltpu.VMEM((128, 1024), BF16),
            pltpu.VMEM((1024, 256), BF16),
            pltpu.VMEM((BANDS, 128, 256), BF16),
            pltpu.VMEM((BANDS, 128, 128), BF16),
            pltpu.VMEM((4, 128, 128), BF16),
            pltpu.VMEM((RING, 272, 128), BF16),
            pltpu.VMEM((4, 128, 128), BF16),
            pltpu.VMEM((4, 128, 128), BF16),
            pltpu.VMEM((4, 8, 128), F32),
            pltpu.VMEM((4, 8, 128), F32),
            pltpu.VMEM((BANDS, 128, 128), BF16),
            pltpu.VMEM((160, 128), BF16),
            pltpu.VMEM((416, 128), BF16),
            pltpu.VMEM((2, 128), F32),
            pltpu.VMEM((2, 128), F32),
            pltpu.VMEM((1, 128), F32),
            pltpu.VMEM((160, 128), F32),
            pltpu.VMEM((200, 128), F32),
            pltpu.VMEM((CHUNK, LANES, 128), F32),
            pltpu.VMEM((WIDE0 + CHUNK - 1, LANES, 128), F32),
            pltpu.VMEM((WIDE0, CHUNK + 2, LANES, 128), BF16),
            pltpu.VMEM((WIDE1, CHUNK, LANES, 128), BF16),
            pltpu.VMEM((WIDE1, CHUNK + 4, LANES, 128), BF16),
            pltpu.VMEM((2, 12, 128, 256), BF16),
            pltpu.VMEM((ROWS, 128), F32),
            dma((12,)),
            dma((12,)),
        ]
        + [dma((8,)) for _ in range(18)],
        compiler_params=pltpu.CompilerParams(
            collective_id=0, has_side_effects=True, vmem_limit_bytes=60 * 1024 * 1024
        ),
    )(
        tokens,
        mappable.reshape(1, BINS),
        attn_gain.reshape(1, -1),
        w_query,
        w_key,
        w_value,
        w_out,
        w_left,
        w_right,
        conv_gain,
        conv_kernel,
        conv_bias,
        contact_weight.reshape(1, 128),
    )
    return (trunk_out, contacts.T)


def solution(mesh):
    return jax.shard_map(
        local,
        mesh=mesh,
        in_specs=(
            P("seq", "band"),
            P("seq"),
            P(),
            P(None, "band"),
            P(None, "band"),
            P(None, "band"),
            P("band", None),
            P(),
            P(),
            P(),
            P(),
            P(),
            P(),
        ),
        out_specs=(P("seq", "band"), P("seq", "band")),
        check_vma=False,
    )
```

```python
import jax
import jax.numpy as jnp
from jax import lax
from jax.experimental import pallas as pl
from jax.experimental.pallas import tpu as pltpu
from jax.sharding import PartitionSpec as P

HEAD = 128
DIAG = 32
BINS = 128
EPS = 1e-06
BANDS = 8
RING = 8
LINE = 4
SEQ = 32
MESH = pl.DeviceIdType.MESH
F32 = jnp.float32
BF16 = jnp.bfloat16


def remote(src, dst, send_sem, recv_sem, **device):
    return pltpu.make_async_remote_copy(
        src_ref=src,
        dst_ref=dst,
        send_sem=send_sem,
        recv_sem=recv_sem,
        device_id=device,
        device_id_type=MESH,
    )


CHUNK = 9
LANES = 16
ROWS = CHUNK * LANES
LEAD = 8
WIDE0 = 44
WIDE1 = 40
GROUP = 8
LATE = 16


def norm_gelu(field, half_gain, keep):
    squares = jnp.sum(field * field, axis=-1, keepdims=True)
    inv = lax.rsqrt(squares + HEAD * EPS)
    if keep is not None:
        inv = jnp.where(keep, inv, 0.0)
    half = (field * inv * half_gain).astype(BF16)
    inner = half * (1.5957691216057308 + 0.285419265090401 * (half * half))
    return half + half * jnp.tanh(inner)


def pair_map(
    seq,
    band,
    leftbuf,
    rightbuf,
    gain_ref,
    bias_ref,
    weight_ref,
    out_ref,
    lf,
    rf,
    lp,
    rp,
    act0,
    field1,
    act1,
    taps_w,
    plain,
    loads,
):
    length = SEQ * BINS
    bins = lax.broadcasted_iota(jnp.int32, (160, 128), 0) + (seq * BINS - 16)
    lf[...] = jnp.where((bins >= 0) & (bins < length), leftbuf[...].astype(F32), 0.0)
    bins = lax.broadcasted_iota(jnp.int32, (192, 128), 0) + (seq * BINS + band * DIAG - 16)
    window = rightbuf[pl.ds(pl.multiple_of(band * DIAG, DIAG), 192)].astype(F32)
    rf[0:192] = jnp.where((bins >= 0) & (bins < length), window, 0.0)
    for a in range(CHUNK):
        lp[a] = lf[pl.ds(LEAD + a, LANES, stride=CHUNK)]
    for t in range(WIDE0 + CHUNK - 1):
        rp[t] = rf[pl.ds(t + 2, LANES, stride=CHUNK)]

    shape = (CHUNK, LANES, 128)
    first = seq * BINS - LEAD
    spot = (
        lax.broadcasted_iota(jnp.int32, shape, 0)
        + lax.broadcasted_iota(jnp.int32, shape, 1) * CHUNK
        + first
    )

    def inside(diag):
        known = (diag >= 0) & (diag < BANDS * DIAG)
        high = jnp.where(known, jnp.minimum(length, length - diag), 0)
        return (spot >= 0) & (spot < high)

    def start_field(delta):
        return lp[...] * rp[pl.ds(delta, CHUNK)]

    root = float(HEAD) ** 0.5 * 0.5
    gain0 = gain_ref[0:1].reshape(1, 1, 128) * root
    gain1 = gain_ref[1:2].reshape(1, 1, 128) * root
    bias0 = bias_ref[0:1].reshape(1, 1, 128)
    bias1 = bias_ref[1:2].reshape(1, 1, 128)
    weight = weight_ref[...].reshape(1, 1, 128)

    def put(dst, where, act, reach):
        dst[where, pl.ds(reach, CHUNK)] = act
        before = pltpu.roll(act[CHUNK - reach :].astype(F32), 1, 1)
        after = pltpu.roll(act[:reach].astype(F32), LANES - 1, 1)
        dst[where, pl.ds(0, reach)] = before.astype(BF16)
        dst[where, pl.ds(reach + CHUNK, reach)] = after.astype(BF16)

    def first_act(delta):
        diag = band * DIAG + delta - 6
        known = jnp.where((diag >= 0) & (diag < BANDS * DIAG), 1.0, 0.0)
        put(act0, delta, norm_gelu(start_field(delta), gain0 * known, None), 1)

    def conv(src, layer, slabs, reach):
        taps = jnp.concatenate(
            [
                jnp.concatenate(
                    [
                        src[slab + reach * (j - p), pl.ds(reach * p, CHUNK)].reshape(ROWS, 128)
                        for slab in slabs
                    ],
                    axis=0,
                )
                for p in range(3)
                for j in range(4)
            ],
            axis=1,
        )
        return jnp.dot(
            taps, taps_w[layer].reshape(12 * 128, 256), preferred_element_type=F32
        )

    def second_act(step, term):
        diag = step * GROUP
        for g in range(GROUP):
            pair, half = g // 2, g % 2
            block = term[pair * ROWS : (pair + 1) * ROWS, half * 128 : (half + 1) * 128]
            value = block.reshape(shape) + start_field(diag + g + 2) + bias0
            field1[diag + g] = value.astype(BF16)
            keep = inside(band * DIAG + diag + g - 4)
            put(act1, diag + g, norm_gelu(value, gain1, keep), 2)

    for g in range(GROUP + 4):
        first_act(g)

    for load in loads:
        load.wait()

    def conv0(step):
        slab = step * GROUP + 2
        return conv(act0, 0, [slab + g for g in range(0, GROUP, 2)], 1)

    def grow(step, term):
        fresh = conv0(step)
        second_act(step - 1, term)
        for g in range(GROUP):
            first_act(step * GROUP + GROUP + 4 + g)
        return fresh

    steps = WIDE1 // GROUP
    term = conv0(0)
    for g in range(GROUP):
        first_act(GROUP + 4 + g)
    term = lax.fori_loop(1, steps - 1, grow, term)
    fresh = conv0(steps - 1)
    second_act(steps - 2, term)
    second_act(steps - 1, fresh)

    lane = lax.broadcasted_iota(jnp.int32, shape, 2)

    def conv1(step):
        slab = step * LATE + 4
        return conv(act1, 1, [slab + g for g in range(LATE) if g % 4 < 2], 2)

    def finish(step, term, found):
        diag = step * LATE
        for g in range(LATE):
            pair, half = (g // 4) * 2 + g % 2, g % 4 // 2
            block = term[pair * ROWS : (pair + 1) * ROWS, half * 128 : (half + 1) * 128]
            value = block.reshape(shape) + field1[diag + g + 4].astype(F32) + bias1
            contact = jnp.sum(value * weight, axis=-1, keepdims=True)
            found = jnp.where(lane == diag + g, contact, found)
        return found

    def last(step, carry):
        term, found = carry
        fresh = conv1(step)
        return fresh, finish(step - 1, term, found)

    steps = DIAG // LATE
    term, found = lax.fori_loop(1, steps, last, (conv1(0), jnp.zeros(shape, F32)))
    found = finish(steps - 1, term, found)
    found = jnp.where(spot + band * DIAG + lane < length, found, 0.0)
    for a in range(CHUNK):
        plain[pl.ds(a, LANES, stride=CHUNK)] = found[a]
    out_ref[...] = plain[LEAD : LEAD + BINS].T[0:DIAG]


def trunk_kernel(
    tok_ref,
    map_ref,
    gain_ref,
    wq_ref,
    wk_ref,
    wv_ref,
    wout_ref,
    wl_ref,
    wr_ref,
    cgain_ref,
    kern_ref,
    bias_ref,
    weight_ref,
    trunk_ref,
    out_ref,
    tok_all,
    gain_v,
    map_v,
    wqkv,
    wout,
    wlr,
    m_all,
    wcol_all,
    q_all,
    kv,
    o_send,
    o_recv,
    st_send,
    st_recv,
    att_all,
    leftbuf,
    rightbuf,
    cgain_v,
    bias_v,
    weight_v,
    lf,
    rf,
    lp,
    rp,
    act0,
    field1,
    act1,
    taps_w,
    plain,
    local_sem,
    tap_sem,
    tok_s,
    tok_r,
    m_s,
    m_r,
    wc_s,
    wc_r,
    q_s,
    q_r,
    kv_s,
    kv_r,
    o_s,
    o_r,
    st_s,
    st_r,
    att_s,
    att_r,
    edge_s,
    edge_r,
):
    seq = lax.axis_index("seq")
    band = lax.axis_index("band")
    core = seq % 2
    ring = (seq // 2) % RING
    half = seq // (2 * RING)
    row = band // 2
    side = band % 2

    def seq_of(half_, ring_, core_):
        return half_ * (2 * RING) + ring_ * 2 + core_

    twin = seq_of(half, ring, 1 - core)
    facing = ring + 1 - 2 * (ring % 2)
    sharers = [
        None,
        seq_of(half, facing, core),
        seq_of(1 - half, ring, core),
        seq_of(1 - half, facing, core),
    ]
    pair = ring // 2
    turn = ring + pair // 2

    def on_line(k):
        other = (pair + LINE + k) % LINE
        return seq_of(half, 2 * other + (turn + other // 2) % 2, core)

    near = {k: (seq + SEQ + k) % SEQ for k in (-3, -2, -1, 1, 2, 3)}

    hops = [None, (2, 1), (1, 1), (3, 1), (0, 1), (2, 0), (1, 0), (3, 0)]

    def to_band(k):
        return (row + hops[k][0]) % 4 * 2 + (side + hops[k][1]) % 2

    def from_band(k):
        return (row + 4 - hops[k][0]) % 4 * 2 + (side + hops[k][1]) % 2

    loads = [
        pltpu.make_async_copy(tok_ref, tok_all.at[band], local_sem.at[0]),
        pltpu.make_async_copy(gain_ref, gain_v, local_sem.at[1]),
        pltpu.make_async_copy(map_ref, map_v, local_sem.at[2]),
        pltpu.make_async_copy(wout_ref, wout, local_sem.at[3]),
        pltpu.make_async_copy(wl_ref, wlr.at[:, pl.ds(0, 128)], local_sem.at[4]),
        pltpu.make_async_copy(wr_ref, wlr.at[:, pl.ds(128, 128)], local_sem.at[5]),
        pltpu.make_async_copy(wq_ref, wqkv.at[:, pl.ds(0, 128)], local_sem.at[6]),
        pltpu.make_async_copy(wk_ref, wqkv.at[:, pl.ds(128, 128)], local_sem.at[7]),
        pltpu.make_async_copy(wv_ref, wqkv.at[:, pl.ds(256, 128)], local_sem.at[8]),
        pltpu.make_async_copy(cgain_ref, cgain_v, local_sem.at[9]),
        pltpu.make_async_copy(bias_ref, bias_v, local_sem.at[10]),
        pltpu.make_async_copy(weight_ref, weight_v, local_sem.at[11]),
    ]
    tap_loads = [
        pltpu.make_async_copy(
            kern_ref.at[layer, p],
            taps_w.at[layer, pl.ds(4 * p + second, 3), :, pl.ds(128 * second, 128)],
            tap_sem.at[layer * 6 + p * 2 + second],
        )
        for layer in range(2)
        for p in range(3)
        for second in range(2)
    ]
    for load in loads:
        load.start()

    barrier = pltpu.get_barrier_semaphore()
    others = [{"seq": other} for other in list(near.values()) + sharers[1:] + [twin]]
    others += [{"seq": on_line(k)} for k in (1, 2, 3)]
    others += [{"band": to_band(k)} for k in range(1, BANDS)]
    for other in others:
        pl.semaphore_signal(barrier, inc=1, device_id=other, device_id_type=MESH)
    for load in tap_loads:
        load.start()
    for layer in range(2):
        for p in range(3):
            taps_w[layer, 4 * p + 3, :, 0:128] = jnp.zeros((128, 128), BF16)
            taps_w[layer, 4 * p, :, 128:256] = jnp.zeros((128, 128), BF16)
    pl.semaphore_wait(barrier, len(others))

    def band_send(src, dst_all, s_sem, r_sem, k):
        return remote(src, dst_all.at[band], s_sem.at[k], r_sem.at[k], band=to_band(k))

    def band_recv(dst_all, s_sem, r_sem, k):
        slot = dst_all.at[from_band(k)]
        return remote(slot, slot, s_sem.at[k], r_sem.at[k], band=to_band(k))

    tok_sends = [band_send(tok_ref, tok_all, tok_s, tok_r, k) for k in range(1, BANDS)]
    for send in tok_sends:
        send.start()

    for load in loads:
        load.wait()
    m_all[band] = jnp.dot(wout[...], wlr[...], preferred_element_type=F32).astype(BF16)
    offset = ((map_v[...] - 1).astype(F32) * 1000000000.0).astype(BF16)
    kv[0, 128:144] = jnp.broadcast_to(offset, (16, 128))
    for k in range(1, BANDS):
        band_recv(tok_all, tok_s, tok_r, k).wait_recv()

    floats = jnp.concatenate([tok_all[c] for c in range(BANDS)], axis=1).astype(F32)
    inv = lax.rsqrt(jnp.mean(floats * floats, axis=-1, keepdims=True) + EPS)
    normed = (floats * inv * gain_v[...]).astype(BF16)
    qkv = jnp.dot(normed, wqkv[...], preferred_element_type=F32)
    kv[0, 0:128] = qkv[:, 128:256].astype(BF16)
    kv[0, 144:272] = qkv[:, 256:384].T.astype(BF16)
    q_all[0] = qkv[:, 0:128].astype(BF16)

    def kv_copy(src, dst, sem, other):
        return remote(kv.at[src], kv.at[dst], kv_s.at[sem], kv_r.at[dst], seq=other)

    kv_direct = [kv_copy(0, j, j, sharers[j]) for j in (1, 2, 3)]
    kv_twin = [kv_copy(j, 4 + j, 4 + j, twin) for j in range(4)]
    q_copies = [
        remote(q_all.at[0], q_all.at[k], q_s.at[k], q_r.at[k], seq=on_line(k)) for k in (1, 2, 3)
    ]
    for copy in [kv_direct[2], q_copies[1], kv_direct[0], kv_direct[1]]:
        copy.start()
    for copy in [q_copies[0], q_copies[2], kv_twin[0]]:
        copy.start()

    across = row * 2 + 1 - side

    def row_peer(k, side_):
        return ((row + 4 + k) % 4) * 2 + side_

    m_own = [remote(m_all.at[band], m_all.at[band], m_s.at[0], m_r.at[0], band=across)] + [
        remote(m_all.at[band], m_all.at[band], m_s.at[k], m_r.at[k], band=row_peer(k, side))
        for k in (1, 2, 3)
    ]
    m_relay = [
        remote(
            m_all.at[across], m_all.at[across], m_s.at[3 + k], m_r.at[3 + k], band=row_peer(k, side)
        )
        for k in (1, 2, 3)
    ]
    m_arrivals = [
        remote(m_all.at[slot], m_all.at[slot], m_s.at[sem], m_r.at[sem], band=across)
        for slot, sem in [(across, 0)]
        + [(row_peer(-k, side), k) for k in (1, 2, 3)]
        + [(row_peer(-k, 1 - side), 3 + k) for k in (1, 2, 3)]
    ]
    wc_sends = [
        band_send(
            wout.at[:, pl.ds(pl.multiple_of(to_band(k) * 128, 128), 128)], wcol_all, wc_s, wc_r, k
        )
        for k in range(1, BANDS)
    ]
    wcol_all[band] = wout[:, pl.ds(pl.multiple_of(band * 128, 128), 128)]
    keep = jnp.broadcast_to(map_v[...].astype(F32), (128, 128)).T
    keep = jnp.concatenate([keep, keep], axis=1)
    lr_tok = jnp.dot(floats.astype(BF16), wlr[...], preferred_element_type=F32)
    for j in (2, 1, 3):
        kv_direct[j - 1].wait_recv()
        kv_twin[j].start()
    for copy in q_copies:
        copy.wait_recv()
    for send in m_own + wc_sends:
        send.start()
    queries = jnp.concatenate([q_all[k] for k in range(4)], axis=0)

    def attend(state, slots):
        keys = jnp.concatenate([kv[j, 0:128] for j in slots], axis=0)
        values_t = jnp.concatenate([kv[j, 144:272] for j in slots], axis=1)
        offs = jnp.concatenate(
            [jnp.broadcast_to(kv[j, 128:144][0:1].astype(F32), (128, 128)).T for j in slots],
            axis=0,
        )
        offs = jnp.concatenate([offs] * 4, axis=1)
        scores = (
            lax.dot_general(
                keys, queries, (((1,), (1,)), ((), ())), preferred_element_type=F32
            )
            * HEAD ** (-0.5)
            + offs
        )
        block_top = jnp.max(scores, axis=0, keepdims=True)
        if state is None:
            top = block_top
        else:
            top = jnp.maximum(state[0], block_top)
        weights = jnp.exp(scores - top)
        block_sum = jnp.sum(weights, axis=0, keepdims=True)
        mixed = jnp.dot(values_t, weights.astype(BF16), preferred_element_type=F32)
        if state is None:
            return top, block_sum, mixed
        fade = jnp.exp(state[0] - top)
        return top, state[1] * fade + block_sum, state[2] * fade + mixed

    kv_twin[0].wait_recv()
    state = attend(None, [0, 4, 1, 2])
    for copy in kv_twin[1:]:
        copy.wait_recv()
    top, total, mixed = attend(state, [3, 5, 6, 7])

    mixed = mixed / total
    o_copies = []
    for k in (2, 1, 3):
        lanes = slice(k * 128, (k + 1) * 128)
        o_send[k] = mixed[:, lanes].astype(BF16)
        st_send[k, 0:4] = jnp.broadcast_to(top[:, lanes], (4, 128))
        st_send[k, 4:8] = jnp.broadcast_to(total[:, lanes], (4, 128))
        o_copies.append(
            remote(st_send.at[k], st_recv.at[k], st_s.at[k], st_r.at[k], seq=on_line(-k))
        )
        o_copies.append(
            remote(o_send.at[k], o_recv.at[k], o_s.at[k], o_r.at[k], seq=on_line(-k))
        )
    for copy in o_copies:
        copy.start()
    m_arrivals[0].wait_recv()
    for send in m_relay:
        send.start()
    for copy in o_copies:
        copy.wait_recv()
    tops = [top[:, 0:128]] + [st_recv[k, 0:1] for k in (1, 2, 3)]
    sums = [total[:, 0:128]] + [st_recv[k, 4:5] for k in (1, 2, 3)]
    parts = [mixed[:, 0:128]] + [o_recv[k].astype(F32) for k in (1, 2, 3)]
    best = jnp.maximum(jnp.maximum(tops[0], tops[1]), jnp.maximum(tops[2], tops[3]))
    shares = [s * jnp.exp(t - best) for s, t in zip(sums, tops)]
    share_sum = shares[0] + shares[1] + shares[2] + shares[3]
    attended = (
        parts[0] * shares[0] + parts[1] * shares[1] + parts[2] * shares[2] + parts[3] * shares[3]
    ) / share_sum
    att_all[band] = attended.T.astype(BF16)
    att_sends = [band_send(att_all.at[band], att_all, att_s, att_r, k) for k in range(1, BANDS)]
    for send in att_sends:
        send.start()
    for copy in m_arrivals[1:]:
        copy.wait_recv()
    for k in range(1, BANDS):
        band_recv(att_all, att_s, att_r, k).wait_recv()

    heads = jnp.concatenate([att_all[c] for c in range(BANDS)], axis=1)
    both = lr_tok + jnp.dot(
        heads, m_all[...].reshape(BANDS * 128, 256), preferred_element_type=F32
    )
    both = (both * keep).astype(BF16)
    leftbuf[16:144] = both[:, 0:128]
    rightbuf[16:144] = both[:, 128:256]

    def edge(src, dst, sem, other):
        return remote(src, dst, edge_s.at[sem], edge_r.at[sem], seq=other)

    own = rightbuf.at[pl.ds(16, 128)]
    edges = [
        edge(rightbuf.at[pl.ds(16, 16)], rightbuf.at[pl.ds(400, 16)], 2, near[-3]),
        edge(own, rightbuf.at[pl.ds(272, 128)], 1, near[-2]),
        edge(own, rightbuf.at[pl.ds(144, 128)], 0, near[-1]),
        edge(rightbuf.at[pl.ds(128, 16)], rightbuf.at[pl.ds(0, 16)], 3, near[1]),
        edge(leftbuf.at[pl.ds(16, 16)], leftbuf.at[pl.ds(144, 16)], 4, near[-1]),
        edge(leftbuf.at[pl.ds(128, 16)], leftbuf.at[pl.ds(0, 16)], 5, near[1]),
    ]
    for copy in edges:
        copy.start()
    for k in range(1, BANDS):
        band_recv(wcol_all, wc_s, wc_r, k).wait_recv()
    summed = jnp.dot(
        heads, wcol_all[...].reshape(BANDS * 128, 128), preferred_element_type=F32
    )
    trunk_ref[...] = (tok_all[band].astype(F32) + summed).astype(BF16)
    for send in tok_sends + q_copies + kv_direct + kv_twin + m_own + m_relay + wc_sends:
        send.wait_send()
    for send in o_copies + att_sends:
        send.wait_send()
    for copy in edges:
        copy.wait_recv()
    for send in edges:
        send.wait_send()
    pair_map(
        seq,
        band,
        leftbuf,
        rightbuf,
        cgain_v,
        bias_v,
        weight_v,
        out_ref,
        lf,
        rf,
        lp,
        rp,
        act0,
        field1,
        act1,
        taps_w,
        plain,
        tap_loads,
    )


def local(
    tokens,
    mappable,
    attn_gain,
    w_query,
    w_key,
    w_value,
    w_out,
    w_left,
    w_right,
    conv_gain,
    conv_kernel,
    conv_bias,
    contact_weight,
):
    vmem = pl.BlockSpec(memory_space=pltpu.VMEM)
    hbm = pl.BlockSpec(memory_space=pltpu.HBM)
    dma = pltpu.SemaphoreType.DMA
    trunk_out, contacts = pl.pallas_call(
        trunk_kernel,
        out_shape=(
            jax.ShapeDtypeStruct((BINS, 128), BF16),
            jax.ShapeDtypeStruct((DIAG, BINS), F32),
        ),
        in_specs=[hbm] * 13,
        out_specs=(vmem, vmem),
        scratch_shapes=[
            pltpu.VMEM((BANDS, 128, 128), BF16),
            pltpu.VMEM((1, 1024), F32),
            pltpu.VMEM((1, BINS), jnp.int32),
            pltpu.VMEM((1024, 384), BF16),
            pltpu.VMEM((128, 1024), BF16),
            pltpu.VMEM((1024, 256), BF16),
            pltpu.VMEM((BANDS, 128, 256), BF16),
            pltpu.VMEM((BANDS, 128, 128), BF16),
            pltpu.VMEM((4, 128, 128), BF16),
            pltpu.VMEM((RING, 272, 128), BF16),
            pltpu.VMEM((4, 128, 128), BF16),
            pltpu.VMEM((4, 128, 128), BF16),
            pltpu.VMEM((4, 8, 128), F32),
            pltpu.VMEM((4, 8, 128), F32),
            pltpu.VMEM((BANDS, 128, 128), BF16),
            pltpu.VMEM((160, 128), BF16),
            pltpu.VMEM((416, 128), BF16),
            pltpu.VMEM((2, 128), F32),
            pltpu.VMEM((2, 128), F32),
            pltpu.VMEM((1, 128), F32),
            pltpu.VMEM((160, 128), F32),
            pltpu.VMEM((200, 128), F32),
            pltpu.VMEM((CHUNK, LANES, 128), F32),
            pltpu.VMEM((WIDE0 + CHUNK - 1, LANES, 128), F32),
            pltpu.VMEM((WIDE0, CHUNK + 2, LANES, 128), BF16),
            pltpu.VMEM((WIDE1, CHUNK, LANES, 128), BF16),
            pltpu.VMEM((WIDE1, CHUNK + 4, LANES, 128), BF16),
            pltpu.VMEM((2, 12, 128, 256), BF16),
            pltpu.VMEM((ROWS, 128), F32),
            dma((12,)),
            dma((12,)),
        ]
        + [dma((8,)) for _ in range(18)],
        compiler_params=pltpu.CompilerParams(
            collective_id=0, has_side_effects=True, vmem_limit_bytes=60 * 1024 * 1024
        ),
    )(
        tokens,
        mappable.reshape(1, BINS),
        attn_gain.reshape(1, -1),
        w_query,
        w_key,
        w_value,
        w_out,
        w_left,
        w_right,
        conv_gain,
        conv_kernel,
        conv_bias,
        contact_weight.reshape(1, 128),
    )
    return (trunk_out, contacts.T)


def solution(mesh):
    return jax.shard_map(
        local,
        mesh=mesh,
        in_specs=(
            P("seq", "band"),
            P("seq"),
            P(),
            P(None, "band"),
            P(None, "band"),
            P(None, "band"),
            P("band", None),
            P(),
            P(),
            P(),
            P(),
            P(),
            P(),
        ),
        out_specs=(P("seq", "band"), P("seq", "band")),
        check_vma=False,
    )
```

```python
import jax
import jax.numpy as jnp
from jax import lax
from jax.experimental import pallas as pl
from jax.experimental.pallas import tpu as pltpu
from jax.sharding import PartitionSpec as P

HEAD = 128
DIAG = 32
BINS = 128
EPS = 1e-06
BANDS = 8
RING = 8
LINE = 4
SEQ = 32
MESH = pl.DeviceIdType.MESH
F32 = jnp.float32
BF16 = jnp.bfloat16


def remote(src, dst, send_sem, recv_sem, **device):
    return pltpu.make_async_remote_copy(
        src_ref=src,
        dst_ref=dst,
        send_sem=send_sem,
        recv_sem=recv_sem,
        device_id=device,
        device_id_type=MESH,
    )


CHUNK = 9
LANES = 16
ROWS = CHUNK * LANES
LEAD = 8
WIDE0 = 44
WIDE1 = 40
GROUP = 8
LATE = 16


def norm_gelu(field, half_gain, keep):
    squares = jnp.sum(field * field, axis=-1, keepdims=True)
    inv = lax.rsqrt(squares + HEAD * EPS)
    if keep is not None:
        inv = jnp.where(keep, inv, 0.0)
    half = (field * inv * half_gain).astype(BF16)
    inner = half * (1.5957691216057308 + 0.285419265090401 * (half * half))
    return half + half * jnp.tanh(inner)


def pair_map(
    seq,
    band,
    leftbuf,
    rightbuf,
    gain_ref,
    bias_ref,
    weight_ref,
    out_ref,
    lf,
    rf,
    lp,
    rp,
    act0,
    field1,
    act1,
    taps_w,
    plain,
    loads,
):
    length = SEQ * BINS
    bins = lax.broadcasted_iota(jnp.int32, (160, 128), 0) + (seq * BINS - 16)
    lf[...] = jnp.where((bins >= 0) & (bins < length), leftbuf[...].astype(F32), 0.0)
    bins = lax.broadcasted_iota(jnp.int32, (192, 128), 0) + (seq * BINS + band * DIAG - 16)
    window = rightbuf[pl.ds(pl.multiple_of(band * DIAG, DIAG), 192)].astype(F32)
    rf[0:192] = jnp.where((bins >= 0) & (bins < length), window, 0.0)
    for a in range(CHUNK):
        lp[a] = lf[pl.ds(LEAD + a, LANES, stride=CHUNK)]
    for t in range(WIDE0 + CHUNK - 1):
        rp[t] = rf[pl.ds(t + 2, LANES, stride=CHUNK)]

    shape = (CHUNK, LANES, 128)
    first = seq * BINS - LEAD
    spot = (
        lax.broadcasted_iota(jnp.int32, shape, 0)
        + lax.broadcasted_iota(jnp.int32, shape, 1) * CHUNK
        + first
    )

    def inside(diag):
        known = (diag >= 0) & (diag < BANDS * DIAG)
        high = jnp.where(known, jnp.minimum(length, length - diag), 0)
        return (spot >= 0) & (spot < high)

    def start_field(delta):
        return lp[...] * rp[pl.ds(delta, CHUNK)]

    root = float(HEAD) ** 0.5 * 0.5
    gain0 = gain_ref[0:1].reshape(1, 1, 128) * root
    gain1 = gain_ref[1:2].reshape(1, 1, 128) * root
    bias0 = bias_ref[0:1].reshape(1, 1, 128)
    bias1 = bias_ref[1:2].reshape(1, 1, 128)
    weight = weight_ref[...].reshape(1, 1, 128)

    def put(dst, where, act, reach):
        dst[where, pl.ds(reach, CHUNK)] = act
        before = pltpu.roll(act[CHUNK - reach :].astype(F32), 1, 1)
        after = pltpu.roll(act[:reach].astype(F32), LANES - 1, 1)
        dst[where, pl.ds(0, reach)] = before.astype(BF16)
        dst[where, pl.ds(reach + CHUNK, reach)] = after.astype(BF16)

    def first_act(delta):
        diag = band * DIAG + delta - 6
        known = jnp.where((diag >= 0) & (diag < BANDS * DIAG), 1.0, 0.0)
        put(act0, delta, norm_gelu(start_field(delta), gain0 * known, None), 1)

    def conv(src, layer, slabs, reach):
        taps = jnp.concatenate(
            [
                jnp.concatenate(
                    [
                        src[slab + reach * (j - p), pl.ds(reach * p, CHUNK)].reshape(ROWS, 128)
                        for slab in slabs
                    ],
                    axis=0,
                )
                for p in range(3)
                for j in range(4)
            ],
            axis=1,
        )
        return jnp.dot(
            taps, taps_w[layer].reshape(12 * 128, 256), preferred_element_type=F32
        )

    def second_act(step, term):
        diag = step * GROUP
        for g in range(GROUP):
            pair, half = g // 2, g % 2
            block = term[pair * ROWS : (pair + 1) * ROWS, half * 128 : (half + 1) * 128]
            value = block.reshape(shape) + start_field(diag + g + 2) + bias0
            field1[diag + g] = value.astype(BF16)
            keep = inside(band * DIAG + diag + g - 4)
            put(act1, diag + g, norm_gelu(value, gain1, keep), 2)

    for g in range(GROUP + 4):
        first_act(g)

    for load in loads:
        load.wait()

    def conv0(step):
        slab = step * GROUP + 2
        return conv(act0, 0, [slab + g for g in range(0, GROUP, 2)], 1)

    def grow(step, term):
        fresh = conv0(step)
        second_act(step - 1, term)
        for g in range(GROUP):
            first_act(step * GROUP + GROUP + 4 + g)
        return fresh

    steps = WIDE1 // GROUP
    term = conv0(0)
    for g in range(GROUP):
        first_act(GROUP + 4 + g)
    term = lax.fori_loop(1, steps - 1, grow, term)
    fresh = conv0(steps - 1)
    second_act(steps - 2, term)
    second_act(steps - 1, fresh)

    lane = lax.broadcasted_iota(jnp.int32, shape, 2)

    def conv1(step):
        slab = step * LATE + 4
        return conv(act1, 1, [slab + g for g in range(LATE) if g % 4 < 2], 2)

    def finish(step, term, found):
        diag = step * LATE
        for g in range(LATE):
            pair, half = (g // 4) * 2 + g % 2, g % 4 // 2
            block = term[pair * ROWS : (pair + 1) * ROWS, half * 128 : (half + 1) * 128]
            value = block.reshape(shape) + field1[diag + g + 4].astype(F32) + bias1
            contact = jnp.sum(value * weight, axis=-1, keepdims=True)
            found = jnp.where(lane == diag + g, contact, found)
        return found

    def last(step, carry):
        term, found = carry
        fresh = conv1(step)
        return fresh, finish(step - 1, term, found)

    steps = DIAG // LATE
    term, found = lax.fori_loop(1, steps, last, (conv1(0), jnp.zeros(shape, F32)))
    found = finish(steps - 1, term, found)
    found = jnp.where(spot + band * DIAG + lane < length, found, 0.0)
    for a in range(CHUNK):
        plain[pl.ds(a, LANES, stride=CHUNK)] = found[a]
    out_ref[...] = plain[LEAD : LEAD + BINS].T[0:DIAG]


def trunk_kernel(
    tok_ref,
    map_ref,
    gain_ref,
    wq_ref,
    wk_ref,
    wv_ref,
    wout_ref,
    wl_ref,
    wr_ref,
    cgain_ref,
    kern_ref,
    bias_ref,
    weight_ref,
    trunk_ref,
    out_ref,
    tok_all,
    gain_v,
    map_v,
    wqkv,
    wout,
    wlr,
    m_all,
    wcol_all,
    q_all,
    kv,
    o_send,
    o_recv,
    st_send,
    st_recv,
    att_all,
    leftbuf,
    rightbuf,
    cgain_v,
    bias_v,
    weight_v,
    lf,
    rf,
    lp,
    rp,
    act0,
    field1,
    act1,
    taps_w,
    plain,
    local_sem,
    tap_sem,
    tok_s,
    tok_r,
    m_s,
    m_r,
    wc_s,
    wc_r,
    q_s,
    q_r,
    kv_s,
    kv_r,
    o_s,
    o_r,
    st_s,
    st_r,
    att_s,
    att_r,
    edge_s,
    edge_r,
):
    seq = lax.axis_index("seq")
    band = lax.axis_index("band")
    core = seq % 2
    ring = (seq // 2) % RING
    half = seq // (2 * RING)
    row = band // 2
    side = band % 2

    def seq_of(half_, ring_, core_):
        return half_ * (2 * RING) + ring_ * 2 + core_

    twin = seq_of(half, ring, 1 - core)
    facing = ring + 1 - 2 * (ring % 2)
    sharers = [
        None,
        seq_of(half, facing, core),
        seq_of(1 - half, ring, core),
        seq_of(1 - half, facing, core),
    ]
    pair = ring // 2
    turn = ring + pair // 2

    def on_line(k):
        other = (pair + LINE + k) % LINE
        return seq_of(half, 2 * other + (turn + other // 2) % 2, core)

    near = {k: (seq + SEQ + k) % SEQ for k in (-3, -2, -1, 1, 2, 3)}

    hops = [None, (2, 1), (1, 1), (3, 1), (0, 1), (2, 0), (1, 0), (3, 0)]

    def to_band(k):
        return (row + hops[k][0]) % 4 * 2 + (side + hops[k][1]) % 2

    def from_band(k):
        return (row + 4 - hops[k][0]) % 4 * 2 + (side + hops[k][1]) % 2

    loads = [
        pltpu.make_async_copy(tok_ref, tok_all.at[band], local_sem.at[0]),
        pltpu.make_async_copy(gain_ref, gain_v, local_sem.at[1]),
        pltpu.make_async_copy(map_ref, map_v, local_sem.at[2]),
        pltpu.make_async_copy(wout_ref, wout, local_sem.at[3]),
        pltpu.make_async_copy(wl_ref, wlr.at[:, pl.ds(0, 128)], local_sem.at[4]),
        pltpu.make_async_copy(wr_ref, wlr.at[:, pl.ds(128, 128)], local_sem.at[5]),
        pltpu.make_async_copy(wq_ref, wqkv.at[:, pl.ds(0, 128)], local_sem.at[6]),
        pltpu.make_async_copy(wk_ref, wqkv.at[:, pl.ds(128, 128)], local_sem.at[7]),
        pltpu.make_async_copy(wv_ref, wqkv.at[:, pl.ds(256, 128)], local_sem.at[8]),
        pltpu.make_async_copy(cgain_ref, cgain_v, local_sem.at[9]),
        pltpu.make_async_copy(bias_ref, bias_v, local_sem.at[10]),
        pltpu.make_async_copy(weight_ref, weight_v, local_sem.at[11]),
    ]
    tap_loads = [
        pltpu.make_async_copy(
            kern_ref.at[layer, p],
            taps_w.at[layer, pl.ds(4 * p + second, 3), :, pl.ds(128 * second, 128)],
            tap_sem.at[layer * 6 + p * 2 + second],
        )
        for layer in range(2)
        for p in range(3)
        for second in range(2)
    ]
    barrier = pltpu.get_barrier_semaphore()
    others = [{"band": to_band(k)} for k in range(1, BANDS)]
    others += [{"seq": on_line(k)} for k in (2, 1, 3)]
    others += [{"seq": near[k]} for k in (-3, 3, -2, 2, -1, 1)]
    others += [{"seq": other} for other in sharers[1:] + [twin]]
    for other in others:
        pl.semaphore_signal(barrier, inc=1, device_id=other, device_id_type=MESH)
    for load in loads + tap_loads:
        load.start()
    for layer in range(2):
        for p in range(3):
            taps_w[layer, 4 * p + 3, :, 0:128] = jnp.zeros((128, 128), BF16)
            taps_w[layer, 4 * p, :, 128:256] = jnp.zeros((128, 128), BF16)
    pl.semaphore_wait(barrier, len(others))

    def band_send(src, dst_all, s_sem, r_sem, k):
        return remote(src, dst_all.at[band], s_sem.at[k], r_sem.at[k], band=to_band(k))

    def band_recv(dst_all, s_sem, r_sem, k):
        slot = dst_all.at[from_band(k)]
        return remote(slot, slot, s_sem.at[k], r_sem.at[k], band=to_band(k))

    tok_sends = [band_send(tok_ref, tok_all, tok_s, tok_r, k) for k in range(1, BANDS)]
    for send in tok_sends:
        send.start()

    for load in loads:
        load.wait()
    m_all[band] = jnp.dot(wout[...], wlr[...], preferred_element_type=F32).astype(BF16)
    offset = ((map_v[...] - 1).astype(F32) * 1000000000.0).astype(BF16)
    kv[0, 128:144] = jnp.broadcast_to(offset, (16, 128))
    for k in range(1, BANDS):
        band_recv(tok_all, tok_s, tok_r, k).wait_recv()

    floats = jnp.concatenate([tok_all[c] for c in range(BANDS)], axis=1).astype(F32)
    inv = lax.rsqrt(jnp.mean(floats * floats, axis=-1, keepdims=True) + EPS)
    normed = (floats * inv * gain_v[...]).astype(BF16)
    qkv = jnp.dot(normed, wqkv[...], preferred_element_type=F32)
    kv[0, 0:128] = qkv[:, 128:256].astype(BF16)
    kv[0, 144:272] = qkv[:, 256:384].T.astype(BF16)
    q_all[0] = qkv[:, 0:128].astype(BF16)

    def kv_copy(src, dst, sem, other):
        return remote(kv.at[src], kv.at[dst], kv_s.at[sem], kv_r.at[dst], seq=other)

    kv_direct = [kv_copy(0, j, j, sharers[j]) for j in (1, 2, 3)]
    kv_twin = [kv_copy(j, 4 + j, 4 + j, twin) for j in range(4)]
    q_copies = [
        remote(q_all.at[0], q_all.at[k], q_s.at[k], q_r.at[k], seq=on_line(k)) for k in (1, 2, 3)
    ]
    for copy in [kv_direct[2], q_copies[1], kv_direct[0], kv_direct[1]]:
        copy.start()
    for copy in [q_copies[0], q_copies[2], kv_twin[0]]:
        copy.start()

    across = row * 2 + 1 - side

    def row_peer(k, side_):
        return ((row + 4 + k) % 4) * 2 + side_

    m_own = [remote(m_all.at[band], m_all.at[band], m_s.at[0], m_r.at[0], band=across)] + [
        remote(m_all.at[band], m_all.at[band], m_s.at[k], m_r.at[k], band=row_peer(k, side))
        for k in (1, 2, 3)
    ]
    m_relay = [
        remote(
            m_all.at[across], m_all.at[across], m_s.at[3 + k], m_r.at[3 + k], band=row_peer(k, side)
        )
        for k in (1, 2, 3)
    ]
    m_arrivals = [
        remote(m_all.at[slot], m_all.at[slot], m_s.at[sem], m_r.at[sem], band=across)
        for slot, sem in [(across, 0)]
        + [(row_peer(-k, side), k) for k in (1, 2, 3)]
        + [(row_peer(-k, 1 - side), 3 + k) for k in (1, 2, 3)]
    ]
    wc_sends = [
        band_send(
            wout.at[:, pl.ds(pl.multiple_of(to_band(k) * 128, 128), 128)], wcol_all, wc_s, wc_r, k
        )
        for k in range(1, BANDS)
    ]
    wcol_all[band] = wout[:, pl.ds(pl.multiple_of(band * 128, 128), 128)]
    keep = jnp.broadcast_to(map_v[...].astype(F32), (128, 128)).T
    keep = jnp.concatenate([keep, keep], axis=1)
    lr_tok = jnp.dot(floats.astype(BF16), wlr[...], preferred_element_type=F32)
    for j in (2, 1, 3):
        kv_direct[j - 1].wait_recv()
        kv_twin[j].start()
    for copy in q_copies:
        copy.wait_recv()
    for send in m_own + wc_sends:
        send.start()
    queries = jnp.concatenate([q_all[k] for k in range(4)], axis=0)

    def attend(state, slots):
        keys = jnp.concatenate([kv[j, 0:128] for j in slots], axis=0)
        values_t = jnp.concatenate([kv[j, 144:272] for j in slots], axis=1)
        offs = jnp.concatenate(
            [jnp.broadcast_to(kv[j, 128:144][0:1].astype(F32), (128, 128)).T for j in slots],
            axis=0,
        )
        offs = jnp.concatenate([offs] * 4, axis=1)
        scores = (
            lax.dot_general(
                keys, queries, (((1,), (1,)), ((), ())), preferred_element_type=F32
            )
            * HEAD ** (-0.5)
            + offs
        )
        block_top = jnp.max(scores, axis=0, keepdims=True)
        if state is None:
            top = block_top
        else:
            top = jnp.maximum(state[0], block_top)
        weights = jnp.exp(scores - top)
        block_sum = jnp.sum(weights, axis=0, keepdims=True)
        mixed = jnp.dot(values_t, weights.astype(BF16), preferred_element_type=F32)
        if state is None:
            return top, block_sum, mixed
        fade = jnp.exp(state[0] - top)
        return top, state[1] * fade + block_sum, state[2] * fade + mixed

    kv_twin[0].wait_recv()
    state = attend(None, [0, 4, 1, 2])
    for copy in kv_twin[1:]:
        copy.wait_recv()
    top, total, mixed = attend(state, [3, 5, 6, 7])

    mixed = mixed / total
    o_copies = []
    for k in (2, 1, 3):
        lanes = slice(k * 128, (k + 1) * 128)
        o_send[k] = mixed[:, lanes].astype(BF16)
        st_send[k, 0:4] = jnp.broadcast_to(top[:, lanes], (4, 128))
        st_send[k, 4:8] = jnp.broadcast_to(total[:, lanes], (4, 128))
        o_copies.append(
            remote(st_send.at[k], st_recv.at[k], st_s.at[k], st_r.at[k], seq=on_line(-k))
        )
        o_copies.append(
            remote(o_send.at[k], o_recv.at[k], o_s.at[k], o_r.at[k], seq=on_line(-k))
        )
    for copy in o_copies:
        copy.start()
    m_arrivals[0].wait_recv()
    for send in m_relay:
        send.start()
    for copy in o_copies:
        copy.wait_recv()
    tops = [top[:, 0:128]] + [st_recv[k, 0:1] for k in (1, 2, 3)]
    sums = [total[:, 0:128]] + [st_recv[k, 4:5] for k in (1, 2, 3)]
    parts = [mixed[:, 0:128]] + [o_recv[k].astype(F32) for k in (1, 2, 3)]
    best = jnp.maximum(jnp.maximum(tops[0], tops[1]), jnp.maximum(tops[2], tops[3]))
    shares = [s * jnp.exp(t - best) for s, t in zip(sums, tops)]
    share_sum = shares[0] + shares[1] + shares[2] + shares[3]
    attended = (
        parts[0] * shares[0] + parts[1] * shares[1] + parts[2] * shares[2] + parts[3] * shares[3]
    ) / share_sum
    att_all[band] = attended.T.astype(BF16)
    att_sends = [band_send(att_all.at[band], att_all, att_s, att_r, k) for k in range(1, BANDS)]
    for send in att_sends:
        send.start()
    for copy in m_arrivals[1:]:
        copy.wait_recv()
    for k in range(1, BANDS):
        band_recv(att_all, att_s, att_r, k).wait_recv()

    heads = jnp.concatenate([att_all[c] for c in range(BANDS)], axis=1)
    both = lr_tok + jnp.dot(
        heads, m_all[...].reshape(BANDS * 128, 256), preferred_element_type=F32
    )
    both = (both * keep).astype(BF16)
    leftbuf[16:144] = both[:, 0:128]
    rightbuf[16:144] = both[:, 128:256]

    def edge(src, dst, sem, other):
        return remote(src, dst, edge_s.at[sem], edge_r.at[sem], seq=other)

    own = rightbuf.at[pl.ds(16, 128)]
    edges = [
        edge(rightbuf.at[pl.ds(16, 16)], rightbuf.at[pl.ds(400, 16)], 2, near[-3]),
        edge(own, rightbuf.at[pl.ds(272, 128)], 1, near[-2]),
        edge(own, rightbuf.at[pl.ds(144, 128)], 0, near[-1]),
        edge(rightbuf.at[pl.ds(128, 16)], rightbuf.at[pl.ds(0, 16)], 3, near[1]),
        edge(leftbuf.at[pl.ds(16, 16)], leftbuf.at[pl.ds(144, 16)], 4, near[-1]),
        edge(leftbuf.at[pl.ds(128, 16)], leftbuf.at[pl.ds(0, 16)], 5, near[1]),
    ]
    for copy in edges:
        copy.start()
    for k in range(1, BANDS):
        band_recv(wcol_all, wc_s, wc_r, k).wait_recv()
    summed = jnp.dot(
        heads, wcol_all[...].reshape(BANDS * 128, 128), preferred_element_type=F32
    )
    trunk_ref[...] = (tok_all[band].astype(F32) + summed).astype(BF16)
    for send in tok_sends + q_copies + kv_direct + kv_twin + m_own + m_relay + wc_sends:
        send.wait_send()
    for send in o_copies + att_sends:
        send.wait_send()
    for copy in edges:
        copy.wait_recv()
    for send in edges:
        send.wait_send()
    pair_map(
        seq,
        band,
        leftbuf,
        rightbuf,
        cgain_v,
        bias_v,
        weight_v,
        out_ref,
        lf,
        rf,
        lp,
        rp,
        act0,
        field1,
        act1,
        taps_w,
        plain,
        tap_loads,
    )


def local(
    tokens,
    mappable,
    attn_gain,
    w_query,
    w_key,
    w_value,
    w_out,
    w_left,
    w_right,
    conv_gain,
    conv_kernel,
    conv_bias,
    contact_weight,
):
    vmem = pl.BlockSpec(memory_space=pltpu.VMEM)
    hbm = pl.BlockSpec(memory_space=pltpu.HBM)
    dma = pltpu.SemaphoreType.DMA
    trunk_out, contacts = pl.pallas_call(
        trunk_kernel,
        out_shape=(
            jax.ShapeDtypeStruct((BINS, 128), BF16),
            jax.ShapeDtypeStruct((DIAG, BINS), F32),
        ),
        in_specs=[hbm] * 13,
        out_specs=(vmem, vmem),
        scratch_shapes=[
            pltpu.VMEM((BANDS, 128, 128), BF16),
            pltpu.VMEM((1, 1024), F32),
            pltpu.VMEM((1, BINS), jnp.int32),
            pltpu.VMEM((1024, 384), BF16),
            pltpu.VMEM((128, 1024), BF16),
            pltpu.VMEM((1024, 256), BF16),
            pltpu.VMEM((BANDS, 128, 256), BF16),
            pltpu.VMEM((BANDS, 128, 128), BF16),
            pltpu.VMEM((4, 128, 128), BF16),
            pltpu.VMEM((RING, 272, 128), BF16),
            pltpu.VMEM((4, 128, 128), BF16),
            pltpu.VMEM((4, 128, 128), BF16),
            pltpu.VMEM((4, 8, 128), F32),
            pltpu.VMEM((4, 8, 128), F32),
            pltpu.VMEM((BANDS, 128, 128), BF16),
            pltpu.VMEM((160, 128), BF16),
            pltpu.VMEM((416, 128), BF16),
            pltpu.VMEM((2, 128), F32),
            pltpu.VMEM((2, 128), F32),
            pltpu.VMEM((1, 128), F32),
            pltpu.VMEM((160, 128), F32),
            pltpu.VMEM((200, 128), F32),
            pltpu.VMEM((CHUNK, LANES, 128), F32),
            pltpu.VMEM((WIDE0 + CHUNK - 1, LANES, 128), F32),
            pltpu.VMEM((WIDE0, CHUNK + 2, LANES, 128), BF16),
            pltpu.VMEM((WIDE1, CHUNK, LANES, 128), BF16),
            pltpu.VMEM((WIDE1, CHUNK + 4, LANES, 128), BF16),
            pltpu.VMEM((2, 12, 128, 256), BF16),
            pltpu.VMEM((ROWS, 128), F32),
            dma((12,)),
            dma((12,)),
        ]
        + [dma((8,)) for _ in range(18)],
        compiler_params=pltpu.CompilerParams(
            collective_id=0, has_side_effects=True, vmem_limit_bytes=60 * 1024 * 1024
        ),
    )(
        tokens,
        mappable.reshape(1, BINS),
        attn_gain.reshape(1, -1),
        w_query,
        w_key,
        w_value,
        w_out,
        w_left,
        w_right,
        conv_gain,
        conv_kernel,
        conv_bias,
        contact_weight.reshape(1, 128),
    )
    return (trunk_out, contacts.T)


def solution(mesh):
    return jax.shard_map(
        local,
        mesh=mesh,
        in_specs=(
            P("seq", "band"),
            P("seq"),
            P(),
            P(None, "band"),
            P(None, "band"),
            P(None, "band"),
            P("band", None),
            P(),
            P(),
            P(),
            P(),
            P(),
            P(),
        ),
        out_specs=(P("seq", "band"), P("seq", "band")),
        check_vma=False,
    )
```

```python
import jax
import jax.numpy as jnp
from jax import lax
from jax.experimental import pallas as pl
from jax.experimental.pallas import tpu as pltpu
from jax.sharding import PartitionSpec as P

HEAD = 128
DIAG = 32
BINS = 128
EPS = 1e-06
BANDS = 8
RING = 8
LINE = 4
SEQ = 32
MESH = pl.DeviceIdType.MESH
F32 = jnp.float32
BF16 = jnp.bfloat16


def remote(src, dst, send_sem, recv_sem, **device):
    return pltpu.make_async_remote_copy(
        src_ref=src,
        dst_ref=dst,
        send_sem=send_sem,
        recv_sem=recv_sem,
        device_id=device,
        device_id_type=MESH,
    )


CHUNK = 9
LANES = 16
ROWS = CHUNK * LANES
LEAD = 8
WIDE0 = 44
WIDE1 = 40
GROUP = 8
LATE = 16


def norm_gelu(field, half_gain, keep):
    squares = jnp.sum(field * field, axis=-1, keepdims=True)
    inv = lax.rsqrt(squares + HEAD * EPS)
    if keep is not None:
        inv = jnp.where(keep, inv, 0.0)
    half = (field * inv * half_gain).astype(BF16)
    inner = half * (1.5957691216057308 + 0.285419265090401 * (half * half))
    return half + half * jnp.tanh(inner)


def pair_map(
    seq,
    band,
    leftbuf,
    rightbuf,
    gain_ref,
    bias_ref,
    weight_ref,
    out_ref,
    lf,
    rf,
    lp,
    rp,
    act0,
    field1,
    act1,
    taps_w,
    plain,
    loads,
):
    length = SEQ * BINS
    bins = lax.broadcasted_iota(jnp.int32, (160, 128), 0) + (seq * BINS - 16)
    lf[...] = jnp.where((bins >= 0) & (bins < length), leftbuf[...].astype(F32), 0.0)
    bins = lax.broadcasted_iota(jnp.int32, (192, 128), 0) + (seq * BINS + band * DIAG - 16)
    window = rightbuf[pl.ds(pl.multiple_of(band * DIAG, DIAG), 192)].astype(F32)
    rf[0:192] = jnp.where((bins >= 0) & (bins < length), window, 0.0)
    for a in range(CHUNK):
        lp[a] = lf[pl.ds(LEAD + a, LANES, stride=CHUNK)]
    for t in range(WIDE0 + CHUNK - 1):
        rp[t] = rf[pl.ds(t + 2, LANES, stride=CHUNK)]

    shape = (CHUNK, LANES, 128)
    first = seq * BINS - LEAD
    spot = (
        lax.broadcasted_iota(jnp.int32, shape, 0)
        + lax.broadcasted_iota(jnp.int32, shape, 1) * CHUNK
        + first
    )

    def inside(diag):
        known = (diag >= 0) & (diag < BANDS * DIAG)
        high = jnp.where(known, jnp.minimum(length, length - diag), 0)
        return (spot >= 0) & (spot < high)

    def start_field(delta):
        return lp[...] * rp[pl.ds(delta, CHUNK)]

    root = float(HEAD) ** 0.5 * 0.5
    gain0 = gain_ref[0:1].reshape(1, 1, 128) * root
    gain1 = gain_ref[1:2].reshape(1, 1, 128) * root
    bias0 = bias_ref[0:1].reshape(1, 1, 128)
    bias1 = bias_ref[1:2].reshape(1, 1, 128)
    weight = weight_ref[...].reshape(1, 1, 128)

    def put(dst, where, act, reach):
        dst[where, pl.ds(reach, CHUNK)] = act
        before = pltpu.roll(act[CHUNK - reach :].astype(F32), 1, 1)
        after = pltpu.roll(act[:reach].astype(F32), LANES - 1, 1)
        dst[where, pl.ds(0, reach)] = before.astype(BF16)
        dst[where, pl.ds(reach + CHUNK, reach)] = after.astype(BF16)

    def first_act(delta):
        diag = band * DIAG + delta - 6
        known = jnp.where((diag >= 0) & (diag < BANDS * DIAG), 1.0, 0.0)
        put(act0, delta, norm_gelu(start_field(delta), gain0 * known, None), 1)

    def conv(src, layer, slabs, reach):
        taps = jnp.concatenate(
            [
                jnp.concatenate(
                    [
                        src[slab + reach * (j - p), pl.ds(reach * p, CHUNK)].reshape(ROWS, 128)
                        for slab in slabs
                    ],
                    axis=0,
                )
                for p in range(3)
                for j in range(4)
            ],
            axis=1,
        )
        return jnp.dot(
            taps, taps_w[layer].reshape(12 * 128, 256), preferred_element_type=F32
        )

    def second_act(step, term):
        diag = step * GROUP
        for g in range(GROUP):
            pair, half = g // 2, g % 2
            block = term[pair * ROWS : (pair + 1) * ROWS, half * 128 : (half + 1) * 128]
            value = block.reshape(shape) + start_field(diag + g + 2) + bias0
            field1[diag + g] = value.astype(BF16)
            keep = inside(band * DIAG + diag + g - 4)
            put(act1, diag + g, norm_gelu(value, gain1, keep), 2)

    for g in range(GROUP + 4):
        first_act(g)

    for load in loads:
        load.wait()

    def conv0(step):
        slab = step * GROUP + 2
        return conv(act0, 0, [slab + g for g in range(0, GROUP, 2)], 1)

    def grow(step, term):
        fresh = conv0(step)
        second_act(step - 1, term)
        for g in range(GROUP):
            first_act(step * GROUP + GROUP + 4 + g)
        return fresh

    steps = WIDE1 // GROUP
    term = conv0(0)
    for g in range(GROUP):
        first_act(GROUP + 4 + g)
    term = lax.fori_loop(1, steps - 1, grow, term)
    fresh = conv0(steps - 1)
    second_act(steps - 2, term)
    second_act(steps - 1, fresh)

    lane = lax.broadcasted_iota(jnp.int32, shape, 2)

    def conv1(step):
        slab = step * LATE + 4
        return conv(act1, 1, [slab + g for g in range(LATE) if g % 4 < 2], 2)

    def finish(step, term, found):
        diag = step * LATE
        for g in range(LATE):
            pair, half = (g // 4) * 2 + g % 2, g % 4 // 2
            block = term[pair * ROWS : (pair + 1) * ROWS, half * 128 : (half + 1) * 128]
            value = block.reshape(shape) + field1[diag + g + 4].astype(F32) + bias1
            contact = jnp.sum(value * weight, axis=-1, keepdims=True)
            found = jnp.where(lane == diag + g, contact, found)
        return found

    def last(step, carry):
        term, found = carry
        fresh = conv1(step)
        return fresh, finish(step - 1, term, found)

    steps = DIAG // LATE
    term, found = lax.fori_loop(1, steps, last, (conv1(0), jnp.zeros(shape, F32)))
    found = finish(steps - 1, term, found)
    found = jnp.where(spot + band * DIAG + lane < length, found, 0.0)
    for a in range(CHUNK):
        plain[pl.ds(a, LANES, stride=CHUNK)] = found[a]
    out_ref[...] = plain[LEAD : LEAD + BINS].T[0:DIAG]


def trunk_kernel(
    tok_ref,
    map_ref,
    gain_ref,
    wq_ref,
    wk_ref,
    wv_ref,
    wout_ref,
    wl_ref,
    wr_ref,
    cgain_ref,
    kern_ref,
    bias_ref,
    weight_ref,
    trunk_ref,
    out_ref,
    tok_all,
    gain_v,
    map_v,
    wqkv,
    wout,
    wlr,
    m_all,
    wcol_all,
    q_all,
    kv,
    o_send,
    o_recv,
    st_send,
    st_recv,
    att_all,
    leftbuf,
    rightbuf,
    cgain_v,
    bias_v,
    weight_v,
    lf,
    rf,
    lp,
    rp,
    act0,
    field1,
    act1,
    taps_w,
    plain,
    local_sem,
    tap_sem,
    tok_s,
    tok_r,
    m_s,
    m_r,
    wc_s,
    wc_r,
    q_s,
    q_r,
    kv_s,
    kv_r,
    o_s,
    o_r,
    st_s,
    st_r,
    att_s,
    att_r,
    edge_s,
    edge_r,
):
    seq = lax.axis_index("seq")
    band = lax.axis_index("band")
    core = seq % 2
    ring = (seq // 2) % RING
    half = seq // (2 * RING)
    row = band // 2
    side = band % 2

    def seq_of(half_, ring_, core_):
        return half_ * (2 * RING) + ring_ * 2 + core_

    twin = seq_of(half, ring, 1 - core)
    facing = ring + 1 - 2 * (ring % 2)
    sharers = [
        None,
        seq_of(half, facing, core),
        seq_of(1 - half, ring, core),
        seq_of(1 - half, facing, core),
    ]
    pair = ring // 2
    turn = ring + pair // 2

    def on_line(k):
        other = (pair + LINE + k) % LINE
        return seq_of(half, 2 * other + (turn + other // 2) % 2, core)

    near = {k: (seq + SEQ + k) % SEQ for k in (-3, -2, -1, 1, 2, 3)}

    hops = [None, (2, 1), (1, 1), (3, 1), (0, 1), (2, 0), (1, 0), (3, 0)]

    def to_band(k):
        return (row + hops[k][0]) % 4 * 2 + (side + hops[k][1]) % 2

    def from_band(k):
        return (row + 4 - hops[k][0]) % 4 * 2 + (side + hops[k][1]) % 2

    loads = [
        pltpu.make_async_copy(tok_ref, tok_all.at[band], local_sem.at[0]),
        pltpu.make_async_copy(gain_ref, gain_v, local_sem.at[1]),
        pltpu.make_async_copy(map_ref, map_v, local_sem.at[2]),
        pltpu.make_async_copy(wout_ref, wout, local_sem.at[3]),
        pltpu.make_async_copy(wl_ref, wlr.at[:, pl.ds(0, 128)], local_sem.at[4]),
        pltpu.make_async_copy(wr_ref, wlr.at[:, pl.ds(128, 128)], local_sem.at[5]),
        pltpu.make_async_copy(wq_ref, wqkv.at[:, pl.ds(0, 128)], local_sem.at[6]),
        pltpu.make_async_copy(wk_ref, wqkv.at[:, pl.ds(128, 128)], local_sem.at[7]),
        pltpu.make_async_copy(wv_ref, wqkv.at[:, pl.ds(256, 128)], local_sem.at[8]),
        pltpu.make_async_copy(cgain_ref, cgain_v, local_sem.at[9]),
        pltpu.make_async_copy(bias_ref, bias_v, local_sem.at[10]),
        pltpu.make_async_copy(weight_ref, weight_v, local_sem.at[11]),
    ]
    tap_loads = [
        pltpu.make_async_copy(
            kern_ref.at[layer, p],
            taps_w.at[layer, pl.ds(4 * p + second, 3), :, pl.ds(128 * second, 128)],
            tap_sem.at[layer * 6 + p * 2 + second],
        )
        for layer in range(2)
        for p in range(3)
        for second in range(2)
    ]
    barrier = pltpu.get_barrier_semaphore()
    others = [{"band": to_band(k)} for k in range(1, BANDS)]
    others += [{"seq": on_line(k)} for k in (2, 1, 3)]
    others += [{"seq": near[k]} for k in (-3, 3, -2, 2, -1, 1)]
    others += [{"seq": other} for other in sharers[1:] + [twin]]
    for other in others:
        pl.semaphore_signal(barrier, inc=1, device_id=other, device_id_type=MESH)
    for load in loads + tap_loads:
        load.start()
    for layer in range(2):
        for p in range(3):
            taps_w[layer, 4 * p + 3, :, 0:128] = jnp.zeros((128, 128), BF16)
            taps_w[layer, 4 * p, :, 128:256] = jnp.zeros((128, 128), BF16)
    pl.semaphore_wait(barrier, len(others))

    def band_send(src, dst_all, s_sem, r_sem, k):
        return remote(src, dst_all.at[band], s_sem.at[k], r_sem.at[k], band=to_band(k))

    def band_recv(dst_all, s_sem, r_sem, k):
        slot = dst_all.at[from_band(k)]
        return remote(slot, slot, s_sem.at[k], r_sem.at[k], band=to_band(k))

    tok_sends = [band_send(tok_ref, tok_all, tok_s, tok_r, k) for k in range(1, BANDS)]
    for send in tok_sends:
        send.start()

    for load in loads:
        load.wait()
    m_all[band] = jnp.dot(wout[...], wlr[...], preferred_element_type=F32).astype(BF16)
    offset = ((map_v[...] - 1).astype(F32) * 1000000000.0).astype(BF16)
    kv[0, 128:144] = jnp.broadcast_to(offset, (16, 128))
    for k in range(1, BANDS):
        band_recv(tok_all, tok_s, tok_r, k).wait_recv()

    floats = jnp.concatenate([tok_all[c] for c in range(BANDS)], axis=1).astype(F32)
    inv = lax.rsqrt(jnp.mean(floats * floats, axis=-1, keepdims=True) + EPS)
    normed = (floats * inv * gain_v[...]).astype(BF16)
    qkv = jnp.dot(normed, wqkv[...], preferred_element_type=F32)
    kv[0, 0:128] = qkv[:, 128:256].astype(BF16)
    kv[0, 144:272] = qkv[:, 256:384].T.astype(BF16)
    q_all[0] = qkv[:, 0:128].astype(BF16)

    def kv_copy(src, dst, sem, other):
        return remote(kv.at[src], kv.at[dst], kv_s.at[sem], kv_r.at[dst], seq=other)

    kv_direct = [kv_copy(0, j, j, sharers[j]) for j in (1, 2, 3)]
    kv_twin = [kv_copy(j, 4 + j, 4 + j, twin) for j in range(4)]
    q_copies = [
        remote(q_all.at[0], q_all.at[k], q_s.at[k], q_r.at[k], seq=on_line(k)) for k in (1, 2, 3)
    ]
    for copy in [kv_direct[2], q_copies[1], kv_direct[0], kv_direct[1]]:
        copy.start()
    for copy in [q_copies[0], q_copies[2], kv_twin[0]]:
        copy.start()

    across = row * 2 + 1 - side

    def row_peer(k, side_):
        return ((row + 4 + k) % 4) * 2 + side_

    m_own = [remote(m_all.at[band], m_all.at[band], m_s.at[0], m_r.at[0], band=across)] + [
        remote(m_all.at[band], m_all.at[band], m_s.at[k], m_r.at[k], band=row_peer(k, side))
        for k in (1, 2, 3)
    ]
    m_relay = [
        remote(
            m_all.at[across], m_all.at[across], m_s.at[3 + k], m_r.at[3 + k], band=row_peer(k, side)
        )
        for k in (1, 2, 3)
    ]
    m_arrivals = [
        remote(m_all.at[slot], m_all.at[slot], m_s.at[sem], m_r.at[sem], band=across)
        for slot, sem in [(across, 0)]
        + [(row_peer(-k, side), k) for k in (1, 2, 3)]
        + [(row_peer(-k, 1 - side), 3 + k) for k in (1, 2, 3)]
    ]
    wc_sends = [
        band_send(
            wout.at[:, pl.ds(pl.multiple_of(to_band(k) * 128, 128), 128)], wcol_all, wc_s, wc_r, k
        )
        for k in range(1, BANDS)
    ]
    wcol_all[band] = wout[:, pl.ds(pl.multiple_of(band * 128, 128), 128)]
    keep = jnp.broadcast_to(map_v[...].astype(F32), (128, 128)).T
    keep = jnp.concatenate([keep, keep], axis=1)
    lr_tok = jnp.dot(floats.astype(BF16), wlr[...], preferred_element_type=F32)
    kv_direct[1].wait_recv()
    kv_twin[2].start()
    for send in wc_sends:
        send.start()
    for j in (1, 3):
        kv_direct[j - 1].wait_recv()
        kv_twin[j].start()
    for copy in q_copies:
        copy.wait_recv()
    queries = jnp.concatenate([q_all[k] for k in range(4)], axis=0)

    def attend(state, slots):
        keys = jnp.concatenate([kv[j, 0:128] for j in slots], axis=0)
        values_t = jnp.concatenate([kv[j, 144:272] for j in slots], axis=1)
        offs = jnp.concatenate(
            [jnp.broadcast_to(kv[j, 128:144][0:1].astype(F32), (128, 128)).T for j in slots],
            axis=0,
        )
        offs = jnp.concatenate([offs] * 4, axis=1)
        scores = (
            lax.dot_general(
                keys, queries, (((1,), (1,)), ((), ())), preferred_element_type=F32
            )
            * HEAD ** (-0.5)
            + offs
        )
        block_top = jnp.max(scores, axis=0, keepdims=True)
        if state is None:
            top = block_top
        else:
            top = jnp.maximum(state[0], block_top)
        weights = jnp.exp(scores - top)
        block_sum = jnp.sum(weights, axis=0, keepdims=True)
        mixed = jnp.dot(values_t, weights.astype(BF16), preferred_element_type=F32)
        if state is None:
            return top, block_sum, mixed
        fade = jnp.exp(state[0] - top)
        return top, state[1] * fade + block_sum, state[2] * fade + mixed

    kv_twin[0].wait_recv()
    state = attend(None, [0, 4, 1, 2])
    for copy in kv_twin[1:]:
        copy.wait_recv()
    top, total, mixed = attend(state, [3, 5, 6, 7])

    mixed = mixed / total
    o_copies = []
    for k in (2, 1, 3):
        lanes = slice(k * 128, (k + 1) * 128)
        o_send[k] = mixed[:, lanes].astype(BF16)
        st_send[k, 0:4] = jnp.broadcast_to(top[:, lanes], (4, 128))
        st_send[k, 4:8] = jnp.broadcast_to(total[:, lanes], (4, 128))
        o_copies.append(
            remote(st_send.at[k], st_recv.at[k], st_s.at[k], st_r.at[k], seq=on_line(-k))
        )
        o_copies.append(
            remote(o_send.at[k], o_recv.at[k], o_s.at[k], o_r.at[k], seq=on_line(-k))
        )
    for copy in o_copies:
        copy.start()
    for send in m_own:
        send.start()
    m_arrivals[0].wait_recv()
    for send in m_relay:
        send.start()
    for copy in o_copies:
        copy.wait_recv()
    tops = [top[:, 0:128]] + [st_recv[k, 0:1] for k in (1, 2, 3)]
    sums = [total[:, 0:128]] + [st_recv[k, 4:5] for k in (1, 2, 3)]
    parts = [mixed[:, 0:128]] + [o_recv[k].astype(F32) for k in (1, 2, 3)]
    best = jnp.maximum(jnp.maximum(tops[0], tops[1]), jnp.maximum(tops[2], tops[3]))
    shares = [s * jnp.exp(t - best) for s, t in zip(sums, tops)]
    share_sum = shares[0] + shares[1] + shares[2] + shares[3]
    attended = (
        parts[0] * shares[0] + parts[1] * shares[1] + parts[2] * shares[2] + parts[3] * shares[3]
    ) / share_sum
    att_all[band] = attended.T.astype(BF16)
    att_sends = [band_send(att_all.at[band], att_all, att_s, att_r, k) for k in range(1, BANDS)]
    for send in att_sends:
        send.start()
    for copy in m_arrivals[1:]:
        copy.wait_recv()
    for k in range(1, BANDS):
        band_recv(att_all, att_s, att_r, k).wait_recv()

    heads = jnp.concatenate([att_all[c] for c in range(BANDS)], axis=1)
    both = lr_tok + jnp.dot(
        heads, m_all[...].reshape(BANDS * 128, 256), preferred_element_type=F32
    )
    both = (both * keep).astype(BF16)
    leftbuf[16:144] = both[:, 0:128]
    rightbuf[16:144] = both[:, 128:256]

    def edge(src, dst, sem, other):
        return remote(src, dst, edge_s.at[sem], edge_r.at[sem], seq=other)

    own = rightbuf.at[pl.ds(16, 128)]
    edges = [
        edge(rightbuf.at[pl.ds(16, 16)], rightbuf.at[pl.ds(400, 16)], 2, near[-3]),
        edge(own, rightbuf.at[pl.ds(272, 128)], 1, near[-2]),
        edge(own, rightbuf.at[pl.ds(144, 128)], 0, near[-1]),
        edge(rightbuf.at[pl.ds(128, 16)], rightbuf.at[pl.ds(0, 16)], 3, near[1]),
        edge(leftbuf.at[pl.ds(16, 16)], leftbuf.at[pl.ds(144, 16)], 4, near[-1]),
        edge(leftbuf.at[pl.ds(128, 16)], leftbuf.at[pl.ds(0, 16)], 5, near[1]),
    ]
    for copy in edges:
        copy.start()
    for k in range(1, BANDS):
        band_recv(wcol_all, wc_s, wc_r, k).wait_recv()
    summed = jnp.dot(
        heads, wcol_all[...].reshape(BANDS * 128, 128), preferred_element_type=F32
    )
    trunk_ref[...] = (tok_all[band].astype(F32) + summed).astype(BF16)
    for send in tok_sends + q_copies + kv_direct + kv_twin + m_own + m_relay + wc_sends:
        send.wait_send()
    for send in o_copies + att_sends:
        send.wait_send()
    for copy in edges:
        copy.wait_recv()
    for send in edges:
        send.wait_send()
    pair_map(
        seq,
        band,
        leftbuf,
        rightbuf,
        cgain_v,
        bias_v,
        weight_v,
        out_ref,
        lf,
        rf,
        lp,
        rp,
        act0,
        field1,
        act1,
        taps_w,
        plain,
        tap_loads,
    )


def local(
    tokens,
    mappable,
    attn_gain,
    w_query,
    w_key,
    w_value,
    w_out,
    w_left,
    w_right,
    conv_gain,
    conv_kernel,
    conv_bias,
    contact_weight,
):
    vmem = pl.BlockSpec(memory_space=pltpu.VMEM)
    hbm = pl.BlockSpec(memory_space=pltpu.HBM)
    dma = pltpu.SemaphoreType.DMA
    trunk_out, contacts = pl.pallas_call(
        trunk_kernel,
        out_shape=(
            jax.ShapeDtypeStruct((BINS, 128), BF16),
            jax.ShapeDtypeStruct((DIAG, BINS), F32),
        ),
        in_specs=[hbm] * 13,
        out_specs=(vmem, vmem),
        scratch_shapes=[
            pltpu.VMEM((BANDS, 128, 128), BF16),
            pltpu.VMEM((1, 1024), F32),
            pltpu.VMEM((1, BINS), jnp.int32),
            pltpu.VMEM((1024, 384), BF16),
            pltpu.VMEM((128, 1024), BF16),
            pltpu.VMEM((1024, 256), BF16),
            pltpu.VMEM((BANDS, 128, 256), BF16),
            pltpu.VMEM((BANDS, 128, 128), BF16),
            pltpu.VMEM((4, 128, 128), BF16),
            pltpu.VMEM((RING, 272, 128), BF16),
            pltpu.VMEM((4, 128, 128), BF16),
            pltpu.VMEM((4, 128, 128), BF16),
            pltpu.VMEM((4, 8, 128), F32),
            pltpu.VMEM((4, 8, 128), F32),
            pltpu.VMEM((BANDS, 128, 128), BF16),
            pltpu.VMEM((160, 128), BF16),
            pltpu.VMEM((416, 128), BF16),
            pltpu.VMEM((2, 128), F32),
            pltpu.VMEM((2, 128), F32),
            pltpu.VMEM((1, 128), F32),
            pltpu.VMEM((160, 128), F32),
            pltpu.VMEM((200, 128), F32),
            pltpu.VMEM((CHUNK, LANES, 128), F32),
            pltpu.VMEM((WIDE0 + CHUNK - 1, LANES, 128), F32),
            pltpu.VMEM((WIDE0, CHUNK + 2, LANES, 128), BF16),
            pltpu.VMEM((WIDE1, CHUNK, LANES, 128), BF16),
            pltpu.VMEM((WIDE1, CHUNK + 4, LANES, 128), BF16),
            pltpu.VMEM((2, 12, 128, 256), BF16),
            pltpu.VMEM((ROWS, 128), F32),
            dma((12,)),
            dma((12,)),
        ]
        + [dma((8,)) for _ in range(18)],
        compiler_params=pltpu.CompilerParams(
            collective_id=0, has_side_effects=True, vmem_limit_bytes=60 * 1024 * 1024
        ),
    )(
        tokens,
        mappable.reshape(1, BINS),
        attn_gain.reshape(1, -1),
        w_query,
        w_key,
        w_value,
        w_out,
        w_left,
        w_right,
        conv_gain,
        conv_kernel,
        conv_bias,
        contact_weight.reshape(1, 128),
    )
    return (trunk_out, contacts.T)


def solution(mesh):
    return jax.shard_map(
        local,
        mesh=mesh,
        in_specs=(
            P("seq", "band"),
            P("seq"),
            P(),
            P(None, "band"),
            P(None, "band"),
            P(None, "band"),
            P("band", None),
            P(),
            P(),
            P(),
            P(),
            P(),
            P(),
        ),
        out_specs=(P("seq", "band"), P("seq", "band")),
        check_vma=False,
    )
```

```python
import jax
import jax.numpy as jnp
from jax import lax
from jax.experimental import pallas as pl
from jax.experimental.pallas import tpu as pltpu
from jax.sharding import PartitionSpec as P

HEAD = 128
DIAG = 32
BINS = 128
EPS = 1e-06
BANDS = 8
RING = 8
LINE = 4
SEQ = 32
MESH = pl.DeviceIdType.MESH
F32 = jnp.float32
BF16 = jnp.bfloat16


def remote(src, dst, send_sem, recv_sem, **device):
    return pltpu.make_async_remote_copy(
        src_ref=src,
        dst_ref=dst,
        send_sem=send_sem,
        recv_sem=recv_sem,
        device_id=device,
        device_id_type=MESH,
    )


CHUNK = 9
LANES = 16
ROWS = CHUNK * LANES
LEAD = 8
WIDE0 = 44
WIDE1 = 40
GROUP = 8
LATE = 16


def norm_gelu(field, half_gain, keep):
    squares = jnp.sum(field * field, axis=-1, keepdims=True)
    inv = lax.rsqrt(squares + HEAD * EPS)
    if keep is not None:
        inv = jnp.where(keep, inv, 0.0)
    half = (field * inv * half_gain).astype(BF16)
    inner = half * (1.5957691216057308 + 0.285419265090401 * (half * half))
    return half + half * jnp.tanh(inner)


def pair_map(
    seq,
    band,
    leftbuf,
    rightbuf,
    gain_ref,
    bias_ref,
    weight_ref,
    out_ref,
    lf,
    rf,
    lp,
    rp,
    act0,
    field1,
    act1,
    taps_w,
    plain,
):
    length = SEQ * BINS
    bins = lax.broadcasted_iota(jnp.int32, (160, 128), 0) + (seq * BINS - 16)
    lf[...] = jnp.where((bins >= 0) & (bins < length), leftbuf[...].astype(F32), 0.0)
    bins = lax.broadcasted_iota(jnp.int32, (192, 128), 0) + (seq * BINS + band * DIAG - 16)
    window = rightbuf[pl.ds(pl.multiple_of(band * DIAG, DIAG), 192)].astype(F32)
    rf[0:192] = jnp.where((bins >= 0) & (bins < length), window, 0.0)
    for a in range(CHUNK):
        lp[a] = lf[pl.ds(LEAD + a, LANES, stride=CHUNK)]
    for t in range(WIDE0 + CHUNK - 1):
        rp[t] = rf[pl.ds(t + 2, LANES, stride=CHUNK)]

    shape = (CHUNK, LANES, 128)
    first = seq * BINS - LEAD
    spot = (
        lax.broadcasted_iota(jnp.int32, shape, 0)
        + lax.broadcasted_iota(jnp.int32, shape, 1) * CHUNK
        + first
    )

    def inside(diag):
        known = (diag >= 0) & (diag < BANDS * DIAG)
        high = jnp.where(known, jnp.minimum(length, length - diag), 0)
        return (spot >= 0) & (spot < high)

    def start_field(delta):
        return lp[...] * rp[pl.ds(delta, CHUNK)]

    root = float(HEAD) ** 0.5 * 0.5
    gain0 = gain_ref[0:1].reshape(1, 1, 128) * root
    gain1 = gain_ref[1:2].reshape(1, 1, 128) * root
    bias0 = bias_ref[0:1].reshape(1, 1, 128)
    bias1 = bias_ref[1:2].reshape(1, 1, 128)
    weight = weight_ref[...].reshape(1, 1, 128)

    def put(dst, where, act, reach):
        dst[where, pl.ds(reach, CHUNK)] = act
        before = pltpu.roll(act[CHUNK - reach :].astype(F32), 1, 1)
        after = pltpu.roll(act[:reach].astype(F32), LANES - 1, 1)
        dst[where, pl.ds(0, reach)] = before.astype(BF16)
        dst[where, pl.ds(reach + CHUNK, reach)] = after.astype(BF16)

    def first_act(delta):
        diag = band * DIAG + delta - 6
        known = jnp.where((diag >= 0) & (diag < BANDS * DIAG), 1.0, 0.0)
        put(act0, delta, norm_gelu(start_field(delta), gain0 * known, None), 1)

    def conv(src, layer, slabs, reach):
        taps = jnp.concatenate(
            [
                jnp.concatenate(
                    [
                        src[slab + reach * (j - p), pl.ds(reach * p, CHUNK)].reshape(ROWS, 128)
                        for slab in slabs
                    ],
                    axis=0,
                )
                for p in range(3)
                for j in range(4)
            ],
            axis=1,
        )
        return jnp.dot(
            taps, taps_w[layer].reshape(12 * 128, 256), preferred_element_type=F32
        )

    def second_act(step, term):
        diag = step * GROUP
        for g in range(GROUP):
            pair, half = g // 2, g % 2
            block = term[pair * ROWS : (pair + 1) * ROWS, half * 128 : (half + 1) * 128]
            value = block.reshape(shape) + start_field(diag + g + 2) + bias0
            field1[diag + g] = value.astype(BF16)
            keep = inside(band * DIAG + diag + g - 4)
            put(act1, diag + g, norm_gelu(value, gain1, keep), 2)

    for g in range(GROUP + 4):
        first_act(g)

    def conv0(step):
        slab = step * GROUP + 2
        return conv(act0, 0, [slab + g for g in range(0, GROUP, 2)], 1)

    def grow(step, term):
        fresh = conv0(step)
        second_act(step - 1, term)
        for g in range(GROUP):
            first_act(step * GROUP + GROUP + 4 + g)
        return fresh

    steps = WIDE1 // GROUP
    term = conv0(0)
    for g in range(GROUP):
        first_act(GROUP + 4 + g)
    term = lax.fori_loop(1, steps - 1, grow, term)
    fresh = conv0(steps - 1)
    second_act(steps - 2, term)
    second_act(steps - 1, fresh)

    lane = lax.broadcasted_iota(jnp.int32, shape, 2)

    def conv1(step):
        slab = step * LATE + 4
        return conv(act1, 1, [slab + g for g in range(LATE) if g % 4 < 2], 2)

    def finish(step, term, found):
        diag = step * LATE
        for g in range(LATE):
            pair, half = (g // 4) * 2 + g % 2, g % 4 // 2
            block = term[pair * ROWS : (pair + 1) * ROWS, half * 128 : (half + 1) * 128]
            value = block.reshape(shape) + field1[diag + g + 4].astype(F32) + bias1
            contact = jnp.sum(value * weight, axis=-1, keepdims=True)
            found = jnp.where(lane == diag + g, contact, found)
        return found

    def last(step, carry):
        term, found = carry
        fresh = conv1(step)
        return fresh, finish(step - 1, term, found)

    steps = DIAG // LATE
    term, found = lax.fori_loop(1, steps, last, (conv1(0), jnp.zeros(shape, F32)))
    found = finish(steps - 1, term, found)
    found = jnp.where(spot + band * DIAG + lane < length, found, 0.0)
    for a in range(CHUNK):
        plain[pl.ds(a, LANES, stride=CHUNK)] = found[a]
    out_ref[...] = plain[LEAD : LEAD + BINS].T[0:DIAG]


def trunk_kernel(
    tok_ref,
    map_ref,
    gain_ref,
    wq_ref,
    wk_ref,
    wv_ref,
    wout_ref,
    wl_ref,
    wr_ref,
    cgain_ref,
    kern_ref,
    bias_ref,
    weight_ref,
    trunk_ref,
    out_ref,
    tok_all,
    gain_v,
    map_v,
    wqkv,
    wout,
    wlr,
    m_all,
    wcol_all,
    q_all,
    kv,
    o_send,
    o_recv,
    st_send,
    st_recv,
    att_all,
    leftbuf,
    rightbuf,
    cgain_v,
    bias_v,
    weight_v,
    lf,
    rf,
    lp,
    rp,
    act0,
    field1,
    act1,
    taps_w,
    plain,
    local_sem,
    tap_sem,
    tok_s,
    tok_r,
    m_s,
    m_r,
    wc_s,
    wc_r,
    q_s,
    q_r,
    kv_s,
    kv_r,
    o_s,
    o_r,
    st_s,
    st_r,
    att_s,
    att_r,
    edge_s,
    edge_r,
):
    seq = lax.axis_index("seq")
    band = lax.axis_index("band")
    core = seq % 2
    ring = (seq // 2) % RING
    half = seq // (2 * RING)
    row = band // 2
    side = band % 2

    def seq_of(half_, ring_, core_):
        return half_ * (2 * RING) + ring_ * 2 + core_

    twin = seq_of(half, ring, 1 - core)
    facing = ring + 1 - 2 * (ring % 2)
    sharers = [
        None,
        seq_of(half, facing, core),
        seq_of(1 - half, ring, core),
        seq_of(1 - half, facing, core),
    ]
    pair = ring // 2
    turn = ring + pair // 2

    def on_line(k):
        other = (pair + LINE + k) % LINE
        return seq_of(half, 2 * other + (turn + other // 2) % 2, core)

    near = {k: (seq + SEQ + k) % SEQ for k in (-3, -2, -1, 1, 2, 3)}

    hops = [None, (2, 1), (1, 1), (3, 1), (0, 1), (2, 0), (1, 0), (3, 0)]

    def to_band(k):
        return (row + hops[k][0]) % 4 * 2 + (side + hops[k][1]) % 2

    def from_band(k):
        return (row + 4 - hops[k][0]) % 4 * 2 + (side + hops[k][1]) % 2

    loads = [
        pltpu.make_async_copy(tok_ref, tok_all.at[band], local_sem.at[0]),
        pltpu.make_async_copy(gain_ref, gain_v, local_sem.at[1]),
        pltpu.make_async_copy(map_ref, map_v, local_sem.at[2]),
        pltpu.make_async_copy(wout_ref, wout, local_sem.at[3]),
        pltpu.make_async_copy(wl_ref, wlr.at[:, pl.ds(0, 128)], local_sem.at[4]),
        pltpu.make_async_copy(wr_ref, wlr.at[:, pl.ds(128, 128)], local_sem.at[5]),
        pltpu.make_async_copy(wq_ref, wqkv.at[:, pl.ds(0, 128)], local_sem.at[6]),
        pltpu.make_async_copy(wk_ref, wqkv.at[:, pl.ds(128, 128)], local_sem.at[7]),
        pltpu.make_async_copy(wv_ref, wqkv.at[:, pl.ds(256, 128)], local_sem.at[8]),
        pltpu.make_async_copy(cgain_ref, cgain_v, local_sem.at[9]),
        pltpu.make_async_copy(bias_ref, bias_v, local_sem.at[10]),
        pltpu.make_async_copy(weight_ref, weight_v, local_sem.at[11]),
    ]
    tap_loads = [
        pltpu.make_async_copy(
            kern_ref.at[layer, p],
            taps_w.at[layer, pl.ds(4 * p + second, 3), :, pl.ds(128 * second, 128)],
            tap_sem.at[layer * 6 + p * 2 + second],
        )
        for layer in range(2)
        for p in range(3)
        for second in range(2)
    ]
    barrier = pltpu.get_barrier_semaphore()
    others = [{"band": to_band(k)} for k in range(1, BANDS)]
    others += [{"seq": on_line(k)} for k in (2, 1, 3)]
    others += [{"seq": near[k]} for k in (-3, 3, -2, 2, -1, 1)]
    others += [{"seq": other} for other in sharers[1:] + [twin]]
    for other in others:
        pl.semaphore_signal(barrier, inc=1, device_id=other, device_id_type=MESH)
    for load in loads + tap_loads:
        load.start()
    for layer in range(2):
        for p in range(3):
            taps_w[layer, 4 * p + 3, :, 0:128] = jnp.zeros((128, 128), BF16)
            taps_w[layer, 4 * p, :, 128:256] = jnp.zeros((128, 128), BF16)
    pl.semaphore_wait(barrier, len(others))

    def band_send(src, dst_all, s_sem, r_sem, k):
        return remote(src, dst_all.at[band], s_sem.at[k], r_sem.at[k], band=to_band(k))

    def band_recv(dst_all, s_sem, r_sem, k):
        slot = dst_all.at[from_band(k)]
        return remote(slot, slot, s_sem.at[k], r_sem.at[k], band=to_band(k))

    tok_sends = [band_send(tok_ref, tok_all, tok_s, tok_r, k) for k in range(1, BANDS)]
    for send in tok_sends:
        send.start()

    for load in loads:
        load.wait()
    m_all[band] = jnp.dot(wout[...], wlr[...], preferred_element_type=F32).astype(BF16)
    offset = ((map_v[...] - 1).astype(F32) * 1000000000.0).astype(BF16)
    kv[0, 128:144] = jnp.broadcast_to(offset, (16, 128))
    for k in range(1, BANDS):
        band_recv(tok_all, tok_s, tok_r, k).wait_recv()

    floats = jnp.concatenate([tok_all[c] for c in range(BANDS)], axis=1).astype(F32)
    inv = lax.rsqrt(jnp.mean(floats * floats, axis=-1, keepdims=True) + EPS)
    normed = (floats * inv * gain_v[...]).astype(BF16)
    qkv = jnp.dot(normed, wqkv[...], preferred_element_type=F32)
    kv[0, 0:128] = qkv[:, 128:256].astype(BF16)
    kv[0, 144:272] = qkv[:, 256:384].T.astype(BF16)
    q_all[0] = qkv[:, 0:128].astype(BF16)

    def kv_copy(src, dst, sem, other):
        return remote(kv.at[src], kv.at[dst], kv_s.at[sem], kv_r.at[dst], seq=other)

    kv_direct = [kv_copy(0, j, j, sharers[j]) for j in (1, 2, 3)]
    kv_twin = [kv_copy(j, 4 + j, 4 + j, twin) for j in range(4)]
    q_copies = [
        remote(q_all.at[0], q_all.at[k], q_s.at[k], q_r.at[k], seq=on_line(k)) for k in (1, 2, 3)
    ]
    for copy in [kv_direct[2], q_copies[1], kv_direct[0], kv_direct[1]]:
        copy.start()
    for copy in [q_copies[0], q_copies[2], kv_twin[0]]:
        copy.start()

    across = row * 2 + 1 - side

    def row_peer(k, side_):
        return ((row + 4 + k) % 4) * 2 + side_

    m_own = [remote(m_all.at[band], m_all.at[band], m_s.at[0], m_r.at[0], band=across)] + [
        remote(m_all.at[band], m_all.at[band], m_s.at[k], m_r.at[k], band=row_peer(k, side))
        for k in (1, 2, 3)
    ]
    m_relay = [
        remote(
            m_all.at[across], m_all.at[across], m_s.at[3 + k], m_r.at[3 + k], band=row_peer(k, side)
        )
        for k in (1, 2, 3)
    ]
    m_arrivals = [
        remote(m_all.at[slot], m_all.at[slot], m_s.at[sem], m_r.at[sem], band=across)
        for slot, sem in [(across, 0)]
        + [(row_peer(-k, side), k) for k in (1, 2, 3)]
        + [(row_peer(-k, 1 - side), 3 + k) for k in (1, 2, 3)]
    ]
    wc_sends = [
        band_send(
            wout.at[:, pl.ds(pl.multiple_of(to_band(k) * 128, 128), 128)], wcol_all, wc_s, wc_r, k
        )
        for k in range(1, BANDS)
    ]
    wcol_all[band] = wout[:, pl.ds(pl.multiple_of(band * 128, 128), 128)]
    keep = jnp.broadcast_to(map_v[...].astype(F32), (128, 128)).T
    keep = jnp.concatenate([keep, keep], axis=1)
    lr_tok = jnp.dot(floats.astype(BF16), wlr[...], preferred_element_type=F32)
    kv_direct[1].wait_recv()
    kv_twin[2].start()
    for send in wc_sends:
        send.start()
    for j in (1, 3):
        kv_direct[j - 1].wait_recv()
        kv_twin[j].start()
    for copy in q_copies:
        copy.wait_recv()
    queries = jnp.concatenate([q_all[k] for k in range(4)], axis=0)

    def attend(state, slots):
        keys = jnp.concatenate([kv[j, 0:128] for j in slots], axis=0)
        values_t = jnp.concatenate([kv[j, 144:272] for j in slots], axis=1)
        offs = jnp.concatenate(
            [jnp.broadcast_to(kv[j, 128:144][0:1].astype(F32), (128, 128)).T for j in slots],
            axis=0,
        )
        offs = jnp.concatenate([offs] * 4, axis=1)
        scores = (
            lax.dot_general(
                keys, queries, (((1,), (1,)), ((), ())), preferred_element_type=F32
            )
            * HEAD ** (-0.5)
            + offs
        )
        block_top = jnp.max(scores, axis=0, keepdims=True)
        if state is None:
            top = block_top
        else:
            top = jnp.maximum(state[0], block_top)
        weights = jnp.exp(scores - top)
        block_sum = jnp.sum(weights, axis=0, keepdims=True)
        mixed = jnp.dot(values_t, weights.astype(BF16), preferred_element_type=F32)
        if state is None:
            return top, block_sum, mixed
        fade = jnp.exp(state[0] - top)
        return top, state[1] * fade + block_sum, state[2] * fade + mixed

    kv_twin[0].wait_recv()
    state = attend(None, [0, 4, 1, 2])
    for copy in kv_twin[1:]:
        copy.wait_recv()
    top, total, mixed = attend(state, [3, 5, 6, 7])

    mixed = mixed / total
    o_copies = []
    for k in (2, 1, 3):
        lanes = slice(k * 128, (k + 1) * 128)
        o_send[k] = mixed[:, lanes].astype(BF16)
        st_send[k, 0:4] = jnp.broadcast_to(top[:, lanes], (4, 128))
        st_send[k, 4:8] = jnp.broadcast_to(total[:, lanes], (4, 128))
        o_copies.append(
            remote(st_send.at[k], st_recv.at[k], st_s.at[k], st_r.at[k], seq=on_line(-k))
        )
        o_copies.append(
            remote(o_send.at[k], o_recv.at[k], o_s.at[k], o_r.at[k], seq=on_line(-k))
        )
    for copy in o_copies:
        copy.start()
    for send in m_own:
        send.start()
    m_arrivals[0].wait_recv()
    for send in m_relay:
        send.start()
    for copy in o_copies:
        copy.wait_recv()
    tops = [top[:, 0:128]] + [st_recv[k, 0:1] for k in (1, 2, 3)]
    sums = [total[:, 0:128]] + [st_recv[k, 4:5] for k in (1, 2, 3)]
    parts = [mixed[:, 0:128]] + [o_recv[k].astype(F32) for k in (1, 2, 3)]
    best = jnp.maximum(jnp.maximum(tops[0], tops[1]), jnp.maximum(tops[2], tops[3]))
    shares = [s * jnp.exp(t - best) for s, t in zip(sums, tops)]
    share_sum = shares[0] + shares[1] + shares[2] + shares[3]
    attended = (
        parts[0] * shares[0] + parts[1] * shares[1] + parts[2] * shares[2] + parts[3] * shares[3]
    ) / share_sum
    att_all[band] = attended.T.astype(BF16)
    att_sends = [band_send(att_all.at[band], att_all, att_s, att_r, k) for k in range(1, BANDS)]
    for send in att_sends:
        send.start()

    def fold(total, side_):
        slots = [row_peer(k, side_) for k in range(4)]
        heads_ = jnp.concatenate([att_all[slot] for slot in slots], axis=1)
        folded = jnp.concatenate([m_all[slot] for slot in slots], axis=0)
        return total + jnp.dot(heads_, folded, preferred_element_type=F32)

    for copy in m_arrivals[1:4]:
        copy.wait_recv()
    for k in (5, 6, 7):
        band_recv(att_all, att_s, att_r, k).wait_recv()
    both = fold(lr_tok, side)
    for copy in m_arrivals[4:]:
        copy.wait_recv()
    for k in (1, 2, 3, 4):
        band_recv(att_all, att_s, att_r, k).wait_recv()
    both = fold(both, 1 - side)
    both = (both * keep).astype(BF16)
    leftbuf[16:144] = both[:, 0:128]
    rightbuf[16:144] = both[:, 128:256]

    def edge(src, dst, sem, other):
        return remote(src, dst, edge_s.at[sem], edge_r.at[sem], seq=other)

    own = rightbuf.at[pl.ds(16, 128)]
    edges = [
        edge(rightbuf.at[pl.ds(16, 16)], rightbuf.at[pl.ds(400, 16)], 2, near[-3]),
        edge(own, rightbuf.at[pl.ds(272, 128)], 1, near[-2]),
        edge(own, rightbuf.at[pl.ds(144, 128)], 0, near[-1]),
        edge(rightbuf.at[pl.ds(128, 16)], rightbuf.at[pl.ds(0, 16)], 3, near[1]),
        edge(leftbuf.at[pl.ds(16, 16)], leftbuf.at[pl.ds(144, 16)], 4, near[-1]),
        edge(leftbuf.at[pl.ds(128, 16)], leftbuf.at[pl.ds(0, 16)], 5, near[1]),
    ]
    for copy in edges:
        copy.start()
    for k in range(1, BANDS):
        band_recv(wcol_all, wc_s, wc_r, k).wait_recv()
    heads = jnp.concatenate([att_all[c] for c in range(BANDS)], axis=1)
    summed = jnp.dot(
        heads, wcol_all[...].reshape(BANDS * 128, 128), preferred_element_type=F32
    )
    trunk_ref[...] = (tok_all[band].astype(F32) + summed).astype(BF16)
    for send in tok_sends + q_copies + kv_direct + kv_twin + m_own + m_relay + wc_sends:
        send.wait_send()
    for send in o_copies + att_sends:
        send.wait_send()
    for load in tap_loads:
        load.wait()
    for copy in edges:
        copy.wait_recv()
    for send in edges:
        send.wait_send()
    pair_map(
        seq,
        band,
        leftbuf,
        rightbuf,
        cgain_v,
        bias_v,
        weight_v,
        out_ref,
        lf,
        rf,
        lp,
        rp,
        act0,
        field1,
        act1,
        taps_w,
        plain,
    )


def local(
    tokens,
    mappable,
    attn_gain,
    w_query,
    w_key,
    w_value,
    w_out,
    w_left,
    w_right,
    conv_gain,
    conv_kernel,
    conv_bias,
    contact_weight,
):
    vmem = pl.BlockSpec(memory_space=pltpu.VMEM)
    hbm = pl.BlockSpec(memory_space=pltpu.HBM)
    dma = pltpu.SemaphoreType.DMA
    trunk_out, contacts = pl.pallas_call(
        trunk_kernel,
        out_shape=(
            jax.ShapeDtypeStruct((BINS, 128), BF16),
            jax.ShapeDtypeStruct((DIAG, BINS), F32),
        ),
        in_specs=[hbm] * 13,
        out_specs=(vmem, vmem),
        scratch_shapes=[
            pltpu.VMEM((BANDS, 128, 128), BF16),
            pltpu.VMEM((1, 1024), F32),
            pltpu.VMEM((1, BINS), jnp.int32),
            pltpu.VMEM((1024, 384), BF16),
            pltpu.VMEM((128, 1024), BF16),
            pltpu.VMEM((1024, 256), BF16),
            pltpu.VMEM((BANDS, 128, 256), BF16),
            pltpu.VMEM((BANDS, 128, 128), BF16),
            pltpu.VMEM((4, 128, 128), BF16),
            pltpu.VMEM((RING, 272, 128), BF16),
            pltpu.VMEM((4, 128, 128), BF16),
            pltpu.VMEM((4, 128, 128), BF16),
            pltpu.VMEM((4, 8, 128), F32),
            pltpu.VMEM((4, 8, 128), F32),
            pltpu.VMEM((BANDS, 128, 128), BF16),
            pltpu.VMEM((160, 128), BF16),
            pltpu.VMEM((416, 128), BF16),
            pltpu.VMEM((2, 128), F32),
            pltpu.VMEM((2, 128), F32),
            pltpu.VMEM((1, 128), F32),
            pltpu.VMEM((160, 128), F32),
            pltpu.VMEM((200, 128), F32),
            pltpu.VMEM((CHUNK, LANES, 128), F32),
            pltpu.VMEM((WIDE0 + CHUNK - 1, LANES, 128), F32),
            pltpu.VMEM((WIDE0, CHUNK + 2, LANES, 128), BF16),
            pltpu.VMEM((WIDE1, CHUNK, LANES, 128), BF16),
            pltpu.VMEM((WIDE1, CHUNK + 4, LANES, 128), BF16),
            pltpu.VMEM((2, 12, 128, 256), BF16),
            pltpu.VMEM((ROWS, 128), F32),
            dma((12,)),
            dma((12,)),
        ]
        + [dma((8,)) for _ in range(18)],
        compiler_params=pltpu.CompilerParams(
            collective_id=0, has_side_effects=True, vmem_limit_bytes=60 * 1024 * 1024
        ),
    )(
        tokens,
        mappable.reshape(1, BINS),
        attn_gain.reshape(1, -1),
        w_query,
        w_key,
        w_value,
        w_out,
        w_left,
        w_right,
        conv_gain,
        conv_kernel,
        conv_bias,
        contact_weight.reshape(1, 128),
    )
    return (trunk_out, contacts.T)


def solution(mesh):
    return jax.shard_map(
        local,
        mesh=mesh,
        in_specs=(
            P("seq", "band"),
            P("seq"),
            P(),
            P(None, "band"),
            P(None, "band"),
            P(None, "band"),
            P("band", None),
            P(),
            P(),
            P(),
            P(),
            P(),
            P(),
        ),
        out_specs=(P("seq", "band"), P("seq", "band")),
        check_vma=False,
    )
```

```python
import jax
import jax.numpy as jnp
from jax import lax
from jax.experimental import pallas as pl
from jax.experimental.pallas import tpu as pltpu
from jax.sharding import PartitionSpec as P

HEAD = 128
DIAG = 32
BINS = 128
EPS = 1e-06
BANDS = 8
RING = 8
LINE = 4
SEQ = 32
MESH = pl.DeviceIdType.MESH
F32 = jnp.float32
BF16 = jnp.bfloat16


def remote(src, dst, send_sem, recv_sem, **device):
    return pltpu.make_async_remote_copy(
        src_ref=src,
        dst_ref=dst,
        send_sem=send_sem,
        recv_sem=recv_sem,
        device_id=device,
        device_id_type=MESH,
    )


CHUNK = 9
LANES = 16
ROWS = CHUNK * LANES
LEAD = 8
WIDE0 = 44
WIDE1 = 40
GROUP = 8
LATE = 16


def norm_gelu(field, half_gain, keep):
    squares = jnp.sum(field * field, axis=-1, keepdims=True)
    inv = lax.rsqrt(squares + HEAD * EPS)
    if keep is not None:
        inv = jnp.where(keep, inv, 0.0)
    half = (field * inv * half_gain).astype(BF16)
    inner = half * (1.5957691216057308 + 0.285419265090401 * (half * half))
    return half + half * jnp.tanh(inner)


def pair_map(
    seq,
    band,
    leftbuf,
    rightbuf,
    gain_ref,
    bias_ref,
    weight_ref,
    out_ref,
    lf,
    rf,
    lp,
    rp,
    act0,
    field1,
    act1,
    taps_w,
    plain,
):
    length = SEQ * BINS
    bins = lax.broadcasted_iota(jnp.int32, (160, 128), 0) + (seq * BINS - 16)
    lf[...] = jnp.where((bins >= 0) & (bins < length), leftbuf[...].astype(F32), 0.0)
    bins = lax.broadcasted_iota(jnp.int32, (192, 128), 0) + (seq * BINS + band * DIAG - 16)
    window = rightbuf[pl.ds(pl.multiple_of(band * DIAG, DIAG), 192)].astype(F32)
    rf[0:192] = jnp.where((bins >= 0) & (bins < length), window, 0.0)
    for a in range(CHUNK):
        lp[a] = lf[pl.ds(LEAD + a, LANES, stride=CHUNK)]
    for t in range(WIDE0 + CHUNK - 1):
        rp[t] = rf[pl.ds(t + 2, LANES, stride=CHUNK)]

    shape = (CHUNK, LANES, 128)
    first = seq * BINS - LEAD
    spot = (
        lax.broadcasted_iota(jnp.int32, shape, 0)
        + lax.broadcasted_iota(jnp.int32, shape, 1) * CHUNK
        + first
    )

    def inside(diag):
        known = (diag >= 0) & (diag < BANDS * DIAG)
        high = jnp.where(known, jnp.minimum(length, length - diag), 0)
        return (spot >= 0) & (spot < high)

    def start_field(delta):
        return lp[...] * rp[pl.ds(delta, CHUNK)]

    root = float(HEAD) ** 0.5 * 0.5
    gain0 = gain_ref[0:1].reshape(1, 1, 128) * root
    gain1 = gain_ref[1:2].reshape(1, 1, 128) * root
    bias0 = bias_ref[0:1].reshape(1, 1, 128)
    bias1 = bias_ref[1:2].reshape(1, 1, 128)
    weight = weight_ref[...].reshape(1, 1, 128)

    def put(dst, where, act, reach):
        dst[where, pl.ds(reach, CHUNK)] = act
        before = pltpu.roll(act[CHUNK - reach :].astype(F32), 1, 1)
        after = pltpu.roll(act[:reach].astype(F32), LANES - 1, 1)
        dst[where, pl.ds(0, reach)] = before.astype(BF16)
        dst[where, pl.ds(reach + CHUNK, reach)] = after.astype(BF16)

    def first_act(delta):
        diag = band * DIAG + delta - 6
        known = jnp.where((diag >= 0) & (diag < BANDS * DIAG), 1.0, 0.0)
        put(act0, delta, norm_gelu(start_field(delta), gain0 * known, None), 1)

    def conv(src, layer, slabs, reach):
        taps = jnp.concatenate(
            [
                jnp.concatenate(
                    [
                        src[slab + reach * (j - p), pl.ds(reach * p, CHUNK)].reshape(ROWS, 128)
                        for slab in slabs
                    ],
                    axis=0,
                )
                for p in range(3)
                for j in range(4)
            ],
            axis=1,
        )
        return jnp.dot(
            taps, taps_w[layer].reshape(12 * 128, 256), preferred_element_type=F32
        )

    def second_act(step, term):
        diag = step * GROUP
        for g in range(GROUP):
            pair, half = g // 2, g % 2
            block = term[pair * ROWS : (pair + 1) * ROWS, half * 128 : (half + 1) * 128]
            value = block.reshape(shape) + start_field(diag + g + 2) + bias0
            field1[diag + g] = value.astype(BF16)
            keep = inside(band * DIAG + diag + g - 4)
            put(act1, diag + g, norm_gelu(value, gain1, keep), 2)

    for g in range(GROUP + 4):
        first_act(g)

    def conv0(step):
        slab = step * GROUP + 2
        return conv(act0, 0, [slab + g for g in range(0, GROUP, 2)], 1)

    def grow(step, term):
        fresh = conv0(step)
        second_act(step - 1, term)
        for g in range(GROUP):
            first_act(step * GROUP + GROUP + 4 + g)
        return fresh

    steps = WIDE1 // GROUP
    term = conv0(0)
    for g in range(GROUP):
        first_act(GROUP + 4 + g)
    term = lax.fori_loop(1, steps - 1, grow, term)
    fresh = conv0(steps - 1)
    second_act(steps - 2, term)
    second_act(steps - 1, fresh)

    lane = lax.broadcasted_iota(jnp.int32, shape, 2)

    def conv1(step):
        slab = step * LATE + 4
        return conv(act1, 1, [slab + g for g in range(LATE) if g % 4 < 2], 2)

    def finish(step, term, found):
        diag = step * LATE
        for g in range(LATE):
            pair, half = (g // 4) * 2 + g % 2, g % 4 // 2
            block = term[pair * ROWS : (pair + 1) * ROWS, half * 128 : (half + 1) * 128]
            value = block.reshape(shape) + field1[diag + g + 4].astype(F32) + bias1
            contact = jnp.sum(value * weight, axis=-1, keepdims=True)
            found = jnp.where(lane == diag + g, contact, found)
        return found

    def last(step, carry):
        term, found = carry
        fresh = conv1(step)
        return fresh, finish(step - 1, term, found)

    steps = DIAG // LATE
    term, found = lax.fori_loop(1, steps, last, (conv1(0), jnp.zeros(shape, F32)))
    found = finish(steps - 1, term, found)
    found = jnp.where(spot + band * DIAG + lane < length, found, 0.0)
    for a in range(CHUNK):
        plain[pl.ds(a, LANES, stride=CHUNK)] = found[a]
    out_ref[...] = plain[LEAD : LEAD + BINS].T[0:DIAG]


def trunk_kernel(
    tok_ref,
    map_ref,
    gain_ref,
    wq_ref,
    wk_ref,
    wv_ref,
    wout_ref,
    wl_ref,
    wr_ref,
    cgain_ref,
    kern_ref,
    bias_ref,
    weight_ref,
    trunk_ref,
    out_ref,
    tok_all,
    gain_v,
    map_v,
    wqkv,
    wout,
    wlr,
    m_all,
    wcol_all,
    q_all,
    kv,
    o_send,
    o_recv,
    st_send,
    st_recv,
    att_all,
    leftbuf,
    rightbuf,
    cgain_v,
    bias_v,
    weight_v,
    lf,
    rf,
    lp,
    rp,
    act0,
    field1,
    act1,
    taps_w,
    plain,
    local_sem,
    tap_sem,
    tok_s,
    tok_r,
    m_s,
    m_r,
    wc_s,
    wc_r,
    q_s,
    q_r,
    kv_s,
    kv_r,
    o_s,
    o_r,
    st_s,
    st_r,
    att_s,
    att_r,
    edge_s,
    edge_r,
):
    seq = lax.axis_index("seq")
    band = lax.axis_index("band")
    core = seq % 2
    ring = (seq // 2) % RING
    half = seq // (2 * RING)
    row = band // 2
    side = band % 2

    def seq_of(half_, ring_, core_):
        return half_ * (2 * RING) + ring_ * 2 + core_

    twin = seq_of(half, ring, 1 - core)
    facing = ring + 1 - 2 * (ring % 2)
    sharers = [
        None,
        seq_of(half, facing, core),
        seq_of(1 - half, ring, core),
        seq_of(1 - half, facing, core),
    ]
    pair = ring // 2
    turn = ring + pair // 2

    def on_line(k):
        other = (pair + LINE + k) % LINE
        return seq_of(half, 2 * other + (turn + other // 2) % 2, core)

    near = {k: (seq + SEQ + k) % SEQ for k in (-3, -2, -1, 1, 2, 3)}

    hops = [None, (2, 1), (1, 1), (3, 1), (0, 1), (2, 0), (1, 0), (3, 0)]

    def to_band(k):
        return (row + hops[k][0]) % 4 * 2 + (side + hops[k][1]) % 2

    def from_band(k):
        return (row + 4 - hops[k][0]) % 4 * 2 + (side + hops[k][1]) % 2

    loads = [
        pltpu.make_async_copy(tok_ref, tok_all.at[band], local_sem.at[0]),
        pltpu.make_async_copy(gain_ref, gain_v, local_sem.at[1]),
        pltpu.make_async_copy(map_ref, map_v, local_sem.at[2]),
        pltpu.make_async_copy(wout_ref, wout, local_sem.at[3]),
        pltpu.make_async_copy(wl_ref, wlr.at[:, pl.ds(0, 128)], local_sem.at[4]),
        pltpu.make_async_copy(wr_ref, wlr.at[:, pl.ds(128, 128)], local_sem.at[5]),
        pltpu.make_async_copy(wq_ref, wqkv.at[:, pl.ds(0, 128)], local_sem.at[6]),
        pltpu.make_async_copy(wk_ref, wqkv.at[:, pl.ds(128, 128)], local_sem.at[7]),
        pltpu.make_async_copy(wv_ref, wqkv.at[:, pl.ds(256, 128)], local_sem.at[8]),
        pltpu.make_async_copy(cgain_ref, cgain_v, local_sem.at[9]),
        pltpu.make_async_copy(bias_ref, bias_v, local_sem.at[10]),
        pltpu.make_async_copy(weight_ref, weight_v, local_sem.at[11]),
    ]
    tap_loads = [
        pltpu.make_async_copy(
            kern_ref.at[layer, p],
            taps_w.at[layer, pl.ds(4 * p + second, 3), :, pl.ds(128 * second, 128)],
            tap_sem.at[layer * 6 + p * 2 + second],
        )
        for layer in range(2)
        for p in range(3)
        for second in range(2)
    ]
    barrier = pltpu.get_barrier_semaphore()
    others = [{"band": to_band(k)} for k in range(1, BANDS)]
    others += [{"seq": on_line(k)} for k in (2, 1, 3)]
    others += [{"seq": near[k]} for k in (-3, 3, -2, 2, -1, 1)]
    others += [{"seq": other} for other in sharers[1:] + [twin]]
    for other in others:
        pl.semaphore_signal(barrier, inc=1, device_id=other, device_id_type=MESH)
    for layer in range(2):
        for p in range(3):
            taps_w[layer, 4 * p + 3, :, 0:128] = jnp.zeros((128, 128), BF16)
            taps_w[layer, 4 * p, :, 128:256] = jnp.zeros((128, 128), BF16)
    pl.semaphore_wait(barrier, len(others))

    def band_send(src, dst_all, s_sem, r_sem, k):
        return remote(src, dst_all.at[band], s_sem.at[k], r_sem.at[k], band=to_band(k))

    def band_recv(dst_all, s_sem, r_sem, k):
        slot = dst_all.at[from_band(k)]
        return remote(slot, slot, s_sem.at[k], r_sem.at[k], band=to_band(k))

    tok_sends = [band_send(tok_ref, tok_all, tok_s, tok_r, k) for k in range(1, BANDS)]
    for send in tok_sends:
        send.start()
    for load in loads + tap_loads:
        load.start()

    for load in loads:
        load.wait()
    m_all[band] = jnp.dot(wout[...], wlr[...], preferred_element_type=F32).astype(BF16)
    offset = ((map_v[...] - 1).astype(F32) * 1000000000.0).astype(BF16)
    kv[0, 128:144] = jnp.broadcast_to(offset, (16, 128))
    for k in range(1, BANDS):
        band_recv(tok_all, tok_s, tok_r, k).wait_recv()

    floats = jnp.concatenate([tok_all[c] for c in range(BANDS)], axis=1).astype(F32)
    inv = lax.rsqrt(jnp.mean(floats * floats, axis=-1, keepdims=True) + EPS)
    normed = (floats * inv * gain_v[...]).astype(BF16)
    qkv = jnp.dot(normed, wqkv[...], preferred_element_type=F32)
    kv[0, 0:128] = qkv[:, 128:256].astype(BF16)
    kv[0, 144:272] = qkv[:, 256:384].T.astype(BF16)
    q_all[0] = qkv[:, 0:128].astype(BF16)

    def kv_copy(src, dst, sem, other):
        return remote(kv.at[src], kv.at[dst], kv_s.at[sem], kv_r.at[dst], seq=other)

    kv_direct = [kv_copy(0, j, j, sharers[j]) for j in (1, 2, 3)]
    kv_twin = [kv_copy(j, 4 + j, 4 + j, twin) for j in range(4)]
    q_copies = [
        remote(q_all.at[0], q_all.at[k], q_s.at[k], q_r.at[k], seq=on_line(k)) for k in (1, 2, 3)
    ]
    for copy in [kv_direct[2], q_copies[1], kv_direct[0], kv_direct[1]]:
        copy.start()
    for copy in [q_copies[0], q_copies[2], kv_twin[0]]:
        copy.start()

    across = row * 2 + 1 - side

    def row_peer(k, side_):
        return ((row + 4 + k) % 4) * 2 + side_

    m_own = [remote(m_all.at[band], m_all.at[band], m_s.at[0], m_r.at[0], band=across)] + [
        remote(m_all.at[band], m_all.at[band], m_s.at[k], m_r.at[k], band=row_peer(k, side))
        for k in (1, 2, 3)
    ]
    m_relay = [
        remote(
            m_all.at[across], m_all.at[across], m_s.at[3 + k], m_r.at[3 + k], band=row_peer(k, side)
        )
        for k in (1, 2, 3)
    ]
    m_arrivals = [
        remote(m_all.at[slot], m_all.at[slot], m_s.at[sem], m_r.at[sem], band=across)
        for slot, sem in [(across, 0)]
        + [(row_peer(-k, side), k) for k in (1, 2, 3)]
        + [(row_peer(-k, 1 - side), 3 + k) for k in (1, 2, 3)]
    ]
    wc_sends = [
        band_send(
            wout.at[:, pl.ds(pl.multiple_of(to_band(k) * 128, 128), 128)], wcol_all, wc_s, wc_r, k
        )
        for k in range(1, BANDS)
    ]
    wcol_all[band] = wout[:, pl.ds(pl.multiple_of(band * 128, 128), 128)]
    keep = jnp.broadcast_to(map_v[...].astype(F32), (128, 128)).T
    keep = jnp.concatenate([keep, keep], axis=1)
    lr_tok = jnp.dot(floats.astype(BF16), wlr[...], preferred_element_type=F32)
    kv_direct[1].wait_recv()
    kv_twin[2].start()
    for send in wc_sends:
        send.start()
    for j in (1, 3):
        kv_direct[j - 1].wait_recv()
        kv_twin[j].start()
    for copy in q_copies:
        copy.wait_recv()
    queries = jnp.concatenate([q_all[k] for k in range(4)], axis=0)

    def attend(state, slots):
        keys = jnp.concatenate([kv[j, 0:128] for j in slots], axis=0)
        values_t = jnp.concatenate([kv[j, 144:272] for j in slots], axis=1)
        offs = jnp.concatenate(
            [jnp.broadcast_to(kv[j, 128:144][0:1].astype(F32), (128, 128)).T for j in slots],
            axis=0,
        )
        offs = jnp.concatenate([offs] * 4, axis=1)
        scores = (
            lax.dot_general(
                keys, queries, (((1,), (1,)), ((), ())), preferred_element_type=F32
            )
            * HEAD ** (-0.5)
            + offs
        )
        block_top = jnp.max(scores, axis=0, keepdims=True)
        if state is None:
            top = block_top
        else:
            top = jnp.maximum(state[0], block_top)
        weights = jnp.exp(scores - top)
        block_sum = jnp.sum(weights, axis=0, keepdims=True)
        mixed = jnp.dot(values_t, weights.astype(BF16), preferred_element_type=F32)
        if state is None:
            return top, block_sum, mixed
        fade = jnp.exp(state[0] - top)
        return top, state[1] * fade + block_sum, state[2] * fade + mixed

    kv_twin[0].wait_recv()
    state = attend(None, [0, 4, 1, 2])
    for copy in kv_twin[1:]:
        copy.wait_recv()
    top, total, mixed = attend(state, [3, 5, 6, 7])

    mixed = mixed / total
    o_copies = []
    for k in (2, 1, 3):
        lanes = slice(k * 128, (k + 1) * 128)
        o_send[k] = mixed[:, lanes].astype(BF16)
        st_send[k, 0:4] = jnp.broadcast_to(top[:, lanes], (4, 128))
        st_send[k, 4:8] = jnp.broadcast_to(total[:, lanes], (4, 128))
        o_copies.append(
            remote(st_send.at[k], st_recv.at[k], st_s.at[k], st_r.at[k], seq=on_line(-k))
        )
        o_copies.append(
            remote(o_send.at[k], o_recv.at[k], o_s.at[k], o_r.at[k], seq=on_line(-k))
        )
    for copy in o_copies:
        copy.start()
    for send in m_own:
        send.start()
    m_arrivals[0].wait_recv()
    for send in m_relay:
        send.start()
    for copy in o_copies:
        copy.wait_recv()
    tops = [top[:, 0:128]] + [st_recv[k, 0:1] for k in (1, 2, 3)]
    sums = [total[:, 0:128]] + [st_recv[k, 4:5] for k in (1, 2, 3)]
    parts = [mixed[:, 0:128]] + [o_recv[k].astype(F32) for k in (1, 2, 3)]
    best = jnp.maximum(jnp.maximum(tops[0], tops[1]), jnp.maximum(tops[2], tops[3]))
    shares = [s * jnp.exp(t - best) for s, t in zip(sums, tops)]
    share_sum = shares[0] + shares[1] + shares[2] + shares[3]
    attended = (
        parts[0] * shares[0] + parts[1] * shares[1] + parts[2] * shares[2] + parts[3] * shares[3]
    ) / share_sum
    att_all[band] = attended.T.astype(BF16)
    att_sends = [band_send(att_all.at[band], att_all, att_s, att_r, k) for k in range(1, BANDS)]
    for send in att_sends:
        send.start()

    def fold(total, side_):
        slots = [row_peer(k, side_) for k in range(4)]
        heads_ = jnp.concatenate([att_all[slot] for slot in slots], axis=1)
        folded = jnp.concatenate([m_all[slot] for slot in slots], axis=0)
        return total + jnp.dot(heads_, folded, preferred_element_type=F32)

    for copy in m_arrivals[1:4]:
        copy.wait_recv()
    for k in (5, 6, 7):
        band_recv(att_all, att_s, att_r, k).wait_recv()
    both = fold(lr_tok, side)
    for copy in m_arrivals[4:]:
        copy.wait_recv()
    for k in (1, 2, 3, 4):
        band_recv(att_all, att_s, att_r, k).wait_recv()
    both = fold(both, 1 - side)
    both = (both * keep).astype(BF16)
    leftbuf[16:144] = both[:, 0:128]
    rightbuf[16:144] = both[:, 128:256]

    def edge(src, dst, sem, other):
        return remote(src, dst, edge_s.at[sem], edge_r.at[sem], seq=other)

    own = rightbuf.at[pl.ds(16, 128)]
    edges = [
        edge(rightbuf.at[pl.ds(16, 16)], rightbuf.at[pl.ds(400, 16)], 2, near[-3]),
        edge(own, rightbuf.at[pl.ds(272, 128)], 1, near[-2]),
        edge(own, rightbuf.at[pl.ds(144, 128)], 0, near[-1]),
        edge(rightbuf.at[pl.ds(128, 16)], rightbuf.at[pl.ds(0, 16)], 3, near[1]),
        edge(leftbuf.at[pl.ds(16, 16)], leftbuf.at[pl.ds(144, 16)], 4, near[-1]),
        edge(leftbuf.at[pl.ds(128, 16)], leftbuf.at[pl.ds(0, 16)], 5, near[1]),
    ]
    for copy in edges:
        copy.start()
    for k in range(1, BANDS):
        band_recv(wcol_all, wc_s, wc_r, k).wait_recv()
    heads = jnp.concatenate([att_all[c] for c in range(BANDS)], axis=1)
    summed = jnp.dot(
        heads, wcol_all[...].reshape(BANDS * 128, 128), preferred_element_type=F32
    )
    trunk_ref[...] = (tok_all[band].astype(F32) + summed).astype(BF16)
    for send in tok_sends + q_copies + kv_direct + kv_twin + m_own + m_relay + wc_sends:
        send.wait_send()
    for send in o_copies + att_sends:
        send.wait_send()
    for load in tap_loads:
        load.wait()
    for copy in edges:
        copy.wait_recv()
    for send in edges:
        send.wait_send()
    pair_map(
        seq,
        band,
        leftbuf,
        rightbuf,
        cgain_v,
        bias_v,
        weight_v,
        out_ref,
        lf,
        rf,
        lp,
        rp,
        act0,
        field1,
        act1,
        taps_w,
        plain,
    )


def local(
    tokens,
    mappable,
    attn_gain,
    w_query,
    w_key,
    w_value,
    w_out,
    w_left,
    w_right,
    conv_gain,
    conv_kernel,
    conv_bias,
    contact_weight,
):
    vmem = pl.BlockSpec(memory_space=pltpu.VMEM)
    hbm = pl.BlockSpec(memory_space=pltpu.HBM)
    dma = pltpu.SemaphoreType.DMA
    trunk_out, contacts = pl.pallas_call(
        trunk_kernel,
        out_shape=(
            jax.ShapeDtypeStruct((BINS, 128), BF16),
            jax.ShapeDtypeStruct((DIAG, BINS), F32),
        ),
        in_specs=[hbm] * 13,
        out_specs=(vmem, vmem),
        scratch_shapes=[
            pltpu.VMEM((BANDS, 128, 128), BF16),
            pltpu.VMEM((1, 1024), F32),
            pltpu.VMEM((1, BINS), jnp.int32),
            pltpu.VMEM((1024, 384), BF16),
            pltpu.VMEM((128, 1024), BF16),
            pltpu.VMEM((1024, 256), BF16),
            pltpu.VMEM((BANDS, 128, 256), BF16),
            pltpu.VMEM((BANDS, 128, 128), BF16),
            pltpu.VMEM((4, 128, 128), BF16),
            pltpu.VMEM((RING, 272, 128), BF16),
            pltpu.VMEM((4, 128, 128), BF16),
            pltpu.VMEM((4, 128, 128), BF16),
            pltpu.VMEM((4, 8, 128), F32),
            pltpu.VMEM((4, 8, 128), F32),
            pltpu.VMEM((BANDS, 128, 128), BF16),
            pltpu.VMEM((160, 128), BF16),
            pltpu.VMEM((416, 128), BF16),
            pltpu.VMEM((2, 128), F32),
            pltpu.VMEM((2, 128), F32),
            pltpu.VMEM((1, 128), F32),
            pltpu.VMEM((160, 128), F32),
            pltpu.VMEM((200, 128), F32),
            pltpu.VMEM((CHUNK, LANES, 128), F32),
            pltpu.VMEM((WIDE0 + CHUNK - 1, LANES, 128), F32),
            pltpu.VMEM((WIDE0, CHUNK + 2, LANES, 128), BF16),
            pltpu.VMEM((WIDE1, CHUNK, LANES, 128), BF16),
            pltpu.VMEM((WIDE1, CHUNK + 4, LANES, 128), BF16),
            pltpu.VMEM((2, 12, 128, 256), BF16),
            pltpu.VMEM((ROWS, 128), F32),
            dma((12,)),
            dma((12,)),
        ]
        + [dma((8,)) for _ in range(18)],
        compiler_params=pltpu.CompilerParams(
            collective_id=0, has_side_effects=True, vmem_limit_bytes=60 * 1024 * 1024
        ),
    )(
        tokens,
        mappable.reshape(1, BINS),
        attn_gain.reshape(1, -1),
        w_query,
        w_key,
        w_value,
        w_out,
        w_left,
        w_right,
        conv_gain,
        conv_kernel,
        conv_bias,
        contact_weight.reshape(1, 128),
    )
    return (trunk_out, contacts.T)


def solution(mesh):
    return jax.shard_map(
        local,
        mesh=mesh,
        in_specs=(
            P("seq", "band"),
            P("seq"),
            P(),
            P(None, "band"),
            P(None, "band"),
            P(None, "band"),
            P("band", None),
            P(),
            P(),
            P(),
            P(),
            P(),
            P(),
        ),
        out_specs=(P("seq", "band"), P("seq", "band")),
        check_vma=False,
    )
```
